32 devices in a mesh: dom: 8 (over y, x, core), blk: 4 (over z).
Axes of the slice: x: 2, y: 2, z: 4, core: 2. Of those that a mesh axis runs over, the one named last changes fastest.
Arguments:
- adjoint_start: float32 [192, 3, 320], P('dom', None, 'blk'), may hold values from -6 to 6
- right_sides: float32 [192, 3, 320], P('dom', None, 'blk'), may hold values from -6 to 6
- jac_blocks: bfloat16 [192, 7, 320, 320], P('dom', None, 'blk'), may hold values from -0.125 to 0.125
- block_inverse: bfloat16 [192, 320, 320], P('dom', 'blk'), may hold values from -0.15625 to 0.15625
- neighbours: int32 [192, 6], P('dom'), may hold values from 0 to 191, as said below
- pseudo_shift: float32 [192], P('dom'), may hold values from 0.25 to 2
- shape_partials: bfloat16 [192, 320, 192], P('dom', 'blk'), may hold values from -0.3125 to 0.3125
- node_ids: int32 [192, 64], P('dom'), may hold values from 0 to 6143, as said below
Outputs:
- adjoint: float32 [192, 3, 320], P('dom', None, 'blk')
- shape_gradient: float32 [9, 6144], P(None, ('dom', 'blk'))
The draws below stay inside these ranges and needn't reach their ends.
Inputs may be any that keep to these rules, and one draw needn't show every extreme that they name: `neighbours`: partition k holds elements k * 24 to (k + 1) * 24 - 1; every neighbour of an element lies in its own partition or in the partition just before or after it. `node_ids`: partition k owns mesh nodes k * 768 to (k + 1) * 768 - 1; every node of an element is owned by the element's partition or by the partition just before or after it.
All inputs are finite; a program needn't handle non-finite values.
Results may differ from the reference program's by a relative error of at most 0.0038.
Values may be sent and summed in bfloat16 or wider, within the bound.
No kernel may reach another device: no remote copies, remote signals or barrier semaphores. Data moves between devices by JAX's collectives and lax.ppermute only.
A program may use at most 64 MiB of HBM per device.

```python
import math
import jax
import jax.numpy as jnp
from jax import lax

B = 320
FACES = 6
RHS = 3
SWEEPS = 2
ENODES = 64
E_DEV = 24
NQ = 192
NODE_DEV = 768
ELEMS = 192
NODES = 6144


def draw_neighbours(key, part):
    part_total = ELEMS // E_DEV
    element = jnp.arange(ELEMS, dtype=jnp.int32)
    owner_part = element // E_DEV
    lowest = jnp.maximum(owner_part - 1, 0) * E_DEV
    highest = jnp.minimum(owner_part + 2, part_total) * E_DEV
    chosen = jax.random.randint(key, (ELEMS, FACES), lowest[:, None], highest[:, None], dtype=jnp.int32)
    chosen = chosen.at[0, 0].set(0)
    chosen = chosen.at[ELEMS - 1, FACES - 1].set(ELEMS - 1)
    return chosen


def draw_node_ids(key, part):
    part_total = ELEMS // E_DEV
    element = jnp.arange(ELEMS, dtype=jnp.int32)
    owner_part = element // E_DEV
    lowest = jnp.maximum(owner_part - 1, 0) * NODE_DEV
    highest = jnp.minimum(owner_part + 2, part_total) * NODE_DEV
    chosen = jax.random.randint(key, (ELEMS, ENODES), lowest[:, None], highest[:, None], dtype=jnp.int32)
    chosen = chosen.at[0, 0].set(0)
    chosen = chosen.at[ELEMS - 1, ENODES - 1].set(NODES - 1)
    return chosen


def block_scale(own_key, extent, pieces, low, top_value):
    level, own = 1.0, jax.random.fold_in(own_key, 6)
    for dim, shards_of in pieces:
        steps = jnp.exp(jax.random.uniform(jax.random.fold_in(own, dim), (shards_of,), jnp.float32, low / len(pieces), top_value / len(pieces)))
        level = level * jnp.repeat(steps, extent[dim] // shards_of).reshape([-1 if axis == dim else 1 for axis in range(len(extent))])
    return level


def gaussian(stream_key, dims, deviation, limit, split=(), kind=jnp.bfloat16):
    result = deviation * jax.random.normal(stream_key, dims, jnp.float32)
    if split:
        result = result * block_scale(stream_key, dims, split, -0.22, 0.18)
    return jnp.clip(result, -limit, limit).astype(kind)


def setup_inputs(seed: int = 0) -> dict:
    keys = jax.random.split(jax.random.key(seed), 9)
    return {
        "adjoint_start": gaussian(keys[0], (ELEMS, RHS, B), 1.0, 6.0, ((0, 8), (2, 4)), jnp.float32),
        "right_sides": gaussian(keys[1], (ELEMS, RHS, B), 1.0, 6.0, ((0, 8), (2, 4)), jnp.float32),
        "jac_blocks": gaussian(keys[2], (ELEMS, FACES + 1, B, B), (7 * B) ** -0.5, 0.125, ((0, 8), (2, 4))),
        "block_inverse": gaussian(keys[3], (ELEMS, B, B), (4 * B) ** -0.5, 0.15625, ((0, 8), (1, 4))),
        "neighbours": draw_neighbours(jax.random.fold_in(keys[8], 71), 0),
        "pseudo_shift": jnp.clip(jnp.exp(math.log(2.0) - 2.0794415 * jax.random.uniform(keys[5], (ELEMS,), jnp.float32) ** block_scale(keys[5], (ELEMS,), ((0, 8),), -0.2, 0.2)), 0.25, 2.0),
        "shape_partials": gaussian(keys[6], (ELEMS, B, NQ), B ** -0.5, 0.3125, ((0, 8), (1, 4))),
        "node_ids": draw_node_ids(jax.random.fold_in(keys[8], 71), 0),
    }


def reference(adjoint_start, right_sides, jac_blocks, block_inverse, neighbours, pseudo_shift, shape_partials, node_ids):
    part_total = ELEMS // E_DEV
    element = jnp.arange(ELEMS, dtype=jnp.int32)
    slots = jnp.concatenate([element[:, None], neighbours], axis=1)
    jac_parts = jac_blocks.reshape(part_total, E_DEV, FACES + 1, B, B)
    inv_parts = block_inverse.reshape(part_total, E_DEV, B, B)
    shape_parts = shape_partials.reshape(part_total, E_DEV, B, NQ)
    high = lax.Precision.HIGHEST

    def apply_jac(pair):
        blocks, picked = pair
        return jnp.einsum("ekrc,ekjc->ejr", blocks.astype(jnp.float32), picked.astype(jnp.float32), precision=high)

    def apply_inv(pair):
        blocks, resid = pair
        return jnp.einsum("erc,ejc->ejr", blocks.astype(jnp.float32), resid.astype(jnp.float32), precision=high)

    def apply_shape(pair):
        half, blocks = pair
        return jnp.einsum("ejr,erq->ejq", half.astype(jnp.float32), blocks.astype(jnp.float32), precision=high)

    adjoint = adjoint_start
    for sweep in range(SWEEPS):
        adj_half = adjoint.astype(jnp.bfloat16)
        picked = adj_half[slots].reshape(part_total, E_DEV, FACES + 1, RHS, B)
        product = lax.map(apply_jac, (jac_parts, picked)).reshape(ELEMS, RHS, B)
        image = pseudo_shift[:, None, None] * adjoint + product
        resid_half = (right_sides - image).astype(jnp.bfloat16)
        update = lax.map(apply_inv, (inv_parts, resid_half.reshape(part_total, E_DEV, RHS, B)))
        adjoint = adjoint + update.reshape(ELEMS, RHS, B)
    final_half = adjoint.astype(jnp.bfloat16)
    weighted = -lax.map(apply_shape, (final_half.reshape(part_total, E_DEV, RHS, B), shape_parts))
    weighted = weighted.reshape(ELEMS, RHS, ENODES, 3)
    values = jnp.transpose(weighted, (0, 2, 1, 3)).reshape(ELEMS * ENODES, RHS * 3)
    gradient = jax.ops.segment_sum(values, node_ids.reshape(-1), NODES)
    return adjoint, gradient.T
```

```python
import functools

import jax
import jax.numpy as jnp
from jax import lax
from jax.experimental import pallas as pl
from jax.experimental.pallas import tpu as pltpu
from jax.sharding import PartitionSpec as P

SWEEPS = 2
NODE_DEV = 768
HALF = jnp.bfloat16
FULL = jnp.float32
LANES = 128
PICK = 8
NT = (((1,), (1,)), ((), ()))
VMEM = pl.BlockSpec(memory_space=pltpu.VMEM)
SMEM = pl.BlockSpec(memory_space=pltpu.SMEM)
ANY = pl.BlockSpec(memory_space=pl.ANY)
MIB = 1024 * 1024


def round_up(size, unit):
    return -(-size // unit) * unit


def iota(shape, dim):
    return lax.broadcasted_iota(jnp.int32, shape, dim)


def hit(condition):
    return jnp.where(condition, 1.0, 0.0)


def call(kernel, name, args, specs, outs, scratch=(), limit=16, flops=0, moved=0):
    return pl.pallas_call(
        kernel,
        in_specs=specs,
        out_specs=[VMEM] * len(outs),
        out_shape=outs,
        scratch_shapes=list(scratch),
        compiler_params=pltpu.CompilerParams(vmem_limit_bytes=limit * MIB),
        cost_estimate=pl.CostEstimate(flops=flops, bytes_accessed=moved, transcendentals=0),
        name=name,
    )(*args)


def over_blk(block):
    count = lax.axis_size("blk")
    return [lax.ppermute(block, "blk", [(i, i ^ k) for i in range(count)]) for k in range(1, count)]


def to_mate(block):
    return lax.ppermute(block, "dom", [(i, i ^ 1) for i in range(lax.axis_size("dom"))])


def to_far(block):
    count = lax.axis_size("dom")
    return lax.ppermute(block, "dom", [(i, (((i + 1) ^ 1) - 1) % count) for i in range(count)])


def round_kernel(adj_ref, half_ref):
    adj = adj_ref[...]
    rows = half_ref.shape[0] - adj.shape[0]
    padded = jnp.concatenate([adj, jnp.zeros((rows, adj.shape[1]), FULL)], axis=0)
    half_ref[...] = padded.astype(HALF)


def prepare_kernel(
    jac_ref, inv_ref, shape_ref, nb_ref, shift_ref, ids_ref,
    jac_out, inv_out, shape_out, pick_out, shift_out, low_out, target_out, spread_out,
    jac_buf, inv_buf, shape_buf, sems,
):
    elements, slots, width, full = jac_ref.shape
    stride = round_up(full, LANES)
    coords = shape_ref.shape[2]
    copies = [pltpu.make_async_copy(jac_ref.at[e], jac_buf.at[e], sems.at[e]) for e in range(elements)]
    copies.append(pltpu.make_async_copy(inv_ref, inv_buf, sems.at[elements]))
    copies.append(pltpu.make_async_copy(shape_ref, shape_buf, sems.at[elements + 1]))
    for copy in copies:
        copy.start()

    dom = lax.axis_index("dom")
    blk = lax.axis_index("blk")
    odd = lax.rem(dom, 2)

    def window(ids, count):
        place = ids - dom * count
        below = jnp.where(place < 0, 1, 0)
        above = jnp.where(place >= count, 1, 0)
        mate = odd * below + (1 - odd) * above
        return 2 * (below + above) - mate, place + (below - above) * count

    rows_part = round_up(3 * elements, 16)
    shape = (PICK, pick_out.shape[1])
    row, lane = iota(shape, 0), iota(shape, 1)
    offset = jnp.where(row < 3, lane - elements * row, -1)

    def pick_rows(e, k):
        if k == 0:
            return hit(offset == e)
        part, inside = window(nb_ref[k - 1, e], elements)
        return hit(offset == part * rows_part + inside)

    @pl.loop(0, elements // 2)
    def _(pair):
        for k in range(slots):
            block = jnp.concatenate([pick_rows(2 * pair, k), pick_rows(2 * pair + 1, k)], axis=0)
            start = pl.multiple_of(k * elements * PICK + pair * 2 * PICK, 16)
            pick_out[pl.ds(start, 2 * PICK), :] = block.astype(HALF)

    shift_out[...] = jnp.zeros(shift_out.shape, FULL)
    for e in range(elements):
        shift_out[pl.ds(e, 3, stride=elements), :] = jnp.full((3, shift_out.shape[1]), shift_ref[e], FULL)

    ids = ids_ref[...]
    blks = lax.axis_size("blk")
    span = NODE_DEV // blks
    part, inside = window(ids, NODE_DEV)
    owner = jnp.zeros_like(inside)
    for cut in range(1, blks):
        owner = owner + jnp.where(inside >= cut * span, 1, 0)
    low = inside - owner * span
    target_out[...] = part * blks + (owner ^ blk)
    shape = (span, LANES)
    for group in range(ids.shape[0]):
        same = iota(shape, 0) == low[group : group + 1, :]
        low_out[:, group * LANES : (group + 1) * LANES] = hit(same).astype(HALF)

    deep = spread_out.shape[0] // 2
    shape = spread_out.shape
    row, lane = iota(shape, 0), iota(shape, 1)
    axis = jnp.where(lane >= LANES, 1, 0) + jnp.where(lane >= 2 * LANES, 1, 0)
    side = lane - axis * LANES
    second = jnp.where(side >= LANES // 2, 1, 0)
    source = second * deep + 3 * (side - second * (LANES // 2)) + axis
    spread_out[...] = hit(row == source).astype(HALF)

    pad = jnp.zeros((width, stride - full), HALF)
    for e in range(elements):
        copies[e].wait()
        for k in range(slots):
            jac_out[e * width : (e + 1) * width, k * stride : k * stride + full] = jac_buf[e, k]
            if stride > full:
                jac_out[e * width : (e + 1) * width, k * stride + full : (k + 1) * stride] = pad
    copies[elements].wait()
    copies[elements + 1].wait()
    for e in range(elements):
        inv_out[e * width : (e + 1) * width, :full] = inv_buf[e]
        if stride > full:
            inv_out[e * width : (e + 1) * width, full:] = pad
        shape_out[e, :, :coords] = shape_buf[e]
        shape_out[e, :, coords:] = jnp.zeros((width, shape_out.shape[2] - coords), HALF)


def put_columns(blocks, stride):
    blk = lax.axis_index("blk")
    width = blocks[0].shape[1]
    shape = (width, stride)
    ahead = iota(shape, 1) - iota(shape, 0)
    total = 0.0
    for k, block in enumerate(blocks):
        place = hit(ahead == (blk ^ k) * width).astype(HALF)
        total = total + jnp.dot(block, place, preferred_element_type=FULL)
    return total.astype(HALF)


def columns_kernel(*refs):
    *blocks, out_ref = refs
    out_ref[...] = put_columns([ref[...] for ref in blocks], out_ref.shape[1])


def residual_kernel(own_ref, mate_ref, far_ref, pick_ref, jac_ref, shift_ref, adj_ref, rhs_ref, out_ref, image):
    rows, width = adj_ref.shape
    elements = rows // 3
    stride = own_ref.shape[1]
    slots = jac_ref.shape[1] // stride
    stacked = [own_ref[...], mate_ref[...], far_ref[...]]
    short = pick_ref.shape[1] - 3 * own_ref.shape[0]
    if short:
        stacked.append(jnp.zeros((short, stride), HALF))
    stacked = jnp.concatenate(stacked, axis=0)
    picked = jnp.dot(pick_ref[...], stacked, preferred_element_type=FULL).astype(HALF)
    image[...] = jnp.zeros(image.shape, FULL)
    for pair in range(elements // 2):
        starts = [k * elements * PICK + pair * 2 * PICK for k in range(slots)]
        left = jnp.concatenate([picked[start : start + 2 * PICK] for start in starts], axis=1)
        for side in range(2):
            e = 2 * pair + side
            blocks = jac_ref[e * width : (e + 1) * width, :]
            product = lax.dot_general(left, blocks, NT, preferred_element_type=FULL)
            first = side * PICK
            image[pl.ds(e, 3, stride=elements), :width] = product[first : first + 3]
    total = shift_ref[:rows, :width] * adj_ref[...] + image[:rows, :width]
    resid = rhs_ref[...] - total
    resid = jnp.concatenate([resid, jnp.zeros((out_ref.shape[0] - rows, width), FULL)], axis=0)
    out_ref[...] = resid.astype(HALF)


def element_of_row(shape, elements, copies=3):
    row = iota(shape, 0)
    for step in range(1, copies + 1):
        row = row - jnp.where(iota(shape, 0) >= step * elements, elements, 0)
    return row


def updated(resid_refs, inv_ref, adj_ref):
    rows, width = adj_ref.shape
    elements = rows // 3
    resid = put_columns([ref[...] for ref in resid_refs], inv_ref.shape[1])
    shape = (resid.shape[0], width)
    owner = element_of_row(shape, elements)
    update = jnp.zeros(shape, FULL)
    for e in range(elements):
        blocks = inv_ref[e * width : (e + 1) * width, :]
        product = lax.dot_general(resid, blocks, NT, preferred_element_type=FULL)
        update = jnp.where(owner == e, product, update)
    adj = jnp.concatenate([adj_ref[...], jnp.zeros((shape[0] - rows, width), FULL)], axis=0)
    return jnp.where(iota(shape, 0) < rows, adj + update, 0.0)


def update_kernel(*refs):
    *resid_refs, inv_ref, adj_ref, adj_out, half_out = refs
    adj = updated(resid_refs, inv_ref, adj_ref)
    adj_out[...] = adj[: adj_out.shape[0]]
    half_out[...] = adj.astype(HALF)


def split(value):
    top = value.astype(HALF)
    return top, (value - top.astype(FULL)).astype(HALF)


def gradient_kernel(*refs):
    blks = lax.axis_size("blk")
    resid_refs = refs[:blks]
    inv_ref, adj_ref, shape_ref, spread_ref, low_ref, target_ref, adj_out = refs[blks : blks + 7]
    piece_outs = refs[blks + 7 : 2 * blks + 7]
    sorted_ref, left_ref, sums_ref = refs[2 * blks + 7 :]
    adj = updated(resid_refs, inv_ref, adj_ref)
    adj_out[...] = adj[: adj_out.shape[0]]
    half = adj.astype(HALF)
    elements = adj_out.shape[0] // 3
    pairs = elements // 2
    tall = round_up(3 * pairs, 16)
    shape = (tall, half.shape[0])
    row, lane = iota(shape, 0), iota(shape, 1)
    group = jnp.where(row >= pairs, 1, 0) + jnp.where(row >= 2 * pairs, 1, 0)
    source = 2 * (row - group * pairs) + group * elements
    source = jnp.where(row < 3 * pairs, source, -2)
    weighted = []
    shape = (tall, shape_ref.shape[2])
    owner = element_of_row(shape, pairs)
    for side in range(2):
        chosen = jnp.dot(hit(lane == source + side).astype(HALF), half, preferred_element_type=FULL).astype(HALF)
        total = jnp.zeros(shape, FULL)
        for pair in range(pairs):
            product = jnp.dot(chosen, shape_ref[2 * pair + side], preferred_element_type=FULL)
            total = jnp.where(owner == pair, product, total)
        weighted.append(total)
    weighted = jnp.concatenate(weighted, axis=1)
    value = 0.0
    for piece in split(weighted):
        value = value + jnp.dot(piece, spread_ref[...], preferred_element_type=FULL)
    top, rest = split(value)
    sorted_ref[:tall] = top.astype(FULL)
    sorted_ref[tall:] = rest.astype(FULL)
    deep = 16
    for pair in range(pairs):
        lanes = slice(pair * LANES, (pair + 1) * LANES)
        mine = iota((deep, LANES), 0) == target_ref[pair : pair + 1, :]
        for part in range(2):
            for j in range(3):
                for c in range(3):
                    at = part * tall + j * pairs + pair
                    values = sorted_ref[at : at + 1, c * LANES : (c + 1) * LANES]
                    start = (part * 9 + j * 3 + c) * deep
                    left_ref[start : start + deep, lanes] = jnp.where(mine, values, 0.0).astype(HALF)
    sums = lax.dot_general(left_ref[...], low_ref[...], NT, preferred_element_type=FULL)
    span = low_ref.shape[0]
    sums = -(sums[: 9 * deep] + sums[9 * deep :])
    tiles = [(tile, tile * LANES, min(span, (tile + 1) * LANES)) for tile in range(sums_ref.shape[0])]
    for tile, start, stop in tiles:
        sums_ref[tile, :, : stop - start] = sums[:, start:stop]
    for k, out_ref in enumerate(piece_outs):
        out_ref[...] = jnp.zeros(out_ref.shape, out_ref.dtype)
        for part in range(3):
            for tile, start, stop in tiles:
                found = sums_ref[tile, pl.ds(part * blks + k, 9, stride=deep), :]
                out_ref[part * 16 : part * 16 + 9, start:stop] = found[:, : stop - start]


def combine_kernel(*refs):
    *piece_refs, own_out, mate_out, far_out = refs
    total = piece_refs[0][...]
    for ref in piece_refs[1:]:
        total = total + ref[...]
    own_out[...] = total[:16]
    mate_out[...] = total[16:32]
    far_out[...] = total[32:48]


def local(
    adjoint_start,
    right_sides,
    jac_blocks,
    block_inverse,
    neighbours,
    pseudo_shift,
    shape_partials,
    node_ids,
):
    elements, sides, width = adjoint_start.shape
    slots, full = jac_blocks.shape[1], jac_blocks.shape[3]
    enodes = node_ids.shape[1]
    coords = shape_partials.shape[2]
    rows = sides * elements
    tall = round_up(rows, 16)
    stride = round_up(full, LANES)
    blks = lax.axis_size("blk")
    span = NODE_DEV // blks
    stacked = round_up(3 * tall, LANES)
    entries = elements * enodes
    sorted_coords = round_up(coords, LANES)

    adj = jnp.transpose(adjoint_start, (1, 0, 2)).reshape(rows, width)
    rhs = jnp.transpose(right_sides, (1, 0, 2)).reshape(rows, width)
    half_shape = jax.ShapeDtypeStruct((tall, width), HALF)
    (half,) = call(round_kernel, "round", [adj], [VMEM], [half_shape])

    jac, inv, shapes, pick, shift, low, target, spread = call(
        prepare_kernel,
        "prepare",
        [jac_blocks, block_inverse, shape_partials, neighbours.T, pseudo_shift, node_ids.reshape(-1, LANES)],
        [ANY, ANY, ANY, SMEM, SMEM, VMEM],
        [
            pltpu.VMEM((elements * width, slots * stride), HALF),
            pltpu.VMEM((elements * width, stride), HALF),
            pltpu.VMEM((elements, width, sorted_coords), HALF),
            pltpu.VMEM((slots * elements * PICK, stacked), HALF),
            pltpu.VMEM((tall, LANES), FULL),
            pltpu.VMEM((span, entries), HALF),
            pltpu.VMEM((entries // LANES, LANES), jnp.int32),
            pltpu.VMEM((2 * sorted_coords, 3 * LANES), HALF),
        ],
        scratch=[
            pltpu.VMEM(jac_blocks.shape, HALF),
            pltpu.VMEM(block_inverse.shape, HALF),
            pltpu.VMEM(shape_partials.shape, HALF),
            pltpu.SemaphoreType.DMA((elements + 2,)),
        ],
        limit=20,
        flops=0,
        moved=24 * MIB,
    )

    for sweep in range(SWEEPS):
        blocks = [half] + over_blk(half)
        wide = jax.ShapeDtypeStruct((tall, stride), HALF)
        (own,) = call(columns_kernel, "columns", blocks, [VMEM] * blks, [wide])
        mate, far = to_mate(own), to_far(own)
        (resid,) = call(
            residual_kernel,
            "residual",
            [own, mate, far, pick, jac, shift, adj, rhs],
            [VMEM] * 8,
            [half_shape],
            scratch=[pltpu.VMEM((tall, LANES), FULL)],
        )
        resids = [resid] + over_blk(resid)
        adj_shape = jax.ShapeDtypeStruct((rows, width), FULL)
        if sweep < SWEEPS - 1:
            adj, half = call(
                update_kernel, "update", resids + [inv, adj], [VMEM] * (blks + 2), [adj_shape, half_shape]
            )
    piece = jax.ShapeDtypeStruct((3 * 16, span), FULL)
    adj, *pieces = call(
        gradient_kernel,
        "gradient",
        resids + [inv, adj, shapes, spread, low, target],
        [VMEM] * (blks + 6),
        [adj_shape] + [piece] * blks,
        scratch=[
            pltpu.VMEM((2 * round_up(rows // 2, 16), 3 * LANES), FULL),
            pltpu.VMEM((2 * 9 * 16, entries), HALF),
            pltpu.VMEM((-(-span // LANES), 9 * 16, LANES), FULL),
        ],
    )
    count = lax.axis_size("blk")
    received = [
        lax.ppermute(pieces[k], "blk", [(i, i ^ k) for i in range(count)]) for k in range(1, count)
    ]
    third = jax.ShapeDtypeStruct((16, span), FULL)
    own, mate, far = call(combine_kernel, "combine", [pieces[0]] + received, [VMEM] * blks, [third] * 3)
    gradient = (own + to_mate(mate) + to_far(far))[:9]
    adjoint = jnp.transpose(adj.reshape(sides, elements, width), (1, 0, 2))
    return (adjoint, gradient)


def solution(mesh):
    in_specs = (
        P("dom", None, "blk"),
        P("dom", None, "blk"),
        P("dom", None, "blk", None),
        P("dom", "blk", None),
        P("dom", None),
        P("dom"),
        P("dom", "blk", None),
        P("dom", None),
    )
    out_specs = (P("dom", None, "blk"), P(None, ("dom", "blk")))
    return jax.shard_map(local, mesh=mesh, in_specs=in_specs, out_specs=out_specs, check_vma=False)
```

```python
import functools

import jax
import jax.numpy as jnp
from jax import lax
from jax.experimental import pallas as pl
from jax.experimental.pallas import tpu as pltpu
from jax.sharding import PartitionSpec as P

SWEEPS = 2
NODE_DEV = 768
HALF = jnp.bfloat16
FULL = jnp.float32
LANES = 128
PICK = 8
NT = (((1,), (1,)), ((), ()))
VMEM = pl.BlockSpec(memory_space=pltpu.VMEM)
HBM = pl.BlockSpec(memory_space=pltpu.HBM)
EARLY, MIDDLE = 4, 12
MIB = 1024 * 1024


def round_up(size, unit):
    return -(-size // unit) * unit


def iota(shape, dim):
    return lax.broadcasted_iota(jnp.int32, shape, dim)


def hit(condition):
    return jnp.where(condition, 1.0, 0.0)


def in_hbm(array):
    return pltpu.with_memory_space_constraint(array, pltpu.HBM)


def call(kernel, name, args, specs, outs, scratch=(), limit=16, flops=0, moved=0):
    return pl.pallas_call(
        kernel,
        in_specs=specs,
        out_specs=[VMEM] * len(outs),
        out_shape=outs,
        scratch_shapes=list(scratch),
        compiler_params=pltpu.CompilerParams(vmem_limit_bytes=limit * MIB),
        cost_estimate=pl.CostEstimate(flops=flops, bytes_accessed=moved, transcendentals=0),
        name=name,
    )(*args)


def far_first():
    return list(reversed(range(1, lax.axis_size("blk"))))


def far_last():
    farthest, *others = far_first()
    return [*others, farthest]


def over_blk(block, order):
    count = lax.axis_size("blk")
    return [lax.ppermute(block, "blk", [(i, i ^ k) for i in range(count)]) for k in order]


def to_mate(block):
    return lax.ppermute(block, "dom", [(i, i ^ 1) for i in range(lax.axis_size("dom"))])


def to_far(block):
    count = lax.axis_size("dom")
    return lax.ppermute(block, "dom", [(i, (((i + 1) ^ 1) - 1) % count) for i in range(count)])


def rounded(block, rows):
    short = rows - block.shape[0]
    if short:
        block = jnp.concatenate([block, jnp.zeros((short, block.shape[1]), block.dtype)], axis=0)
    return block.astype(HALF)


def window(ids, count):
    dom = lax.axis_index("dom")
    odd = lax.rem(dom, 2)
    place = ids - dom * count
    below = jnp.where(place < 0, 1, 0)
    above = jnp.where(place >= count, 1, 0)
    mate = odd * below + (1 - odd) * above
    return 2 * (below + above) - mate, place + (below - above) * count


def started(pairs, sems):
    copies = [pltpu.make_async_copy(source, target, sems.at[i]) for i, (source, target) in enumerate(pairs)]
    for copy in copies:
        copy.start()
    return copies


def slots_kernel(
    nb_hbm, shift_hbm, jac_hbm, adj_hbm, rhs_hbm,
    pick_out, shift_out, jac_out, adj_out, rhs_out, nb_ref, shift_ref, sems,
):
    pairs = [(nb_hbm, nb_ref), (shift_hbm, shift_ref), (adj_hbm, adj_out), (rhs_hbm, rhs_out)]
    kept = jac_out.shape[0]
    copies = started(pairs + [(jac_hbm.at[pl.ds(0, kept)], jac_out)], sems)
    copies[0].wait()
    faces, elements = nb_ref.shape
    rows_part = round_up(3 * elements, 16)
    part, inside = window(nb_ref[...], elements)
    bases = jnp.concatenate([iota((1, elements), 1), part * rows_part + inside], axis=0).astype(FULL)
    deep = elements * PICK
    shape = (deep, elements)
    behind = iota(shape, 0) - PICK * iota(shape, 1)
    owner = hit(jnp.logical_and(behind >= 0, behind < PICK)).astype(HALF)
    columns = lax.dot_general(owner, bases.astype(HALF), NT, preferred_element_type=FULL)
    shape = (elements, PICK, pick_out.shape[1])
    row, lane = iota(shape, 1).reshape(deep, -1), iota(shape, 2).reshape(deep, -1)
    offset = jnp.where(row < 3, lane - elements * row, -1).astype(FULL)
    for k in range(faces + 1):
        pick_out[k * deep : (k + 1) * deep, :] = hit(offset == columns[:, k : k + 1]).astype(HALF)
    shift_out[...] = jnp.zeros(shift_out.shape, FULL)
    copies[1].wait()
    for e in range(elements):
        shift_out[pl.ds(e, 3, stride=elements), :] = jnp.full((3, shift_out.shape[1]), shift_ref[e], FULL)
    for copy in copies[2:]:
        copy.wait()


def read_kernel(first, source, out_ref, sems):
    for copy in started([(source.at[pl.ds(first, out_ref.shape[0])], out_ref)], sems):
        copy.wait()


def nodes_kernel(ids_hbm, shape_hbm, low_out, target_out, spread_out, shape_out, ids_ref, sems):
    copies = started([(ids_hbm, ids_ref), (shape_hbm, shape_out)], sems)
    copies[0].wait()
    blk = lax.axis_index("blk")
    blks = lax.axis_size("blk")
    span = NODE_DEV // blks
    ids = ids_ref[...]
    pairs = ids.shape[0] // 2
    ids = [jnp.concatenate([ids[2 * p : 2 * p + 1], ids[2 * p + 1 : 2 * p + 2]], axis=1) for p in range(pairs)]
    part, inside = window(jnp.concatenate(ids, axis=0), NODE_DEV)
    owner = jnp.zeros_like(inside)
    for cut in range(1, blks):
        owner = owner + jnp.where(inside >= cut * span, 1, 0)
    low = inside - owner * span
    target_out[...] = part * blks + (owner ^ blk)
    shape = (span, LANES)
    for group in range(pairs):
        same = iota(shape, 0) == low[group : group + 1, :]
        low_out[:, group * LANES : (group + 1) * LANES] = hit(same).astype(HALF)

    deep = spread_out.shape[0] // 2
    shape = spread_out.shape
    row, lane = iota(shape, 0), iota(shape, 1)
    axis = jnp.where(lane >= LANES, 1, 0) + jnp.where(lane >= 2 * LANES, 1, 0)
    side = lane - axis * LANES
    second = jnp.where(side >= LANES // 2, 1, 0)
    source = second * deep + 3 * (side - second * (LANES // 2)) + axis
    spread_out[...] = hit(row == source).astype(HALF)
    for copy in copies[1:]:
        copy.wait()


def widened(block, lanes):
    short = lanes - block.shape[1]
    if short == 0:
        return block
    return jnp.concatenate([block, jnp.zeros((block.shape[0], short), block.dtype)], axis=1)


def put_columns(blocks, order, stride):
    blk = lax.axis_index("blk")
    width = blocks[0].shape[1]
    shape = (width, stride)
    ahead = iota(shape, 1) - iota(shape, 0)
    total = 0.0
    for k, block in zip([0, *order], blocks):
        place = hit(ahead == (blk ^ k) * width).astype(HALF)
        total = total + jnp.dot(block, place, preferred_element_type=FULL)
    return total.astype(HALF)


def columns_kernel(order, *refs):
    *blocks, out_ref = refs
    rows, stride = out_ref.shape
    out_ref[...] = put_columns([rounded(ref[...], rows) for ref in blocks], order, stride)


def first_residual_kernel(
    own_ref, mate_ref, far_ref, pick_ref, shift_ref, adj_ref, rhs_ref, early_ref, middle_ref, jac_hbm, inv_hbm,
    out_ref, late_out, inv_out, image, sems,
):
    late = late_out.shape[0]
    copies = started([(jac_hbm.at[pl.ds(jac_hbm.shape[0] - late, late)], late_out), (inv_hbm, inv_out)], sems)
    residual(
        own_ref, mate_ref, far_ref, pick_ref, shift_ref, adj_ref, rhs_ref, [early_ref, middle_ref, late_out], out_ref,
        image, copies[0].wait,
    )
    copies[1].wait()


def residual_kernel(
    own_ref, mate_ref, far_ref, pick_ref, shift_ref, adj_ref, rhs_ref, early_ref, middle_ref, late_ref, out_ref, image
):
    residual(
        own_ref, mate_ref, far_ref, pick_ref, shift_ref, adj_ref, rhs_ref, [early_ref, middle_ref, late_ref], out_ref,
        image, lambda: None,
    )


def residual(
    own_ref, mate_ref, far_ref, pick_ref, shift_ref, adj_ref, rhs_ref, jac_refs, out_ref, image, wait_late
):
    jac = [ref.at[e] for ref in jac_refs for e in range(ref.shape[0])]
    rows, width = adj_ref.shape
    elements = rows // 3
    stride = own_ref.shape[1]
    slots = jac[0].shape[0]
    stacked = [own_ref[...], mate_ref[...], far_ref[...]]
    short = pick_ref.shape[1] - 3 * own_ref.shape[0]
    if short:
        stacked.append(jnp.zeros((short, stride), HALF))
    stacked = jnp.concatenate(stacked, axis=0)
    picked = jnp.dot(pick_ref[...], stacked, preferred_element_type=FULL).astype(HALF)
    image[...] = jnp.zeros(image.shape, FULL)
    for pair in range(elements // 2):
        starts = [k * elements * PICK + pair * 2 * PICK for k in range(slots)]
        left = jnp.concatenate([picked[start : start + 2 * PICK] for start in starts], axis=1)
        for side in range(2):
            e = 2 * pair + side
            if e == elements - jac_refs[-1].shape[0]:
                wait_late()
            blocks = jnp.concatenate([widened(jac[e][k], stride) for k in range(slots)], axis=1)
            product = lax.dot_general(left, blocks, NT, preferred_element_type=FULL)
            first = side * PICK
            image[pl.ds(e, 3, stride=elements), :width] = product[first : first + 3]
    total = shift_ref[:rows, :width] * adj_ref[...] + image[:rows, :width]
    resid = rhs_ref[...] - total
    resid = jnp.concatenate([resid, jnp.zeros((out_ref.shape[0] - rows, width), FULL)], axis=0)
    out_ref[...] = resid.astype(HALF)


def element_of_row(shape, elements, copies=3):
    row = iota(shape, 0)
    for step in range(1, copies + 1):
        row = row - jnp.where(iota(shape, 0) >= step * elements, elements, 0)
    return row


def updated(resid_refs, inv_ref, adj_ref, update):
    rows, width = adj_ref.shape
    elements = rows // 3
    stride = round_up(inv_ref.shape[2], LANES)
    resid = put_columns([ref[...] for ref in resid_refs], far_first(), stride)
    shape = (elements, PICK, resid.shape[0])
    deep = elements * PICK
    element, row, lane = [iota(shape, dim).reshape(deep, -1) for dim in range(3)]
    pick = hit(jnp.where(row < 3, row * elements + element, -1) == lane).astype(HALF)
    resid = jnp.dot(pick, resid, preferred_element_type=FULL).astype(HALF)
    update[...] = jnp.zeros(update.shape, FULL)
    for pair in range(elements // 2):
        left = resid[pair * 2 * PICK : (pair + 1) * 2 * PICK]
        for side in range(2):
            e = 2 * pair + side
            product = lax.dot_general(left, widened(inv_ref[e], stride), NT, preferred_element_type=FULL)
            first = side * PICK
            update[pl.ds(e, 3, stride=elements), :width] = product[first : first + 3]
    short = jnp.zeros((update.shape[0] - rows, width), FULL)
    return jnp.concatenate([adj_ref[...] + update[:rows, :width], short], axis=0)


def update_kernel(*refs):
    *resid_refs, inv_ref, adj_ref, adj_out, half_out, update = refs
    adj = updated(resid_refs, inv_ref, adj_ref, update)
    adj_out[...] = adj[: adj_out.shape[0]]
    half_out[...] = adj.astype(HALF)


def split(value):
    top = value.astype(HALF)
    return top, (value - top.astype(FULL)).astype(HALF)


def gradient_kernel(*refs):
    blks = lax.axis_size("blk")
    resid_refs = refs[:blks]
    inv_ref, adj_ref, shape_ref, spread_ref, low_ref, target_ref, adj_out = refs[blks : blks + 7]
    piece_outs = refs[blks + 7 : 2 * blks + 7]
    sorted_ref, left_ref, sums_ref, update = refs[2 * blks + 7 :]
    adj = updated(resid_refs, inv_ref, adj_ref, update)
    adj_out[...] = adj[: adj_out.shape[0]]
    half = adj.astype(HALF)
    elements = adj_out.shape[0] // 3
    pairs = elements // 2
    tall = round_up(3 * pairs, 16)
    shape = (tall, half.shape[0])
    row, lane = iota(shape, 0), iota(shape, 1)
    group = jnp.where(row >= pairs, 1, 0) + jnp.where(row >= 2 * pairs, 1, 0)
    source = 2 * (row - group * pairs) + group * elements
    source = jnp.where(row < 3 * pairs, source, -2)
    weighted = []
    coords = shape_ref.shape[2]
    shape = (tall, coords)
    owner = element_of_row(shape, pairs)
    for side in range(2):
        chosen = jnp.dot(hit(lane == source + side).astype(HALF), half, preferred_element_type=FULL).astype(HALF)
        total = jnp.zeros(shape, FULL)
        for pair in range(pairs):
            product = jnp.dot(chosen, shape_ref[2 * pair + side], preferred_element_type=FULL)
            total = jnp.where(owner == pair, product, total)
        weighted.append(widened(total, spread_ref.shape[0] // 2))
    weighted = jnp.concatenate(weighted, axis=1)
    value = 0.0
    for piece in split(weighted):
        value = value + jnp.dot(piece, spread_ref[...], preferred_element_type=FULL)
    top, rest = split(value)
    sorted_ref[:tall] = top.astype(FULL)
    sorted_ref[tall:] = rest.astype(FULL)
    deep = 16
    for pair in range(pairs):
        lanes = slice(pair * LANES, (pair + 1) * LANES)
        mine = iota((deep, LANES), 0) == target_ref[pair : pair + 1, :]
        for part in range(2):
            for j in range(3):
                for c in range(3):
                    at = part * tall + j * pairs + pair
                    values = sorted_ref[at : at + 1, c * LANES : (c + 1) * LANES]
                    start = (part * 9 + j * 3 + c) * deep
                    left_ref[start : start + deep, lanes] = jnp.where(mine, values, 0.0).astype(HALF)
    sums = lax.dot_general(left_ref[...], low_ref[...], NT, preferred_element_type=FULL)
    span = low_ref.shape[0]
    sums = -(sums[: 9 * deep] + sums[9 * deep :])
    tiles = [(tile, tile * LANES, min(span, (tile + 1) * LANES)) for tile in range(sums_ref.shape[0])]
    for tile, start, stop in tiles:
        sums_ref[tile, :, : stop - start] = sums[:, start:stop]
    for k, out_ref in enumerate(piece_outs):
        for part in range(3):
            for tile, start, stop in tiles:
                found = sums_ref[tile, pl.ds(part * blks + k, 9, stride=deep), :][:, : stop - start]
                found = jnp.concatenate([found, jnp.zeros((7, stop - start), FULL)], axis=0)
                out_ref[part * 16 : (part + 1) * 16, start:stop] = found.astype(out_ref.dtype)


def combine_kernel(*refs):
    *piece_refs, own_out, mate_out, far_out = refs
    total = piece_refs[0][...]
    for ref in piece_refs[1:]:
        total = total + ref[...].astype(FULL)
    own_out[...] = total[:16]
    mate_out[...] = total[16:32]
    far_out[...] = total[32:48]


def local(
    adjoint_start,
    right_sides,
    jac_blocks,
    block_inverse,
    neighbours,
    pseudo_shift,
    shape_partials,
    node_ids,
):
    elements, sides, width = adjoint_start.shape
    slots, full = jac_blocks.shape[1], jac_blocks.shape[3]
    enodes = node_ids.shape[1]
    coords = shape_partials.shape[2]
    rows = sides * elements
    tall = round_up(rows, 16)
    stride = round_up(full, LANES)
    blks = lax.axis_size("blk")
    span = NODE_DEV // blks
    stacked = round_up(3 * tall, LANES)
    entries = elements * enodes
    sorted_coords = round_up(coords, LANES)

    adj_hbm = jnp.transpose(adjoint_start, (1, 0, 2)).reshape(rows, width)
    rhs = jnp.transpose(right_sides, (1, 0, 2)).reshape(rows, width)
    half_shape = jax.ShapeDtypeStruct((tall, width), HALF)
    jac_hbm = in_hbm(jac_blocks)

    early, middle = min(EARLY, elements - 2), min(MIDDLE, elements - 1 - EARLY)
    adj_shape = jax.ShapeDtypeStruct((rows, width), FULL)
    pick, shift, early_jac, adj, rhs = call(
        slots_kernel,
        "slots",
        [in_hbm(neighbours.T), in_hbm(pseudo_shift), jac_hbm, in_hbm(adj_hbm), in_hbm(rhs)],
        [HBM] * 5,
        [
            jax.ShapeDtypeStruct((slots * elements * PICK, stacked), HALF),
            jax.ShapeDtypeStruct((tall, LANES), FULL),
            pltpu.VMEM((early, *jac_blocks.shape[1:]), HALF),
            pltpu.VMEM((rows, width), FULL),
            pltpu.VMEM((rows, width), FULL),
        ],
        scratch=[
            pltpu.VMEM((slots - 1, elements), jnp.int32),
            pltpu.SMEM((elements,), FULL),
            pltpu.SemaphoreType.DMA((5,)),
        ],
        moved=3 * MIB,
    )
    middle_shape = pltpu.VMEM((middle, *jac_blocks.shape[1:]), HALF)
    late_shape = pltpu.VMEM((elements - early - middle, *jac_blocks.shape[1:]), HALF)
    inv_shape = pltpu.VMEM(block_inverse.shape, HALF)
    (middle_jac,) = call(
        functools.partial(read_kernel, early),
        "blocks",
        [jac_hbm],
        [HBM],
        [middle_shape],
        [pltpu.SemaphoreType.DMA((1,))],
        moved=6 * MIB,
    )
    low, target, spread, shapes = call(
        nodes_kernel,
        "nodes",
        [in_hbm(node_ids), in_hbm(shape_partials)],
        [HBM, HBM],
        [
            jax.ShapeDtypeStruct((span, entries), HALF),
            jax.ShapeDtypeStruct((entries // LANES, LANES), jnp.int32),
            jax.ShapeDtypeStruct((2 * sorted_coords, 3 * LANES), HALF),
            pltpu.VMEM(shape_partials.shape, HALF),
        ],
        scratch=[pltpu.VMEM(node_ids.shape, jnp.int32), pltpu.SemaphoreType.DMA((2,))],
        moved=3 * MIB,
    )

    for sweep in range(SWEEPS):
        order = far_last() if sweep else far_first()
        blocks = [half] + over_blk(half, order) if sweep else [adj] + over_blk(adj_hbm, order)
        wide = jax.ShapeDtypeStruct((tall, stride), HALF)
        (own,) = call(functools.partial(columns_kernel, order), "columns", blocks, [VMEM] * blks, [wide], moved=1 * MIB)
        far, mate = to_far(own), to_mate(own)
        inputs = [own, mate, far, pick, shift, adj, rhs, early_jac, middle_jac]
        image = pltpu.VMEM((tall, LANES), FULL)
        if sweep == 0:
            resid, late_jac, inv = call(
                first_residual_kernel,
                "first_residual",
                inputs + [jac_hbm, in_hbm(block_inverse)],
                [VMEM] * 9 + [HBM] * 2,
                [half_shape, late_shape, inv_shape],
                scratch=[image, pltpu.SemaphoreType.DMA((2,))],
                moved=16 * MIB,
            )
        else:
            (resid,) = call(
                residual_kernel, "residual", inputs + [late_jac], [VMEM] * 10, [half_shape], [image], moved=16 * MIB
            )
        resids = [resid] + over_blk(resid, far_first())
        if sweep < SWEEPS - 1:
            adj, half = call(
                update_kernel,
                "update",
                resids + [inv, adj],
                [VMEM] * (blks + 2),
                [adj_shape, half_shape],
                scratch=[pltpu.VMEM((tall, LANES), FULL)],
                moved=8 * MIB,
            )
    pieces = [jax.ShapeDtypeStruct((3 * 16, span), HALF if k else FULL) for k in range(blks)]
    adj, *pieces = call(
        gradient_kernel,
        "gradient",
        resids + [inv, adj, shapes, spread, low, target],
        [VMEM] * (blks + 6),
        [adj_shape] + pieces,
        scratch=[
            pltpu.VMEM((2 * round_up(rows // 2, 16), 3 * LANES), FULL),
            pltpu.VMEM((2 * 9 * 16, entries), HALF),
            pltpu.VMEM((-(-span // LANES), 9 * 16, LANES), FULL),
            pltpu.VMEM((tall, LANES), FULL),
        ],
    )
    count = lax.axis_size("blk")
    received = [
        lax.ppermute(pieces[k], "blk", [(i, i ^ k) for i in range(count)]) for k in far_first()
    ]
    third = jax.ShapeDtypeStruct((16, span), FULL)
    own, mate, far = call(combine_kernel, "combine", [pieces[0]] + received, [VMEM] * blks, [third] * 3)
    gradient = (own + to_mate(mate) + to_far(far))[:9]
    adjoint = jnp.transpose(adj.reshape(sides, elements, width), (1, 0, 2))
    return (adjoint, gradient)


def solution(mesh):
    in_specs = (
        P("dom", None, "blk"),
        P("dom", None, "blk"),
        P("dom", None, "blk", None),
        P("dom", "blk", None),
        P("dom", None),
        P("dom"),
        P("dom", "blk", None),
        P("dom", None),
    )
    out_specs = (P("dom", None, "blk"), P(None, ("dom", "blk")))
    return jax.shard_map(local, mesh=mesh, in_specs=in_specs, out_specs=out_specs, check_vma=False)
```

```python
import functools

import jax
import jax.numpy as jnp
from jax import lax
from jax.experimental import pallas as pl
from jax.experimental.pallas import tpu as pltpu
from jax.sharding import PartitionSpec as P

SWEEPS = 2
NODE_DEV = 768
HALF = jnp.bfloat16
FULL = jnp.float32
LANES = 128
PICK = 8
NT = (((1,), (1,)), ((), ()))
VMEM = pl.BlockSpec(memory_space=pltpu.VMEM)
SMEM = pl.BlockSpec(memory_space=pltpu.SMEM)
HBM = pl.BlockSpec(memory_space=pltpu.HBM)
GROUP = 30
MIB = 1024 * 1024


def round_up(size, unit):
    return -(-size // unit) * unit


def iota(shape, dim):
    return lax.broadcasted_iota(jnp.int32, shape, dim)


def hit(condition):
    return jnp.where(condition, 1.0, 0.0)


def in_hbm(array):
    return pltpu.with_memory_space_constraint(array, pltpu.HBM)


def call(kernel, name, args, specs, outs, scratch=(), limit=16, flops=0, moved=0, aliases=None):
    return pl.pallas_call(
        kernel,
        in_specs=specs,
        out_specs=[SMEM if getattr(out, "memory_space", None) is pltpu.SMEM else VMEM for out in outs],
        input_output_aliases=aliases or {},
        out_shape=outs,
        scratch_shapes=list(scratch),
        compiler_params=pltpu.CompilerParams(vmem_limit_bytes=limit * MIB),
        cost_estimate=pl.CostEstimate(flops=flops, bytes_accessed=moved, transcendentals=0),
        name=name,
    )(*args)


def distances():
    return list(range(1, lax.axis_size("blk")))


def over_blk(block, order):
    count = lax.axis_size("blk")
    return [lax.ppermute(block, "blk", [(i, i ^ k) for i in range(count)]) for k in order]


def to_mate(block):
    return lax.ppermute(block, "dom", [(i, i ^ 1) for i in range(lax.axis_size("dom"))])


def to_far(block):
    count = lax.axis_size("dom")
    return lax.ppermute(block, "dom", [(i, (((i + 1) ^ 1) - 1) % count) for i in range(count)])


def rounded(block, rows):
    short = rows - block.shape[0]
    if short:
        block = jnp.concatenate([block, jnp.zeros((short, block.shape[1]), block.dtype)], axis=0)
    return block.astype(HALF)


def window(ids, count):
    dom = lax.axis_index("dom")
    odd = lax.rem(dom, 2)
    place = ids - dom * count
    below = jnp.where(place < 0, 1, 0)
    above = jnp.where(place >= count, 1, 0)
    mate = odd * below + (1 - odd) * above
    return 2 * (below + above) - mate, place + (below - above) * count


def started(pairs, sems):
    copies = [pltpu.make_async_copy(source, target, sems.at[i]) for i, (source, target) in enumerate(pairs)]
    for copy in copies:
        copy.start()
    return copies


def slots_kernel(
    nb_hbm, shift_hbm, adj_hbm, rhs_hbm, _,
    pick_out, shift_out, list_out, count_out, adj_out, rhs_out, nb_ref, scalar_nb_ref, shift_ref, sems,
):
    pairs = [(nb_hbm, nb_ref), (shift_hbm, shift_ref), (adj_hbm, adj_out), (rhs_hbm, rhs_out)]
    copies = started(pairs + [(nb_hbm, scalar_nb_ref)], sems)
    copies[0].wait()
    copies[1].wait()
    copies[4].wait()
    list_far(scalar_nb_ref, list_out, count_out)
    faces, elements = nb_ref.shape
    rows_part = round_up(3 * elements, 16)
    part, inside = window(nb_ref[...], elements)
    bases = jnp.concatenate([iota((1, elements), 1), part * rows_part + inside], axis=0).astype(FULL)
    deep = elements * PICK
    shape = (deep, elements)
    behind = iota(shape, 0) - PICK * iota(shape, 1)
    owner = hit(jnp.logical_and(behind >= 0, behind < PICK)).astype(HALF)
    columns = lax.dot_general(owner, bases.astype(HALF), NT, preferred_element_type=FULL)
    shape = (elements, PICK, pick_out.shape[1])
    row, lane = iota(shape, 1).reshape(deep, -1), iota(shape, 2).reshape(deep, -1)
    offset = jnp.where(row < 3, lane - elements * row, -1).astype(FULL)
    for k in range(faces + 1):
        pick_out[k * deep : (k + 1) * deep, :] = hit(offset == columns[:, k : k + 1]).astype(HALF)
    shift_out[...] = jnp.zeros(shift_out.shape, FULL)
    for e in range(elements):
        shift_out[pl.ds(e, 3, stride=elements), :] = jnp.full((3, shift_out.shape[1]), shift_ref[e], FULL)
    for copy in (copies[2], copies[3]):
        copy.wait()


def list_far(nb_ref, list_out, count_out):
    faces, elements = nb_ref.shape

    count = jnp.int32(0)
    for e in range(elements):
        for k in range(1, faces + 1):
            part, inside = window(nb_ref[k - 1, e], elements)
            list_out[count] = (e * (faces + 1) + k) * 32 + inside
            count = count + lax.shift_right_logical(part, 1)
    for step in range(GROUP):
        list_out[count + step] = elements
    count_out[0] = lax.div(count + GROUP - 1, GROUP)


def nodes_kernel(ids_ref, shape_ref, low_out, target_out, shape_out):
    blk = lax.axis_index("blk")
    blks = lax.axis_size("blk")
    span = NODE_DEV // blks
    ids = ids_ref[...]
    pairs = ids.shape[0] // 2
    ids = [jnp.concatenate([ids[2 * p : 2 * p + 1], ids[2 * p + 1 : 2 * p + 2]], axis=1) for p in range(pairs)]
    part, inside = window(jnp.concatenate(ids, axis=0), NODE_DEV)
    owner = jnp.zeros_like(inside)
    for cut in range(1, blks):
        owner = owner + jnp.where(inside >= cut * span, 1, 0)
    low = inside - owner * span
    target_out[...] = part * blks + (owner ^ blk)
    shape = (span, LANES)
    for group in range(pairs):
        same = iota(shape, 0) == low[group : group + 1, :]
        low_out[:, group * LANES : (group + 1) * LANES] = hit(same).astype(HALF)

    elements, width, coords = shape_ref.shape
    shape = (coords, shape_out.shape[2])
    row, lane = iota(shape, 0), iota(shape, 1)
    axis = jnp.where(lane >= LANES, 1, 0) + jnp.where(lane >= 2 * LANES, 1, 0)
    side = lane - axis * LANES
    for odd in range(2):
        place = side - odd * (LANES // 2)
        inside = jnp.logical_and(place >= 0, place < LANES // 2)
        sort = hit(jnp.logical_and(inside, row == 3 * place + axis)).astype(HALF)
        for e in range(odd, elements, 2):
            shape_out[e] = jnp.dot(shape_ref[e], sort, preferred_element_type=FULL).astype(HALF)


def widened(block, lanes):
    short = lanes - block.shape[1]
    if short == 0:
        return block
    return jnp.concatenate([block, jnp.zeros((block.shape[0], short), block.dtype)], axis=1)


def put_columns(blocks, order, stride):
    blk = lax.axis_index("blk")
    width = blocks[0].shape[1]
    blocks = [widened(block.astype(FULL), LANES) for block in blocks]
    lane = iota(blocks[0].shape, 1)
    tiles = [0.0] * (stride // LANES)
    for owner in range(len(blocks)):
        found = blocks[0]
        for k, block in zip(order, blocks[1:]):
            found = jnp.where((blk ^ owner) == k, block, found)
        tile, offset = divmod(owner * width, LANES)
        if offset:
            found = pltpu.roll(found, offset, 1)
        if offset + width <= LANES:
            tiles[tile] = tiles[tile] + found
        else:
            tiles[tile] = tiles[tile] + jnp.where(lane >= offset, found, 0.0)
            tiles[tile + 1] = tiles[tile + 1] + jnp.where(lane < offset, found, 0.0)
    return jnp.concatenate(tiles, axis=1).astype(HALF)


def columns_kernel(order, *refs):
    *blocks, out_ref = refs
    rows, stride = out_ref.shape
    out_ref[...] = put_columns([rounded(ref[...], rows) for ref in blocks], order, stride)


def near_kernel(own_ref, mate_ref, pick_ref, shift_ref, adj_ref, rhs_ref, jac_ref, _, out_ref, image):
    products([own_ref[...], mate_ref[...]], pick_ref, jac_ref, image)
    out_ref[...] = without(shift_ref, adj_ref, rhs_ref, image)


def without(shift_ref, adj_ref, rhs_ref, image):
    rows, width = adj_ref.shape
    return rhs_ref[...] - (shift_ref[:rows, :width] * adj_ref[...] + image[:rows, :width])


def products(parts, pick_ref, jac_ref, image):
    elements, slots, width, _ = jac_ref.shape
    rows_part, stride = parts[0].shape
    short = pick_ref.shape[1] - len(parts) * rows_part
    if short:
        parts = parts + [jnp.zeros((short, stride), HALF)]
    stacked = jnp.concatenate(parts, axis=0)
    picked = jnp.dot(pick_ref[...], stacked, preferred_element_type=FULL).astype(HALF)
    image[...] = jnp.zeros(image.shape, FULL)
    for pair in range(elements // 2):
        starts = [k * elements * PICK + pair * 2 * PICK for k in range(slots)]
        left = jnp.concatenate([picked[start : start + 2 * PICK] for start in starts], axis=1)
        for side in range(2):
            e = 2 * pair + side
            blocks = jnp.concatenate([widened(jac_ref[e, k], stride) for k in range(slots)], axis=1)
            product = lax.dot_general(left, blocks, NT, preferred_element_type=FULL)
            first = side * PICK
            image[pl.ds(e, 3, stride=elements), :width] = product[first : first + 3]


def far_kernel(near_ref, far_ref, jac_ref, list_ref, count_ref, _shapes, _ids, out_ref, spread, sums, image):
    elements, slots, width, _ = jac_ref.shape
    rows, stride = far_ref.shape
    deep = spread.shape[1]
    shape = (elements, deep, rows)
    element, row, lane = [iota(shape, dim).reshape(elements * deep, rows) for dim in range(3)]
    pick = hit(jnp.where(row < 3, row * elements + element, -1) == lane).astype(HALF)
    taken = jnp.dot(pick, far_ref[...], preferred_element_type=FULL).astype(HALF)
    spread[:elements] = taken.reshape(elements, deep, stride)
    spread[elements:] = jnp.zeros((spread.shape[0] - elements, deep, stride), HALF)
    sums[...] = jnp.zeros(sums.shape, FULL)

    @pl.loop(0, count_ref[0])
    def _(step):
        for i in range(GROUP):
            word = list_ref[step * GROUP + i]
            block = lax.shift_right_logical(word, 5)
            place = lax.bitwise_and(word, 31)
            e = lax.div(block, slots)
            blocks = widened(jac_ref[e, block - e * slots], stride)
            product = lax.dot_general(spread[place], blocks, NT, preferred_element_type=FULL)
            sums[e, :, :width] += product[:PICK]

    for e in range(elements):
        image[pl.ds(e, 3, stride=elements), :] = sums[e, :3, :]
    real = near_ref.shape[0]
    out_ref[...] = rounded(near_ref[...] - image[:real, :width], out_ref.shape[0])


def element_of_row(shape, elements, copies=3):
    row = iota(shape, 0)
    for step in range(1, copies + 1):
        row = row - jnp.where(iota(shape, 0) >= step * elements, elements, 0)
    return row


def updated(resid_refs, inv_ref, adj_ref, update):
    rows, width = adj_ref.shape
    elements = rows // 3
    stride = round_up(inv_ref.shape[2], LANES)
    resid = put_columns([ref[...] for ref in resid_refs], distances(), stride)
    shape = (elements, PICK, resid.shape[0])
    deep = elements * PICK
    element, row, lane = [iota(shape, dim).reshape(deep, -1) for dim in range(3)]
    pick = hit(jnp.where(row < 3, row * elements + element, -1) == lane).astype(HALF)
    resid = jnp.dot(pick, resid, preferred_element_type=FULL).astype(HALF)
    update[...] = jnp.zeros(update.shape, FULL)
    for pair in range(elements // 2):
        left = resid[pair * 2 * PICK : (pair + 1) * 2 * PICK]
        for side in range(2):
            e = 2 * pair + side
            product = lax.dot_general(left, widened(inv_ref[e], stride), NT, preferred_element_type=FULL)
            first = side * PICK
            update[pl.ds(e, 3, stride=elements), :width] = product[first : first + 3]
    short = jnp.zeros((update.shape[0] - rows, width), FULL)
    return jnp.concatenate([adj_ref[...] + update[:rows, :width], short], axis=0)


def update_kernel(*refs):
    *resid_refs, inv_ref, adj_ref, adj_out, half_out, update = refs
    adj = updated(resid_refs, inv_ref, adj_ref, update)
    adj_out[...] = adj[: adj_out.shape[0]]
    half_out[...] = adj.astype(HALF)


def split(value):
    top = value.astype(HALF)
    return top, (value - top.astype(FULL)).astype(HALF)


def gradient_kernel(*refs):
    blks = lax.axis_size("blk")
    resid_refs = refs[:blks]
    inv_ref, adj_ref, shape_ref, low_ref, target_ref, adj_out = refs[blks : blks + 6]
    piece_outs = refs[blks + 6 : 2 * blks + 6]
    sorted_ref, left_ref, sums_ref, update = refs[2 * blks + 6 :]
    adj = updated(resid_refs, inv_ref, adj_ref, update)
    adj_out[...] = adj[: adj_out.shape[0]]
    half = adj.astype(HALF)
    elements = adj_out.shape[0] // 3
    pairs = elements // 2
    tall, width = half.shape
    coords = shape_ref.shape[2]
    depth = 3 if elements % 3 == 0 and 3 * width <= 256 else 1
    shape = (width, depth * width)
    row, lane = iota(shape, 0), iota(shape, 1)
    repeat = jnp.zeros(shape, FULL)
    for step in range(depth):
        repeat = repeat + hit(lane == row + step * width)
    left = jnp.dot(half, repeat.astype(HALF), preferred_element_type=FULL)
    shape = left.shape
    owner = element_of_row(shape, elements)
    group = jnp.zeros(shape, jnp.int32)
    for step in range(1, elements // depth):
        group = group + jnp.where(owner >= step * depth, 1, 0)
    first = (owner - group * depth) * width
    behind = iota(shape, 1) - first
    left = jnp.where(jnp.logical_and(behind >= 0, behind < width), left, 0.0).astype(HALF)
    shape = (tall, coords)
    owner = element_of_row(shape, elements)
    total = jnp.zeros(shape, FULL)
    for start in range(0, elements, depth):
        partials = jnp.concatenate([shape_ref[start + step] for step in range(depth)], axis=0)
        product = jnp.dot(left, partials, preferred_element_type=FULL)
        total = jnp.where(owner >= start, product, total)
    top, rest = split(total)
    sorted_ref[:tall] = top.astype(FULL)
    sorted_ref[tall:] = rest.astype(FULL)
    deep = 16
    for pair in range(pairs):
        lanes = slice(pair * LANES, (pair + 1) * LANES)
        mine = iota((deep, LANES), 0) == target_ref[pair : pair + 1, :]
        for part in range(2):
            for j in range(3):
                for c in range(3):
                    at = part * tall + j * elements + 2 * pair
                    lanes_of_axis = slice(c * LANES, (c + 1) * LANES)
                    values = sorted_ref[at : at + 1, lanes_of_axis] + sorted_ref[at + 1 : at + 2, lanes_of_axis]
                    start = (part * 9 + j * 3 + c) * deep
                    left_ref[start : start + deep, lanes] = jnp.where(mine, values, 0.0).astype(HALF)
    sums = lax.dot_general(left_ref[...], low_ref[...], NT, preferred_element_type=FULL)
    span = low_ref.shape[0]
    sums = -(sums[: 9 * deep] + sums[9 * deep :])
    tiles = [(tile, tile * LANES, min(span, (tile + 1) * LANES)) for tile in range(sums_ref.shape[0])]
    for tile, start, stop in tiles:
        sums_ref[tile, :, : stop - start] = sums[:, start:stop]
    for k, out_ref in enumerate(piece_outs):
        for tile, start, stop in tiles:
            found = [sums_ref[tile, pl.ds(part * blks + k, 9, stride=deep), :][:, : stop - start] for part in range(3)]
            found = jnp.concatenate(found + [jnp.zeros((5, stop - start), FULL)], axis=0)
            out_ref[:, start:stop] = found.astype(out_ref.dtype)


def combine_kernel(*refs):
    *piece_refs, own_out, mate_out, far_out = refs
    total = piece_refs[0][...]
    for ref in piece_refs[1:]:
        total = total + ref[...].astype(FULL)
    own_out[...] = total[:9]
    mate_out[...] = total[9:18]
    far_out[...] = total[18:27]


def local(
    adjoint_start,
    right_sides,
    jac_blocks,
    block_inverse,
    neighbours,
    pseudo_shift,
    shape_partials,
    node_ids,
):
    elements, sides, width = adjoint_start.shape
    slots, full = jac_blocks.shape[1], jac_blocks.shape[3]
    enodes = node_ids.shape[1]
    rows = sides * elements
    tall = round_up(rows, 16)
    stride = round_up(full, LANES)
    blks = lax.axis_size("blk")
    span = NODE_DEV // blks
    stacked = round_up(3 * tall, LANES)
    entries = elements * enodes

    adj_hbm = jnp.transpose(adjoint_start, (1, 0, 2)).reshape(rows, width)
    rhs = jnp.transpose(right_sides, (1, 0, 2)).reshape(rows, width)
    half_shape = jax.ShapeDtypeStruct((tall, width), HALF)

    adj_shape = jax.ShapeDtypeStruct((rows, width), FULL)
    pick, shift, far_list, far_count, adj, rhs = call(
        slots_kernel,
        "slots",
        [in_hbm(neighbours.T), in_hbm(pseudo_shift), in_hbm(adj_hbm), in_hbm(rhs), in_hbm(jac_blocks)],
        [HBM] * 5,
        [
            jax.ShapeDtypeStruct((slots * elements * PICK, stacked), HALF),
            jax.ShapeDtypeStruct((tall, LANES), FULL),
            pltpu.SMEM((round_up(elements * (slots - 1) + GROUP, LANES),), jnp.int32),
            pltpu.SMEM((1,), jnp.int32),
            pltpu.VMEM((rows, width), FULL),
            pltpu.VMEM((rows, width), FULL),
        ],
        scratch=[
            pltpu.VMEM((slots - 1, elements), jnp.int32),
            pltpu.SMEM((slots - 1, elements), jnp.int32),
            pltpu.SMEM((elements,), FULL),
            pltpu.SemaphoreType.DMA((6,)),
        ],
        moved=16 * MIB,
    )
    low, target, shapes = call(
        nodes_kernel,
        "nodes",
        [node_ids, shape_partials],
        [VMEM, VMEM],
        [
            jax.ShapeDtypeStruct((span, entries), HALF),
            jax.ShapeDtypeStruct((entries // LANES, LANES), jnp.int32),
            jax.ShapeDtypeStruct((elements, width, 3 * LANES), HALF),
        ],
        moved=3 * MIB,
    )

    for sweep in range(SWEEPS):
        order = distances()
        blocks = [half] + over_blk(half, order) if sweep else [adj] + over_blk(adj_hbm, order)
        wide = jax.ShapeDtypeStruct((tall, stride), HALF)
        (own,) = call(functools.partial(columns_kernel, order), "columns", blocks, [VMEM] * blks, [wide], moved=1 * MIB)
        far, mate = to_far(own), to_mate(own)
        image = pltpu.VMEM((tall, LANES), FULL)
        near_inputs = [own, mate, pick, shift, adj, rhs]
        far_scratch = [
            pltpu.VMEM((elements + 8, 16, stride), HALF),
            pltpu.VMEM((elements, PICK, LANES), FULL),
            image,
        ]
        (near,) = call(
            near_kernel,
            "near",
            near_inputs + [jac_blocks, in_hbm(block_inverse)],
            [VMEM] * 7 + [HBM],
            [adj_shape],
            [image],
            moved=12 * MIB,
        )
        (resid,) = call(
            far_kernel,
            "far",
            [near, far, jac_blocks, far_list, far_count, in_hbm(shape_partials), in_hbm(node_ids)],
            [VMEM] * 3 + [SMEM] * 2 + [HBM] * 2,
            [half_shape],
            far_scratch,
            moved=4 * MIB,
        )
        resids = [resid] + over_blk(resid, distances())
        if sweep < SWEEPS - 1:
            adj, half = call(
                update_kernel,
                "update",
                resids + [block_inverse, adj],
                [VMEM] * (blks + 2),
                [adj_shape, half_shape],
                scratch=[pltpu.VMEM((tall, LANES), FULL)],
                moved=8 * MIB,
            )
    pieces = [jax.ShapeDtypeStruct((32, span), HALF if k else FULL) for k in range(blks)]
    adj, *pieces = call(
        gradient_kernel,
        "gradient",
        resids + [block_inverse, adj, shapes, low, target],
        [VMEM] * (blks + 5),
        [adj_shape] + pieces,
        scratch=[
            pltpu.VMEM((2 * tall, 3 * LANES), FULL),
            pltpu.VMEM((2 * 9 * 16, entries), HALF),
            pltpu.VMEM((-(-span // LANES), 9 * 16, LANES), FULL),
            pltpu.VMEM((tall, LANES), FULL),
        ],
    )
    count = lax.axis_size("blk")
    received = [
        lax.ppermute(pieces[k], "blk", [(i, i ^ k) for i in range(count)]) for k in reversed(distances())
    ]
    third = jax.ShapeDtypeStruct((9, span), FULL)
    own, mate, far = call(combine_kernel, "combine", [pieces[0]] + received, [VMEM] * blks, [third] * 3)
    gradient = own + to_mate(mate) + to_far(far)
    adjoint = jnp.transpose(adj.reshape(sides, elements, width), (1, 0, 2))
    return (adjoint, gradient)


def solution(mesh):
    in_specs = (
        P("dom", None, "blk"),
        P("dom", None, "blk"),
        P("dom", None, "blk", None),
        P("dom", "blk", None),
        P("dom", None),
        P("dom"),
        P("dom", "blk", None),
        P("dom", None),
    )
    out_specs = (P("dom", None, "blk"), P(None, ("dom", "blk")))
    return jax.shard_map(local, mesh=mesh, in_specs=in_specs, out_specs=out_specs, check_vma=False)
```

```python
import functools

import jax
import jax.numpy as jnp
from jax import lax
from jax.experimental import pallas as pl
from jax.experimental.pallas import tpu as pltpu
from jax.sharding import PartitionSpec as P

SWEEPS = 2
NODE_DEV = 768
HALF = jnp.bfloat16
FULL = jnp.float32
LANES = 128
PICK = 8
NT = (((1,), (1,)), ((), ()))
VMEM = pl.BlockSpec(memory_space=pltpu.VMEM)
SMEM = pl.BlockSpec(memory_space=pltpu.SMEM)
HBM = pl.BlockSpec(memory_space=pltpu.HBM)
GROUP = 60
MIB = 1024 * 1024


def round_up(size, unit):
    return -(-size // unit) * unit


def iota(shape, dim):
    return lax.broadcasted_iota(jnp.int32, shape, dim)


def hit(condition):
    return jnp.where(condition, 1.0, 0.0)


def in_hbm(array):
    return pltpu.with_memory_space_constraint(array, pltpu.HBM)


def call(kernel, name, args, specs, outs, scratch=(), limit=16, flops=0, moved=0, aliases=None):
    return pl.pallas_call(
        kernel,
        in_specs=specs,
        out_specs=[SMEM if getattr(out, "memory_space", None) is pltpu.SMEM else VMEM for out in outs],
        input_output_aliases=aliases or {},
        out_shape=outs,
        scratch_shapes=list(scratch),
        compiler_params=pltpu.CompilerParams(vmem_limit_bytes=limit * MIB),
        cost_estimate=pl.CostEstimate(flops=flops, bytes_accessed=moved, transcendentals=0),
        name=name,
    )(*args)


def distances():
    return list(range(1, lax.axis_size("blk")))


def over_blk(block, order):
    count = lax.axis_size("blk")
    return [lax.ppermute(block, "blk", [(i, i ^ k) for i in range(count)]) for k in order]


def to_mate(block):
    return lax.ppermute(block, "dom", [(i, i ^ 1) for i in range(lax.axis_size("dom"))])


def to_far(block):
    count = lax.axis_size("dom")
    return lax.ppermute(block, "dom", [(i, (((i + 1) ^ 1) - 1) % count) for i in range(count)])


def rounded(block, rows):
    short = rows - block.shape[0]
    if short:
        block = jnp.concatenate([block, jnp.zeros((short, block.shape[1]), block.dtype)], axis=0)
    return block.astype(HALF)


def window(ids, count):
    dom = lax.axis_index("dom")
    odd = lax.rem(dom, 2)
    place = ids - dom * count
    below = jnp.where(place < 0, 1, 0)
    above = jnp.where(place >= count, 1, 0)
    mate = odd * below + (1 - odd) * above
    return 2 * (below + above) - mate, place + (below - above) * count


def started(pairs, sems):
    copies = [pltpu.make_async_copy(source, target, sems.at[i]) for i, (source, target) in enumerate(pairs)]
    for copy in copies:
        copy.start()
    return copies


def slots_kernel(
    nb_hbm, shift_hbm, adj_hbm, rhs_hbm, _,
    pick_out, shift_out, list_out, count_out, adj_out, rhs_out, nb_ref, scalar_nb_ref, shift_ref, sems,
):
    pairs = [(nb_hbm, nb_ref), (shift_hbm, shift_ref), (adj_hbm, adj_out), (rhs_hbm, rhs_out)]
    copies = started(pairs + [(nb_hbm, scalar_nb_ref)], sems)
    copies[0].wait()
    copies[1].wait()
    copies[4].wait()
    list_far(scalar_nb_ref, list_out, count_out)
    faces, elements = nb_ref.shape
    rows_part = round_up(3 * elements, 16)
    part, inside = window(nb_ref[...], elements)
    bases = jnp.concatenate([iota((1, elements), 1), part * rows_part + inside], axis=0).astype(FULL)
    deep = elements * PICK
    shape = (deep, elements)
    behind = iota(shape, 0) - PICK * iota(shape, 1)
    owner = hit(jnp.logical_and(behind >= 0, behind < PICK)).astype(HALF)
    columns = lax.dot_general(owner, bases.astype(HALF), NT, preferred_element_type=FULL)
    shape = (elements, PICK, pick_out.shape[1])
    row, lane = iota(shape, 1).reshape(deep, -1), iota(shape, 2).reshape(deep, -1)
    offset = jnp.where(row < 3, lane - elements * row, -1).astype(FULL)
    for k in range(faces + 1):
        pick_out[k * deep : (k + 1) * deep, :] = hit(offset == columns[:, k : k + 1]).astype(HALF)
    shift_out[...] = jnp.zeros(shift_out.shape, FULL)
    for e in range(elements):
        shift_out[pl.ds(e, 3, stride=elements), :] = jnp.full((3, shift_out.shape[1]), shift_ref[e], FULL)
    for copy in (copies[2], copies[3]):
        copy.wait()


def list_far(nb_ref, list_out, count_out):
    faces, elements = nb_ref.shape

    count = jnp.int32(0)
    for e in range(elements):
        for k in range(1, faces + 1):
            part, inside = window(nb_ref[k - 1, e], elements)
            list_out[count] = (e * (faces + 1) + k) * 32 + inside
            count = count + lax.shift_right_logical(part, 1)
    for step in range(GROUP):
        list_out[count + step] = elements
    count_out[0] = lax.div(count + GROUP - 1, GROUP)


def nodes_kernel(ids_ref, shape_ref, low_out, target_out, shape_out):
    blk = lax.axis_index("blk")
    blks = lax.axis_size("blk")
    span = NODE_DEV // blks
    ids = ids_ref[...]
    pairs = ids.shape[0] // 2
    ids = [jnp.concatenate([ids[2 * p : 2 * p + 1], ids[2 * p + 1 : 2 * p + 2]], axis=1) for p in range(pairs)]
    part, inside = window(jnp.concatenate(ids, axis=0), NODE_DEV)
    owner = jnp.zeros_like(inside)
    for cut in range(1, blks):
        owner = owner + jnp.where(inside >= cut * span, 1, 0)
    low = inside - owner * span
    target_out[...] = part * blks + (owner ^ blk)
    shape = (span, LANES)
    for group in range(pairs):
        same = iota(shape, 0) == low[group : group + 1, :]
        low_out[:, group * LANES : (group + 1) * LANES] = hit(same).astype(HALF)

    elements, _, coords = shape_ref.shape
    nodes = coords // 3
    row, lane = iota((coords, coords), 0), iota((coords, coords), 1)
    axis = jnp.where(lane >= nodes, 1, 0) + jnp.where(lane >= 2 * nodes, 1, 0)
    sort = hit(row == 3 * (lane - axis * nodes) + axis).astype(HALF)
    for e in range(elements):
        shape_out[e] = jnp.dot(shape_ref[e], sort, preferred_element_type=FULL).astype(HALF)


def widened(block, lanes):
    short = lanes - block.shape[1]
    if short == 0:
        return block
    return jnp.concatenate([block, jnp.zeros((block.shape[0], short), block.dtype)], axis=1)


def laid(blocks, width, stride):
    lane = iota(blocks[0].shape, 1)
    tiles = [0.0] * (stride // LANES)
    for place, block in enumerate(blocks):
        tile, offset = divmod(place * width, LANES)
        if offset:
            block = pltpu.roll(block, offset, 1)
        if offset + width <= LANES:
            tiles[tile] = tiles[tile] + block
        else:
            tiles[tile] = tiles[tile] + jnp.where(lane >= offset, block, 0.0)
            tiles[tile + 1] = tiles[tile + 1] + jnp.where(lane < offset, block, 0.0)
    return tiles


def put_columns(blocks, order, stride):
    blk = lax.axis_index("blk")
    width = blocks[0].shape[1]
    blocks = [widened(block.astype(FULL), LANES) for block in blocks]
    placed = []
    for owner in range(len(blocks)):
        found = blocks[0]
        for k, block in zip(order, blocks[1:]):
            found = jnp.where((blk ^ owner) == k, block, found)
        placed.append(found)
    return laid(placed, width, stride)


def cut_of(rows, full):
    tail = full % LANES
    if tail == 0:
        return 0
    return round_up(rows // 2, 8) if tail <= LANES // 2 else rows


def packed_rows(rows, full):
    return round_up(full // LANES * rows + cut_of(rows, full), 16)


def columns_kernel(order, rows, full, *refs):
    *blocks, out_ref = refs
    tiles = put_columns([ref[...] for ref in blocks], order, round_up(full, LANES))
    cut = cut_of(rows, full)
    parts = [tile[:rows] for tile in tiles[: full // LANES]]
    if cut:
        last = tiles[-1][:cut]
        if cut < rows:
            lower = pltpu.roll(tiles[-1][cut:rows], LANES // 2, 1)
            last = last + jnp.concatenate([lower, jnp.zeros((2 * cut - rows, LANES), FULL)], axis=0)
        parts.append(last)
    out_ref[...] = rounded(jnp.concatenate(parts, axis=0), out_ref.shape[0])


def unpacked(ref, rows, full):
    block = ref[...].astype(FULL)
    whole, cut = full // LANES, cut_of(rows, full)
    tiles = [block[i * rows : (i + 1) * rows] for i in range(whole)]
    if cut:
        last = block[whole * rows : whole * rows + cut]
        if cut < rows:
            low = iota(last.shape, 1) < LANES // 2
            lower = pltpu.roll(jnp.where(low, 0.0, last), LANES // 2, 1)
            last = jnp.concatenate([jnp.where(low, last, 0.0), lower[: rows - cut]], axis=0)
        tiles.append(last)
    return rounded(jnp.concatenate(tiles, axis=1), round_up(rows, 16))


def near_kernel(own_ref, mate_ref, pick_ref, shift_ref, adj_ref, rhs_ref, jac_ref, _, out_ref, image):
    rows, full = adj_ref.shape[0], jac_ref.shape[3]
    products([unpacked(own_ref, rows, full), unpacked(mate_ref, rows, full)], pick_ref, jac_ref, image)
    out_ref[...] = without(shift_ref, adj_ref, rhs_ref, image)


def without(shift_ref, adj_ref, rhs_ref, image):
    rows, width = adj_ref.shape
    return rhs_ref[...] - (shift_ref[:rows, :width] * adj_ref[...] + image[:rows, :width])


def products(parts, pick_ref, jac_ref, image):
    elements, slots, width, _ = jac_ref.shape
    rows_part, stride = parts[0].shape
    short = pick_ref.shape[1] - len(parts) * rows_part
    if short:
        parts = parts + [jnp.zeros((short, stride), HALF)]
    stacked = jnp.concatenate(parts, axis=0)
    picked = jnp.dot(pick_ref[...], stacked, preferred_element_type=FULL).astype(HALF)
    image[...] = jnp.zeros(image.shape, FULL)
    for pair in range(elements // 2):
        starts = [k * elements * PICK + pair * 2 * PICK for k in range(slots)]
        left = jnp.concatenate([picked[start : start + 2 * PICK] for start in starts], axis=1)
        for side in range(2):
            e = 2 * pair + side
            blocks = jnp.concatenate([widened(jac_ref[e, k], stride) for k in range(slots)], axis=1)
            product = lax.dot_general(left, blocks, NT, preferred_element_type=FULL)
            first = side * PICK
            image[pl.ds(e, 3, stride=elements), :width] = product[first : first + 3]


def pair_products(lefts, blocks):
    full = blocks[0].shape[1]
    deep = full // (2 * LANES) * (2 * LANES)
    lower = iota((2 * PICK, LANES), 0) >= PICK
    mine = [jnp.logical_not(lower), lower]
    rest = [jnp.where(mine[i], lefts[i][:, deep : deep + LANES], 0.0).astype(HALF) for i in range(2)]
    blocks_rest = [widened(block[:, deep:], LANES) for block in blocks]
    shared = lax.dot_general(
        jnp.concatenate(rest, axis=1), jnp.concatenate(blocks_rest, axis=1), NT, preferred_element_type=FULL
    )
    products = []
    for i, (left, block) in enumerate(zip(lefts, blocks)):
        product = lax.dot_general(left[:, :deep], block[:, :deep], NT, preferred_element_type=FULL)
        half = slice(i * PICK, (i + 1) * PICK)
        products.append(product[half] + shared[half])
    return products


def far_kernel(near_ref, far_ref, jac_ref, list_ref, count_ref, _shapes, _ids, out_ref, spread, sums, image):
    elements, slots, width, _ = jac_ref.shape
    far = unpacked(far_ref, near_ref.shape[0], jac_ref.shape[3])
    rows, stride = far.shape
    deep = spread.shape[1]
    shape = (elements, deep, rows)
    element, row, lane = [iota(shape, dim).reshape(elements * deep, rows) for dim in range(3)]
    row = row - jnp.where(row >= PICK, PICK, 0)
    pick = hit(jnp.where(row < 3, row * elements + element, -1) == lane).astype(HALF)
    taken = jnp.dot(pick, far, preferred_element_type=FULL).astype(HALF)
    spread[:elements] = taken.reshape(elements, deep, stride)
    spread[elements:] = jnp.zeros((spread.shape[0] - elements, deep, stride), HALF)
    sums[...] = jnp.zeros(sums.shape, FULL)

    @pl.loop(0, count_ref[0])
    def _(step):
        for i in range(0, GROUP, 2):
            owners, lefts, blocks = [], [], []
            for side in range(2):
                word = list_ref[step * GROUP + i + side]
                block = lax.shift_right_logical(word, 5)
                owners.append(lax.div(block, slots))
                lefts.append(spread[lax.bitwise_and(word, 31)])
                blocks.append(jac_ref[owners[side], block - owners[side] * slots])
            for e, product in zip(owners, pair_products(lefts, blocks)):
                sums[e, :, :width] += product

    for e in range(elements):
        image[pl.ds(e, 3, stride=elements), :] = sums[e, :3, :]
    real = near_ref.shape[0]
    out_ref[...] = rounded(near_ref[...] - image[:real, :width], out_ref.shape[0])


def element_of_row(shape, elements, copies=3):
    row = iota(shape, 0)
    for step in range(1, copies + 1):
        row = row - jnp.where(iota(shape, 0) >= step * elements, elements, 0)
    return row


def updated(resid_refs, inv_ref, adj_ref, update):
    rows, width = adj_ref.shape
    elements = rows // 3
    stride = round_up(inv_ref.shape[2], LANES)
    resid = put_columns([ref[...] for ref in resid_refs], distances(), stride)
    resid = jnp.concatenate(resid, axis=1).astype(HALF)
    shape = (elements, PICK, resid.shape[0])
    deep = elements * PICK
    element, row, lane = [iota(shape, dim).reshape(deep, -1) for dim in range(3)]
    pick = hit(jnp.where(row < 3, row * elements + element, -1) == lane).astype(HALF)
    resid = jnp.dot(pick, resid, preferred_element_type=FULL).astype(HALF)
    update[...] = jnp.zeros(update.shape, FULL)
    for pair in range(elements // 2):
        left = resid[pair * 2 * PICK : (pair + 1) * 2 * PICK]
        for side, product in enumerate(pair_products([left, left], [inv_ref[2 * pair], inv_ref[2 * pair + 1]])):
            update[pl.ds(2 * pair + side, 3, stride=elements), :width] = product[:3]
    short = jnp.zeros((update.shape[0] - rows, width), FULL)
    return jnp.concatenate([adj_ref[...] + update[:rows, :width], short], axis=0)


def update_kernel(*refs):
    *resid_refs, inv_ref, adj_ref, adj_out, half_out, update = refs
    adj = updated(resid_refs, inv_ref, adj_ref, update)
    adj_out[...] = adj[: adj_out.shape[0]]
    half_out[...] = adj.astype(HALF)


def split(value):
    top = value.astype(HALF)
    return top, (value - top.astype(FULL)).astype(HALF)


def gradient_kernel(*refs):
    blks = lax.axis_size("blk")
    resid_refs = refs[:blks]
    inv_ref, adj_ref, shape_ref, low_ref, target_ref, adj_out = refs[blks : blks + 6]
    part_outs = refs[blks + 6 : blks + 9]
    sorted_ref, left_ref, sums_ref, update = refs[blks + 9 :]
    adj = updated(resid_refs, inv_ref, adj_ref, update)
    adj_out[...] = adj[: adj_out.shape[0]]
    half = adj.astype(HALF)
    elements = adj_out.shape[0] // 3
    pairs = elements // 2
    tall, width = half.shape
    coords = shape_ref.shape[2]
    depth = 3 if elements % 3 == 0 and 3 * width <= 256 else 1
    block = widened(half.astype(FULL), LANES)
    left = jnp.concatenate(laid([block] * depth, width, round_up(depth * width, LANES)), axis=1)[:, : depth * width]
    shape = left.shape
    owner = element_of_row(shape, elements)
    group = jnp.zeros(shape, jnp.int32)
    for step in range(1, elements // depth):
        group = group + jnp.where(owner >= step * depth, 1, 0)
    first = (owner - group * depth) * width
    behind = iota(shape, 1) - first
    left = jnp.where(jnp.logical_and(behind >= 0, behind < width), left, 0.0).astype(HALF)
    shape = (tall, coords)
    owner = element_of_row(shape, elements)
    total = jnp.zeros(shape, FULL)
    for start in range(0, elements, depth):
        partials = jnp.concatenate([shape_ref[start + step] for step in range(depth)], axis=0)
        product = jnp.dot(left, partials, preferred_element_type=FULL)
        total = jnp.where(owner >= start, product, total)
    low = iota((tall, LANES), 1) < LANES // 2
    odd = lax.bitwise_and(owner[:, :LANES], 1) == 1
    values = [total[:, :LANES], widened(total[:, LANES:], LANES)]
    turned = [pltpu.roll(value, LANES // 2, 1) for value in values]
    value = [
        jnp.where(odd, jnp.where(low, 0.0, turned[0]), jnp.where(low, values[0], 0.0)),
        jnp.where(odd, jnp.where(low, 0.0, values[0]), jnp.where(low, turned[0], 0.0)),
        jnp.where(odd, turned[1], values[1]),
    ]
    top, rest = split(jnp.concatenate(value, axis=1))
    sorted_ref[:tall] = top.astype(FULL)
    sorted_ref[tall:] = rest.astype(FULL)
    deep = 16
    for pair in range(pairs):
        lanes = slice(pair * LANES, (pair + 1) * LANES)
        mine = iota((deep, LANES), 0) == target_ref[pair : pair + 1, :]
        for part in range(2):
            for j in range(3):
                for c in range(3):
                    at = part * tall + j * elements + 2 * pair
                    lanes_of_axis = slice(c * LANES, (c + 1) * LANES)
                    values = sorted_ref[at : at + 1, lanes_of_axis] + sorted_ref[at + 1 : at + 2, lanes_of_axis]
                    start = (part * 9 + j * 3 + c) * deep
                    left_ref[start : start + deep, lanes] = jnp.where(mine, values, 0.0).astype(HALF)
    sums = lax.dot_general(left_ref[...], low_ref[...], NT, preferred_element_type=FULL)
    span = low_ref.shape[0]
    sums = -(sums[: 9 * deep] + sums[9 * deep :])
    tiles = [(tile, tile * LANES, min(span, (tile + 1) * LANES)) for tile in range(sums_ref.shape[0])]
    for tile, start, stop in tiles:
        sums_ref[tile, :, : stop - start] = sums[:, start:stop]
    for part, out_ref in enumerate(part_outs):
        for tile, start, stop in tiles:
            found = [sums_ref[tile, pl.ds(part * blks + k, 9, stride=deep), :][:, : stop - start] for k in range(blks)]
            found = jnp.concatenate(found + [jnp.zeros((out_ref.shape[0] - 9 * blks, stop - start), FULL)], axis=0)
            out_ref[:, start:stop] = found.astype(out_ref.dtype)


def combine_kernel(own_ref, mate_ref, far_ref, *piece_outs):
    total = own_ref[...] + mate_ref[...].astype(FULL) + far_ref[...].astype(FULL)
    for k, out_ref in enumerate(piece_outs):
        piece = total[9 * k : 9 * (k + 1)]
        out_ref[...] = rounded(piece, 16) if k else piece


def local(
    adjoint_start,
    right_sides,
    jac_blocks,
    block_inverse,
    neighbours,
    pseudo_shift,
    shape_partials,
    node_ids,
):
    elements, sides, width = adjoint_start.shape
    slots, full = jac_blocks.shape[1], jac_blocks.shape[3]
    enodes = node_ids.shape[1]
    rows = sides * elements
    tall = round_up(rows, 16)
    stride = round_up(full, LANES)
    blks = lax.axis_size("blk")
    span = NODE_DEV // blks
    stacked = round_up(3 * tall, LANES)
    entries = elements * enodes

    adj_hbm = jnp.transpose(adjoint_start, (1, 0, 2)).reshape(rows, width)
    rhs = jnp.transpose(right_sides, (1, 0, 2)).reshape(rows, width)
    half_shape = jax.ShapeDtypeStruct((tall, width), HALF)

    adj_shape = jax.ShapeDtypeStruct((rows, width), FULL)
    pick, shift, far_list, far_count, adj, rhs = call(
        slots_kernel,
        "slots",
        [in_hbm(neighbours.T), in_hbm(pseudo_shift), in_hbm(adj_hbm), in_hbm(rhs), in_hbm(jac_blocks)],
        [HBM] * 5,
        [
            jax.ShapeDtypeStruct((slots * elements * PICK, stacked), HALF),
            jax.ShapeDtypeStruct((tall, LANES), FULL),
            pltpu.SMEM((round_up(elements * (slots - 1) + GROUP, LANES),), jnp.int32),
            pltpu.SMEM((1,), jnp.int32),
            pltpu.VMEM((rows, width), FULL),
            pltpu.VMEM((rows, width), FULL),
        ],
        scratch=[
            pltpu.VMEM((slots - 1, elements), jnp.int32),
            pltpu.SMEM((slots - 1, elements), jnp.int32),
            pltpu.SMEM((elements,), FULL),
            pltpu.SemaphoreType.DMA((6,)),
        ],
        moved=16 * MIB,
    )
    low, target, shapes = call(
        nodes_kernel,
        "nodes",
        [node_ids, shape_partials],
        [VMEM, VMEM],
        [
            jax.ShapeDtypeStruct((span, entries), HALF),
            jax.ShapeDtypeStruct((entries // LANES, LANES), jnp.int32),
            jax.ShapeDtypeStruct(shape_partials.shape, HALF),
        ],
        moved=3 * MIB,
    )

    for sweep in range(SWEEPS):
        order = distances()
        blocks = [half] + over_blk(half, order) if sweep else [adj] + over_blk(adj_hbm, order)
        wide = jax.ShapeDtypeStruct((packed_rows(rows, full), LANES), HALF)
        (own,) = call(functools.partial(columns_kernel, order, rows, full), "columns", blocks, [VMEM] * blks, [wide], moved=1 * MIB)
        far, mate = to_far(own), to_mate(own)
        image = pltpu.VMEM((tall, LANES), FULL)
        near_inputs = [own, mate, pick, shift, adj, rhs]
        far_scratch = [
            pltpu.VMEM((elements + 8, 16, stride), HALF),
            pltpu.VMEM((elements, PICK, LANES), FULL),
            image,
        ]
        (near,) = call(
            near_kernel,
            "near",
            near_inputs + [jac_blocks, in_hbm(block_inverse)],
            [VMEM] * 7 + [HBM],
            [adj_shape],
            [image],
            moved=12 * MIB,
        )
        (resid,) = call(
            far_kernel,
            "far",
            [near, far, jac_blocks, far_list, far_count, in_hbm(shape_partials), in_hbm(node_ids)],
            [VMEM] * 3 + [SMEM] * 2 + [HBM] * 2,
            [half_shape],
            far_scratch,
            moved=4 * MIB,
        )
        resids = [resid] + over_blk(resid, distances())
        if sweep < SWEEPS - 1:
            adj, half = call(
                update_kernel,
                "update",
                resids + [block_inverse, adj],
                [VMEM] * (blks + 2),
                [adj_shape, half_shape],
                scratch=[pltpu.VMEM((tall, LANES), FULL)],
                moved=8 * MIB,
            )
    deep = round_up(9 * blks, 16)
    adj, own, mate, far = call(
        gradient_kernel,
        "gradient",
        resids + [block_inverse, adj, shapes, low, target],
        [VMEM] * (blks + 5),
        [adj_shape] + [jax.ShapeDtypeStruct((deep, span), kind) for kind in (FULL, HALF, HALF)],
        scratch=[
            pltpu.VMEM((2 * tall, 3 * LANES), FULL),
            pltpu.VMEM((2 * 9 * 16, entries), HALF),
            pltpu.VMEM((-(-span // LANES), 9 * 16, LANES), FULL),
            pltpu.VMEM((tall, LANES), FULL),
        ],
    )
    far, mate = to_far(far), to_mate(mate)
    shapes = [jax.ShapeDtypeStruct((16, span), HALF)] * (blks - 1)
    pieces = call(
        combine_kernel, "combine", [own, mate, far], [VMEM] * 3, [jax.ShapeDtypeStruct((9, span), FULL)] + shapes
    )
    gradient = pieces[0]
    count = lax.axis_size("blk")
    for k in reversed(distances()):
        gradient = gradient + lax.ppermute(pieces[k], "blk", [(i, i ^ k) for i in range(count)])[:9].astype(FULL)
    adjoint = jnp.transpose(adj.reshape(sides, elements, width), (1, 0, 2))
    return (adjoint, gradient)


def solution(mesh):
    in_specs = (
        P("dom", None, "blk"),
        P("dom", None, "blk"),
        P("dom", None, "blk", None),
        P("dom", "blk", None),
        P("dom", None),
        P("dom"),
        P("dom", "blk", None),
        P("dom", None),
    )
    out_specs = (P("dom", None, "blk"), P(None, ("dom", "blk")))
    return jax.shard_map(local, mesh=mesh, in_specs=in_specs, out_specs=out_specs, check_vma=False)
```

```python
import functools

import jax
import jax.numpy as jnp
from jax import lax
from jax.experimental import pallas as pl
from jax.experimental.pallas import tpu as pltpu
from jax.sharding import PartitionSpec as P

SWEEPS = 2
NODE_DEV = 768
HALF = jnp.bfloat16
FULL = jnp.float32
LANES = 128
PICK = 8
QUAD = 4
NT = (((1,), (1,)), ((), ()))
VMEM = pl.BlockSpec(memory_space=pltpu.VMEM)
SMEM = pl.BlockSpec(memory_space=pltpu.SMEM)
HBM = pl.BlockSpec(memory_space=pltpu.HBM)
GROUP = 60
MIB = 1024 * 1024


def round_up(size, unit):
    return -(-size // unit) * unit


def iota(shape, dim):
    return lax.broadcasted_iota(jnp.int32, shape, dim)


def hit(condition):
    return jnp.where(condition, 1.0, 0.0)


def in_hbm(array):
    return pltpu.with_memory_space_constraint(array, pltpu.HBM)


def call(kernel, name, args, specs, outs, scratch=(), limit=16, flops=0, moved=0, aliases=None):
    return pl.pallas_call(
        kernel,
        in_specs=specs,
        out_specs=[SMEM if getattr(out, "memory_space", None) is pltpu.SMEM else VMEM for out in outs],
        input_output_aliases=aliases or {},
        out_shape=outs,
        scratch_shapes=list(scratch),
        compiler_params=pltpu.CompilerParams(vmem_limit_bytes=limit * MIB),
        cost_estimate=pl.CostEstimate(flops=flops, bytes_accessed=moved, transcendentals=0),
        name=name,
    )(*args)


def distances():
    return list(range(1, lax.axis_size("blk")))


def over_blk(block, order):
    count = lax.axis_size("blk")
    return [lax.ppermute(block, "blk", [(i, i ^ k) for i in range(count)]) for k in order]


def to_mate(block):
    return lax.ppermute(block, "dom", [(i, i ^ 1) for i in range(lax.axis_size("dom"))])


def to_far(block):
    count = lax.axis_size("dom")
    return lax.ppermute(block, "dom", [(i, (((i + 1) ^ 1) - 1) % count) for i in range(count)])


def rounded(block, rows):
    short = rows - block.shape[0]
    if short:
        block = jnp.concatenate([block, jnp.zeros((short, block.shape[1]), block.dtype)], axis=0)
    return block.astype(HALF)


def window(ids, count):
    dom = lax.axis_index("dom")
    odd = lax.rem(dom, 2)
    place = ids - dom * count
    below = jnp.where(place < 0, 1, 0)
    above = jnp.where(place >= count, 1, 0)
    mate = odd * below + (1 - odd) * above
    return 2 * (below + above) - mate, place + (below - above) * count


def started(pairs, sems):
    copies = [pltpu.make_async_copy(source, target, sems.at[i]) for i, (source, target) in enumerate(pairs)]
    for copy in copies:
        copy.start()
    return copies


def slots_kernel(
    nb_hbm, shift_hbm, adj_hbm, rhs_hbm, _,
    pick_out, shift_out, list_out, count_out, adj_out, rhs_out, nb_ref, scalar_nb_ref, shift_ref, sems,
):
    pairs = [(nb_hbm, nb_ref), (shift_hbm, shift_ref), (adj_hbm, adj_out), (rhs_hbm, rhs_out)]
    copies = started(pairs + [(nb_hbm, scalar_nb_ref)], sems)
    copies[0].wait()
    copies[1].wait()
    copies[4].wait()
    list_far(scalar_nb_ref, list_out, count_out)
    faces, elements = nb_ref.shape
    rows_part = round_up(3 * elements, 16)
    part, inside = window(nb_ref[...], elements)
    bases = jnp.concatenate([iota((1, elements), 1), part * rows_part + inside], axis=0).astype(FULL)
    deep = elements * PICK
    shape = (deep, elements)
    behind = iota(shape, 0) - PICK * iota(shape, 1)
    owner = hit(jnp.logical_and(behind >= 0, behind < PICK)).astype(HALF)
    columns = lax.dot_general(owner, bases.astype(HALF), NT, preferred_element_type=FULL)
    shape = (elements, PICK, pick_out.shape[1])
    row, lane = iota(shape, 1).reshape(deep, -1), iota(shape, 2).reshape(deep, -1)
    offset = jnp.where(row < 3, lane - elements * row, -1).astype(FULL)
    for k in range(faces + 1):
        pick_out[k * deep : (k + 1) * deep, :] = hit(offset == columns[:, k : k + 1]).astype(HALF)
    shift_out[...] = jnp.zeros(shift_out.shape, FULL)
    for e in range(elements):
        shift_out[pl.ds(e, 3, stride=elements), :] = jnp.full((3, shift_out.shape[1]), shift_ref[e], FULL)
    for copy in (copies[2], copies[3]):
        copy.wait()


def list_far(nb_ref, list_out, count_out):
    faces, elements = nb_ref.shape

    count = jnp.int32(0)
    for e in range(elements):
        for k in range(1, faces + 1):
            part, inside = window(nb_ref[k - 1, e], elements)
            list_out[count] = (e * (faces + 1) + k) * 32 + inside
            count = count + lax.shift_right_logical(part, 1)
    for step in range(GROUP):
        list_out[count + step] = elements
    count_out[0] = lax.div(count + GROUP - 1, GROUP)


def nodes_kernel(ids_ref, shape_ref, low_out, target_out, shape_out):
    blk = lax.axis_index("blk")
    blks = lax.axis_size("blk")
    span = NODE_DEV // blks
    ids = ids_ref[...]
    pairs = ids.shape[0] // 2
    ids = [jnp.concatenate([ids[2 * p : 2 * p + 1], ids[2 * p + 1 : 2 * p + 2]], axis=1) for p in range(pairs)]
    part, inside = window(jnp.concatenate(ids, axis=0), NODE_DEV)
    owner = jnp.zeros_like(inside)
    for cut in range(1, blks):
        owner = owner + jnp.where(inside >= cut * span, 1, 0)
    low = inside - owner * span
    target_out[...] = part * blks + (owner ^ blk)
    shape = (span, LANES)
    for group in range(pairs):
        same = iota(shape, 0) == low[group : group + 1, :]
        low_out[:, group * LANES : (group + 1) * LANES] = hit(same).astype(HALF)

    elements, _, coords = shape_ref.shape
    nodes = coords // 3
    row, lane = iota((coords, coords), 0), iota((coords, coords), 1)
    axis = jnp.where(lane >= nodes, 1, 0) + jnp.where(lane >= 2 * nodes, 1, 0)
    sort = hit(row == 3 * (lane - axis * nodes) + axis).astype(HALF)
    for e in range(elements):
        shape_out[e] = jnp.dot(shape_ref[e], sort, preferred_element_type=FULL).astype(HALF)


def widened(block, lanes):
    short = lanes - block.shape[1]
    if short == 0:
        return block
    return jnp.concatenate([block, jnp.zeros((block.shape[0], short), block.dtype)], axis=1)


def laid(blocks, width, stride):
    lane = iota(blocks[0].shape, 1)
    tiles = [0.0] * (stride // LANES)
    for place, block in enumerate(blocks):
        tile, offset = divmod(place * width, LANES)
        if offset:
            block = pltpu.roll(block, offset, 1)
        if offset + width <= LANES:
            tiles[tile] = tiles[tile] + block
        else:
            tiles[tile] = tiles[tile] + jnp.where(lane >= offset, block, 0.0)
            tiles[tile + 1] = tiles[tile + 1] + jnp.where(lane < offset, block, 0.0)
    return tiles


def put_columns(blocks, order, stride):
    blk = lax.axis_index("blk")
    width = blocks[0].shape[1]
    blocks = [widened(block.astype(FULL), LANES) for block in blocks]
    placed = []
    for owner in range(len(blocks)):
        found = blocks[0]
        for k, block in zip(order, blocks[1:]):
            found = jnp.where((blk ^ owner) == k, block, found)
        placed.append(found)
    return laid(placed, width, stride)


def cut_of(rows, full):
    tail = full % LANES
    if tail == 0:
        return 0
    return round_up(rows // 2, 8) if tail <= LANES // 2 else rows


def packed_rows(rows, full):
    return round_up(full // LANES * rows + cut_of(rows, full), 16)


def columns_kernel(order, rows, full, *refs):
    *blocks, out_ref = refs
    tiles = put_columns([ref[...] for ref in blocks], order, round_up(full, LANES))
    cut = cut_of(rows, full)
    parts = [tile[:rows] for tile in tiles[: full // LANES]]
    if cut:
        last = tiles[-1][:cut]
        if cut < rows:
            lower = pltpu.roll(tiles[-1][cut:rows], LANES // 2, 1)
            last = last + jnp.concatenate([lower, jnp.zeros((2 * cut - rows, LANES), FULL)], axis=0)
        parts.append(last)
    out_ref[...] = rounded(jnp.concatenate(parts, axis=0), out_ref.shape[0])


def unpacked(ref, rows, full, last_tile=lambda tile: tile):
    block = ref[...].astype(FULL)
    whole, cut = full // LANES, cut_of(rows, full)
    tiles = [block[i * rows : (i + 1) * rows] for i in range(whole)]
    if cut:
        last = block[whole * rows : whole * rows + cut]
        if cut < rows:
            low = iota(last.shape, 1) < LANES // 2
            lower = pltpu.roll(jnp.where(low, 0.0, last), LANES // 2, 1)
            last = jnp.concatenate([jnp.where(low, last, 0.0), lower[: rows - cut]], axis=0)
        tiles.append(last_tile(last))
    return rounded(jnp.concatenate(tiles, axis=1), round_up(rows, 16))


def near_kernel(own_ref, mate_ref, pick_ref, shift_ref, adj_ref, rhs_ref, jac_ref, _, out_ref, image):
    rows, full = adj_ref.shape[0], jac_ref.shape[3]
    products([unpacked(ref, rows, full, twice) for ref in (own_ref, mate_ref)], pick_ref, jac_ref, image)
    out_ref[...] = without(shift_ref, adj_ref, rhs_ref, image)


def without(shift_ref, adj_ref, rhs_ref, image):
    rows, width = adj_ref.shape
    return rhs_ref[...] - (shift_ref[:rows, :width] * adj_ref[...] + image[:rows, :width])


def products(parts, pick_ref, jac_ref, image):
    elements, slots, width, full = jac_ref.shape
    rows_part, stride = parts[0].shape
    short = pick_ref.shape[1] - len(parts) * rows_part
    if short:
        parts = parts + [jnp.zeros((short, stride), HALF)]
    stacked = jnp.concatenate(parts, axis=0)
    picked = jnp.dot(pick_ref[...], stacked, preferred_element_type=FULL).astype(HALF)
    image[...] = jnp.zeros(image.shape, FULL)
    deep = full // (2 * LANES) * (2 * LANES)
    low = iota((2 * PICK, LANES), 1) < LANES // 2
    for pair in range(elements // 2):
        starts = [k * elements * PICK + pair * 2 * PICK for k in range(slots)]
        lefts = [picked[start : start + 2 * PICK] for start in starts]
        tails = [left[:, deep:] for left in lefts]
        tails = [jnp.where(low, *tails[k : k + 2]) if k + 1 < slots else tails[k] for k in range(0, slots, 2)]
        left = jnp.concatenate([left[:, :deep] for left in lefts] + tails, axis=1)
        for side in range(2):
            e = 2 * pair + side
            ends = [widened(jac_ref[e, k][:, deep:], LANES) for k in range(slots)]
            for k in range(1, slots, 2):
                ends[k - 1] = ends[k - 1] + pltpu.roll(ends[k], LANES // 2, 1)
            blocks = jnp.concatenate([jac_ref[e, k][:, :deep] for k in range(slots)] + ends[::2], axis=1)
            product = lax.dot_general(left, blocks, NT, preferred_element_type=FULL)
            first = side * PICK
            image[pl.ds(e, 3, stride=elements), :width] = product[first : first + 3]


def twice(tail):
    return tail + pltpu.roll(tail, LANES // 2, 1)


def quad_products(lefts, blocks):
    full = blocks[0].shape[1]
    deep = full // (2 * LANES) * (2 * LANES)
    shape = (4 * QUAD, LANES)
    low = iota(shape, 1) < LANES // 2
    mine = []
    for i in range(4):
        place = iota(shape, 0) - i * QUAD
        mine.append(jnp.logical_and(jnp.logical_and(place >= 0, place < QUAD), low if i % 2 == 0 else jnp.logical_not(low)))
    tails = [left[:, deep : deep + LANES] for left in lefts]
    left = [jnp.where(mine[i], tails[i], jnp.where(mine[i + 1], tails[i + 1], 0.0).astype(HALF)) for i in (0, 2)]
    low = iota((blocks[0].shape[0], LANES), 1) < LANES // 2
    ends = [widened(block[:, deep:], LANES) for block in blocks]
    right = [jnp.where(low, ends[i], pltpu.roll(ends[i + 1], LANES // 2, 1)) for i in (0, 2)]
    shared = lax.dot_general(
        jnp.concatenate(left, axis=1), jnp.concatenate(right, axis=1), NT, preferred_element_type=FULL
    )
    products = []
    for i, (left, block) in enumerate(zip(lefts, blocks)):
        product = lax.dot_general(left[:, :deep], block[:, :deep], NT, preferred_element_type=FULL)
        part = slice(i * QUAD, (i + 1) * QUAD)
        products.append(product[part] + shared[part])
    return products


def far_kernel(near_ref, far_ref, jac_ref, list_ref, count_ref, _shapes, _ids, out_ref, spread, sums, image):
    elements, slots, width, _ = jac_ref.shape
    far = unpacked(far_ref, near_ref.shape[0], jac_ref.shape[3], twice)
    rows, stride = far.shape
    deep = spread.shape[1]
    shape = (elements, deep, rows)
    element, row, lane = [iota(shape, dim).reshape(elements * deep, rows) for dim in range(3)]
    row = lax.bitwise_and(row, QUAD - 1)
    pick = hit(jnp.where(row < 3, row * elements + element, -1) == lane).astype(HALF)
    taken = jnp.dot(pick, far, preferred_element_type=FULL).astype(HALF)
    spread[:elements] = taken.reshape(elements, deep, stride)
    spread[elements:] = jnp.zeros((spread.shape[0] - elements, deep, stride), HALF)
    sums[...] = jnp.zeros(sums.shape, FULL)

    @pl.loop(0, count_ref[0])
    def _(step):
        for i in range(0, GROUP, 4):
            owners, lefts, blocks = [], [], []
            for side in range(4):
                word = list_ref[step * GROUP + i + side]
                block = lax.shift_right_logical(word, 5)
                owners.append(lax.div(block, slots))
                lefts.append(spread[lax.bitwise_and(word, 31)])
                blocks.append(jac_ref[owners[side], block - owners[side] * slots])
            for e, product in zip(owners, quad_products(lefts, blocks)):
                sums[e, :QUAD, :width] += product

    for e in range(elements):
        image[pl.ds(e, 3, stride=elements), :] = sums[e, :3, :]
    real = near_ref.shape[0]
    out_ref[...] = rounded(near_ref[...] - image[:real, :width], out_ref.shape[0])


def element_of_row(shape, elements, copies=3):
    row = iota(shape, 0)
    for step in range(1, copies + 1):
        row = row - jnp.where(iota(shape, 0) >= step * elements, elements, 0)
    return row


def updated(resid_refs, inv_ref, adj_ref, update):
    rows, width = adj_ref.shape
    elements = rows // 3
    stride = round_up(inv_ref.shape[2], LANES)
    resid = put_columns([ref[...] for ref in resid_refs], distances(), stride)
    resid[-1] = twice(resid[-1])
    resid = jnp.concatenate(resid, axis=1).astype(HALF)
    shape = (elements, QUAD, resid.shape[0])
    deep = elements * QUAD
    element, row, lane = [iota(shape, dim).reshape(deep, -1) for dim in range(3)]
    pick = hit(jnp.where(row < 3, row * elements + element, -1) == lane).astype(HALF)
    resid = jnp.dot(pick, resid, preferred_element_type=FULL).astype(HALF)
    update[...] = jnp.zeros(update.shape, FULL)
    for first in range(0, elements, 4):
        left = resid[first * QUAD : (first + 4) * QUAD]
        for i, product in enumerate(quad_products([left] * 4, [inv_ref[first + i] for i in range(4)])):
            update[pl.ds(first + i, 3, stride=elements), :width] = product[:3]
    short = jnp.zeros((update.shape[0] - rows, width), FULL)
    return jnp.concatenate([adj_ref[...] + update[:rows, :width], short], axis=0)


def update_kernel(*refs):
    *resid_refs, inv_ref, adj_ref, adj_out, half_out, update = refs
    adj = updated(resid_refs, inv_ref, adj_ref, update)
    adj_out[...] = adj[: adj_out.shape[0]]
    half_out[...] = adj.astype(HALF)


def split(value):
    top = value.astype(HALF)
    return top, (value - top.astype(FULL)).astype(HALF)


def gradient_kernel(*refs):
    blks = lax.axis_size("blk")
    resid_refs = refs[:blks]
    inv_ref, adj_ref, shape_ref, low_ref, target_ref, adj_out = refs[blks : blks + 6]
    part_outs = refs[blks + 6 : blks + 9]
    sorted_ref, left_ref, sums_ref, update = refs[blks + 9 :]
    adj = updated(resid_refs, inv_ref, adj_ref, update)
    adj_out[...] = adj[: adj_out.shape[0]]
    half = adj.astype(HALF)
    elements = adj_out.shape[0] // 3
    pairs = elements // 2
    tall, width = half.shape
    coords = shape_ref.shape[2]
    depth = 3 if elements % 3 == 0 and 3 * width <= 256 else 1
    block = widened(half.astype(FULL), LANES)
    left = jnp.concatenate(laid([block] * depth, width, round_up(depth * width, LANES)), axis=1)[:, : depth * width]
    shape = left.shape
    owner = element_of_row(shape, elements)
    group = jnp.zeros(shape, jnp.int32)
    for step in range(1, elements // depth):
        group = group + jnp.where(owner >= step * depth, 1, 0)
    first = (owner - group * depth) * width
    behind = iota(shape, 1) - first
    left = jnp.where(jnp.logical_and(behind >= 0, behind < width), left, 0.0).astype(HALF)
    shape = (tall, coords)
    owner = element_of_row(shape, elements)
    total = jnp.zeros(shape, FULL)
    for start in range(0, elements, depth):
        partials = jnp.concatenate([shape_ref[start + step] for step in range(depth)], axis=0)
        product = jnp.dot(left, partials, preferred_element_type=FULL)
        total = jnp.where(owner >= start, product, total)
    low = iota((tall, LANES), 1) < LANES // 2
    odd = lax.bitwise_and(owner[:, :LANES], 1) == 1
    values = [total[:, :LANES], widened(total[:, LANES:], LANES)]
    turned = [pltpu.roll(value, LANES // 2, 1) for value in values]
    value = [
        jnp.where(odd, jnp.where(low, 0.0, turned[0]), jnp.where(low, values[0], 0.0)),
        jnp.where(odd, jnp.where(low, 0.0, values[0]), jnp.where(low, turned[0], 0.0)),
        jnp.where(odd, turned[1], values[1]),
    ]
    top, rest = split(jnp.concatenate(value, axis=1))
    sorted_ref[:tall] = top.astype(FULL)
    sorted_ref[tall:] = rest.astype(FULL)
    deep = 16
    for pair in range(pairs):
        lanes = slice(pair * LANES, (pair + 1) * LANES)
        mine = iota((deep, LANES), 0) == target_ref[pair : pair + 1, :]
        for part in range(2):
            for j in range(3):
                for c in range(3):
                    at = part * tall + j * elements + 2 * pair
                    lanes_of_axis = slice(c * LANES, (c + 1) * LANES)
                    values = sorted_ref[at : at + 1, lanes_of_axis] + sorted_ref[at + 1 : at + 2, lanes_of_axis]
                    start = (part * 9 + j * 3 + c) * deep
                    left_ref[start : start + deep, lanes] = jnp.where(mine, values, 0.0).astype(HALF)
    sums = lax.dot_general(left_ref[...], low_ref[...], NT, preferred_element_type=FULL)
    span = low_ref.shape[0]
    sums = -(sums[: 9 * deep] + sums[9 * deep :])
    tiles = [(tile, tile * LANES, min(span, (tile + 1) * LANES)) for tile in range(sums_ref.shape[0])]
    for tile, start, stop in tiles:
        sums_ref[tile, :, : stop - start] = sums[:, start:stop]
    for part, out_ref in enumerate(part_outs):
        for tile, start, stop in tiles:
            found = [sums_ref[tile, pl.ds(part * blks + k, 9, stride=deep), :][:, : stop - start] for k in range(blks)]
            found = jnp.concatenate(found + [jnp.zeros((out_ref.shape[0] - 9 * blks, stop - start), FULL)], axis=0)
            out_ref[:, start:stop] = found.astype(out_ref.dtype)


def combine_kernel(own_ref, mate_ref, far_ref, *piece_outs):
    total = own_ref[...] + mate_ref[...].astype(FULL) + far_ref[...].astype(FULL)
    for k, out_ref in enumerate(piece_outs):
        piece = total[9 * k : 9 * (k + 1)]
        out_ref[...] = rounded(piece, 16) if k else piece


def local(
    adjoint_start,
    right_sides,
    jac_blocks,
    block_inverse,
    neighbours,
    pseudo_shift,
    shape_partials,
    node_ids,
):
    elements, sides, width = adjoint_start.shape
    slots, full = jac_blocks.shape[1], jac_blocks.shape[3]
    enodes = node_ids.shape[1]
    rows = sides * elements
    tall = round_up(rows, 16)
    stride = round_up(full, LANES)
    blks = lax.axis_size("blk")
    span = NODE_DEV // blks
    stacked = round_up(3 * tall, LANES)
    entries = elements * enodes

    adj_hbm = jnp.transpose(adjoint_start, (1, 0, 2)).reshape(rows, width)
    rhs = jnp.transpose(right_sides, (1, 0, 2)).reshape(rows, width)
    half_shape = jax.ShapeDtypeStruct((tall, width), HALF)

    adj_shape = jax.ShapeDtypeStruct((rows, width), FULL)
    pick, shift, far_list, far_count, adj, rhs = call(
        slots_kernel,
        "slots",
        [in_hbm(neighbours.T), in_hbm(pseudo_shift), in_hbm(adj_hbm), in_hbm(rhs), in_hbm(jac_blocks)],
        [HBM] * 5,
        [
            jax.ShapeDtypeStruct((slots * elements * PICK, stacked), HALF),
            jax.ShapeDtypeStruct((tall, LANES), FULL),
            pltpu.SMEM((round_up(elements * (slots - 1) + GROUP, LANES),), jnp.int32),
            pltpu.SMEM((1,), jnp.int32),
            pltpu.VMEM((rows, width), FULL),
            pltpu.VMEM((rows, width), FULL),
        ],
        scratch=[
            pltpu.VMEM((slots - 1, elements), jnp.int32),
            pltpu.SMEM((slots - 1, elements), jnp.int32),
            pltpu.SMEM((elements,), FULL),
            pltpu.SemaphoreType.DMA((6,)),
        ],
        moved=16 * MIB,
    )
    low, target, shapes = call(
        nodes_kernel,
        "nodes",
        [node_ids, shape_partials],
        [VMEM, VMEM],
        [
            jax.ShapeDtypeStruct((span, entries), HALF),
            jax.ShapeDtypeStruct((entries // LANES, LANES), jnp.int32),
            jax.ShapeDtypeStruct(shape_partials.shape, HALF),
        ],
        moved=3 * MIB,
    )

    for sweep in range(SWEEPS):
        order = distances()
        blocks = [half] + over_blk(half, order) if sweep else [adj] + over_blk(adj_hbm, order)
        wide = jax.ShapeDtypeStruct((packed_rows(rows, full), LANES), HALF)
        (own,) = call(functools.partial(columns_kernel, order, rows, full), "columns", blocks, [VMEM] * blks, [wide], moved=1 * MIB)
        far, mate = to_far(own), to_mate(own)
        image = pltpu.VMEM((tall, LANES), FULL)
        near_inputs = [own, mate, pick, shift, adj, rhs]
        far_scratch = [
            pltpu.VMEM((elements + 8, 16, stride), HALF),
            pltpu.VMEM((elements, PICK, LANES), FULL),
            image,
        ]
        (near,) = call(
            near_kernel,
            "near",
            near_inputs + [jac_blocks, in_hbm(block_inverse)],
            [VMEM] * 7 + [HBM],
            [adj_shape],
            [image],
            moved=12 * MIB,
        )
        (resid,) = call(
            far_kernel,
            "far",
            [near, far, jac_blocks, far_list, far_count, in_hbm(shape_partials), in_hbm(node_ids)],
            [VMEM] * 3 + [SMEM] * 2 + [HBM] * 2,
            [half_shape],
            far_scratch,
            moved=4 * MIB,
        )
        resids = [resid] + over_blk(resid, distances())
        if sweep < SWEEPS - 1:
            adj, half = call(
                update_kernel,
                "update",
                resids + [block_inverse, adj],
                [VMEM] * (blks + 2),
                [adj_shape, half_shape],
                scratch=[pltpu.VMEM((tall, LANES), FULL)],
                moved=8 * MIB,
            )
    deep = round_up(9 * blks, 16)
    adj, own, mate, far = call(
        gradient_kernel,
        "gradient",
        resids + [block_inverse, adj, shapes, low, target],
        [VMEM] * (blks + 5),
        [adj_shape] + [jax.ShapeDtypeStruct((deep, span), kind) for kind in (FULL, HALF, HALF)],
        scratch=[
            pltpu.VMEM((2 * tall, 3 * LANES), FULL),
            pltpu.VMEM((2 * 9 * 16, entries), HALF),
            pltpu.VMEM((-(-span // LANES), 9 * 16, LANES), FULL),
            pltpu.VMEM((tall, LANES), FULL),
        ],
    )
    far, mate = to_far(far), to_mate(mate)
    shapes = [jax.ShapeDtypeStruct((16, span), HALF)] * (blks - 1)
    pieces = call(
        combine_kernel, "combine", [own, mate, far], [VMEM] * 3, [jax.ShapeDtypeStruct((9, span), FULL)] + shapes
    )
    gradient = pieces[0]
    count = lax.axis_size("blk")
    for k in reversed(distances()):
        gradient = gradient + lax.ppermute(pieces[k], "blk", [(i, i ^ k) for i in range(count)])[:9].astype(FULL)
    adjoint = jnp.transpose(adj.reshape(sides, elements, width), (1, 0, 2))
    return (adjoint, gradient)


def solution(mesh):
    in_specs = (
        P("dom", None, "blk"),
        P("dom", None, "blk"),
        P("dom", None, "blk", None),
        P("dom", "blk", None),
        P("dom", None),
        P("dom"),
        P("dom", "blk", None),
        P("dom", None),
    )
    out_specs = (P("dom", None, "blk"), P(None, ("dom", "blk")))
    return jax.shard_map(local, mesh=mesh, in_specs=in_specs, out_specs=out_specs, check_vma=False)
```

```python
import functools

import jax
import jax.numpy as jnp
from jax import lax
from jax.experimental import pallas as pl
from jax.experimental.pallas import tpu as pltpu
from jax.sharding import PartitionSpec as P

SWEEPS = 2
NODE_DEV = 768
HALF = jnp.bfloat16
FULL = jnp.float32
LANES = 128
QUAD = 4
NT = (((1,), (1,)), ((), ()))
VMEM = pl.BlockSpec(memory_space=pltpu.VMEM)
SMEM = pl.BlockSpec(memory_space=pltpu.SMEM)
HBM = pl.BlockSpec(memory_space=pltpu.HBM)
GROUP = 60
MIB = 1024 * 1024


def round_up(size, unit):
    return -(-size // unit) * unit


def iota(shape, dim):
    return lax.broadcasted_iota(jnp.int32, shape, dim)


def hit(condition):
    return jnp.where(condition, 1.0, 0.0)


def in_hbm(array):
    return pltpu.with_memory_space_constraint(array, pltpu.HBM)


def call(kernel, name, args, specs, outs, scratch=(), limit=16, flops=0, moved=0, aliases=None):
    return pl.pallas_call(
        kernel,
        in_specs=specs,
        out_specs=[SMEM if getattr(out, "memory_space", None) is pltpu.SMEM else VMEM for out in outs],
        input_output_aliases=aliases or {},
        out_shape=outs,
        scratch_shapes=list(scratch),
        compiler_params=pltpu.CompilerParams(vmem_limit_bytes=limit * MIB),
        cost_estimate=pl.CostEstimate(flops=flops, bytes_accessed=moved, transcendentals=0),
        name=name,
    )(*args)


def distances():
    return list(range(1, lax.axis_size("blk")))


def over_blk(block, order):
    count = lax.axis_size("blk")
    return [lax.ppermute(block, "blk", [(i, i ^ k) for i in range(count)]) for k in order]


def to_mate(block):
    return lax.ppermute(block, "dom", [(i, i ^ 1) for i in range(lax.axis_size("dom"))])


def to_far(block):
    count = lax.axis_size("dom")
    return lax.ppermute(block, "dom", [(i, (((i + 1) ^ 1) - 1) % count) for i in range(count)])


def rounded(block, rows):
    short = rows - block.shape[0]
    if short:
        block = jnp.concatenate([block, jnp.zeros((short, block.shape[1]), block.dtype)], axis=0)
    return block.astype(HALF)


def window(ids, count):
    dom = lax.axis_index("dom")
    odd = lax.rem(dom, 2)
    place = ids - dom * count
    below = jnp.where(place < 0, 1, 0)
    above = jnp.where(place >= count, 1, 0)
    mate = odd * below + (1 - odd) * above
    return 2 * (below + above) - mate, place + (below - above) * count


def started(pairs, sems):
    copies = [pltpu.make_async_copy(source, target, sems.at[i]) for i, (source, target) in enumerate(pairs)]
    for copy in copies:
        copy.start()
    return copies


def slots_kernel(
    nb_hbm, shift_hbm, adj_hbm, rhs_hbm, _,
    pick_out, shift_out, list_out, count_out, adj_out, rhs_out, nb_ref, scalar_nb_ref, shift_ref, sems,
):
    pairs = [(nb_hbm, nb_ref), (shift_hbm, shift_ref), (adj_hbm, adj_out), (rhs_hbm, rhs_out)]
    copies = started(pairs + [(nb_hbm, scalar_nb_ref)], sems)
    copies[0].wait()
    copies[1].wait()
    copies[4].wait()
    list_far(scalar_nb_ref, list_out, count_out)
    faces, elements = nb_ref.shape
    rows_part = round_up(3 * elements, 16)
    part, inside = window(nb_ref[...], elements)
    bases = jnp.concatenate([iota((1, elements), 1), part * rows_part + inside], axis=0).astype(FULL)
    deep = elements * QUAD
    shape = (deep, elements)
    behind = iota(shape, 0) - QUAD * iota(shape, 1)
    owner = hit(jnp.logical_and(behind >= 0, behind < QUAD)).astype(HALF)
    columns = lax.dot_general(owner, bases.astype(HALF), NT, preferred_element_type=FULL)
    shape = (elements, QUAD, pick_out.shape[1])
    row, lane = iota(shape, 1).reshape(deep, -1), iota(shape, 2).reshape(deep, -1)
    offset = jnp.where(row < 3, lane - elements * row, -1).astype(FULL)
    for k in range(faces + 1):
        pick_out[k * deep : (k + 1) * deep, :] = hit(offset == columns[:, k : k + 1]).astype(HALF)
    shift_out[...] = jnp.zeros(shift_out.shape, FULL)
    for e in range(elements):
        shift_out[pl.ds(e, 3, stride=elements), :] = jnp.full((3, shift_out.shape[1]), shift_ref[e], FULL)
    for copy in (copies[2], copies[3]):
        copy.wait()


def list_far(nb_ref, list_out, count_out):
    faces, elements = nb_ref.shape

    count = jnp.int32(0)
    for e in range(elements):
        for k in range(1, faces + 1):
            part, inside = window(nb_ref[k - 1, e], elements)
            list_out[count] = (e * (faces + 1) + k) * 32 + inside
            count = count + lax.shift_right_logical(part, 1)
    for step in range(GROUP):
        list_out[count + step] = elements
    count_out[0] = lax.div(count + GROUP - 1, GROUP)


def nodes_kernel(ids_ref, shape_ref, low_out, target_out, shape_out):
    blk = lax.axis_index("blk")
    blks = lax.axis_size("blk")
    span = NODE_DEV // blks
    ids = ids_ref[...]
    pairs = ids.shape[0] // 2
    ids = [jnp.concatenate([ids[2 * p : 2 * p + 1], ids[2 * p + 1 : 2 * p + 2]], axis=1) for p in range(pairs)]
    part, inside = window(jnp.concatenate(ids, axis=0), NODE_DEV)
    owner = jnp.zeros_like(inside)
    for cut in range(1, blks):
        owner = owner + jnp.where(inside >= cut * span, 1, 0)
    low = inside - owner * span
    target_out[...] = part * blks + (owner ^ blk)
    shape = (span, LANES)
    for group in range(pairs):
        same = iota(shape, 0) == low[group : group + 1, :]
        low_out[:, group * LANES : (group + 1) * LANES] = hit(same).astype(HALF)

    elements, _, coords = shape_ref.shape
    nodes = coords // 3
    row, lane = iota((coords, coords), 0), iota((coords, coords), 1)
    axis = jnp.where(lane >= nodes, 1, 0) + jnp.where(lane >= 2 * nodes, 1, 0)
    sort = hit(row == 3 * (lane - axis * nodes) + axis).astype(HALF)
    for e in range(elements):
        shape_out[e] = jnp.dot(shape_ref[e], sort, preferred_element_type=FULL).astype(HALF)


def widened(block, lanes):
    short = lanes - block.shape[1]
    if short == 0:
        return block
    return jnp.concatenate([block, jnp.zeros((block.shape[0], short), block.dtype)], axis=1)


def laid(blocks, width, stride):
    lane = iota(blocks[0].shape, 1)
    tiles = [0.0] * (stride // LANES)
    for place, block in enumerate(blocks):
        tile, offset = divmod(place * width, LANES)
        if offset:
            block = pltpu.roll(block, offset, 1)
        if offset + width <= LANES:
            tiles[tile] = tiles[tile] + block
        else:
            tiles[tile] = tiles[tile] + jnp.where(lane >= offset, block, 0.0)
            tiles[tile + 1] = tiles[tile + 1] + jnp.where(lane < offset, block, 0.0)
    return tiles


def put_columns(blocks, order, stride):
    blk = lax.axis_index("blk")
    width = blocks[0].shape[1]
    blocks = [widened(block.astype(FULL), LANES) for block in blocks]
    placed = []
    for owner in range(len(blocks)):
        found = blocks[0]
        for k, block in zip(order, blocks[1:]):
            found = jnp.where((blk ^ owner) == k, block, found)
        placed.append(found)
    return laid(placed, width, stride)


def cut_of(rows, full):
    tail = full % LANES
    if tail == 0:
        return 0
    return round_up(rows // 2, 8) if tail <= LANES // 2 else rows


def packed_rows(rows, full):
    return round_up(full // LANES * rows + cut_of(rows, full), 16)


def columns_kernel(order, rows, full, *refs):
    *blocks, out_ref = refs
    tiles = put_columns([ref[...] for ref in blocks], order, round_up(full, LANES))
    cut = cut_of(rows, full)
    parts = [tile[:rows] for tile in tiles[: full // LANES]]
    if cut:
        last = tiles[-1][:cut]
        if cut < rows:
            lower = pltpu.roll(tiles[-1][cut:rows], LANES // 2, 1)
            last = last + jnp.concatenate([lower, jnp.zeros((2 * cut - rows, LANES), FULL)], axis=0)
        parts.append(last)
    out_ref[...] = rounded(jnp.concatenate(parts, axis=0), out_ref.shape[0])


def unpacked(ref, rows, full, last_tile=lambda tile: tile):
    block = ref[...].astype(FULL)
    whole, cut = full // LANES, cut_of(rows, full)
    tiles = [block[i * rows : (i + 1) * rows] for i in range(whole)]
    if cut:
        last = block[whole * rows : whole * rows + cut]
        if cut < rows:
            low = iota(last.shape, 1) < LANES // 2
            lower = pltpu.roll(jnp.where(low, 0.0, last), LANES // 2, 1)
            last = jnp.concatenate([jnp.where(low, last, 0.0), lower[: rows - cut]], axis=0)
        tiles.append(last_tile(last))
    return rounded(jnp.concatenate(tiles, axis=1), round_up(rows, 16))


def near_kernel(own_ref, mate_ref, pick_ref, shift_ref, adj_ref, rhs_ref, jac_ref, _, out_ref, image):
    rows, full = adj_ref.shape[0], jac_ref.shape[3]
    products([unpacked(ref, rows, full, twice) for ref in (own_ref, mate_ref)], pick_ref, jac_ref, image)
    out_ref[...] = without(shift_ref, adj_ref, rhs_ref, image)


def without(shift_ref, adj_ref, rhs_ref, image):
    rows, width = adj_ref.shape
    return rhs_ref[...] - (shift_ref[:rows, :width] * adj_ref[...] + image[:rows, :width])


def products(parts, pick_ref, jac_ref, image):
    elements, slots, width, full = jac_ref.shape
    rows_part, stride = parts[0].shape
    short = pick_ref.shape[1] - len(parts) * rows_part
    if short:
        parts = parts + [jnp.zeros((short, stride), HALF)]
    stacked = jnp.concatenate(parts, axis=0)
    picked = jnp.dot(pick_ref[...], stacked, preferred_element_type=FULL).astype(HALF)
    image[...] = jnp.zeros(image.shape, FULL)
    deep = full // (2 * LANES) * (2 * LANES)
    low = iota((4 * QUAD, LANES), 1) < LANES // 2
    for first in range(0, elements, 4):
        starts = [(k * elements + first) * QUAD for k in range(slots)]
        lefts = [picked[start : start + 4 * QUAD] for start in starts]
        tails = [left[:, deep:] for left in lefts]
        tails = [jnp.where(low, *tails[k : k + 2]) if k + 1 < slots else tails[k] for k in range(0, slots, 2)]
        left = jnp.concatenate([left[:, :deep] for left in lefts] + tails, axis=1)
        for i in range(4):
            e = first + i
            ends = [widened(jac_ref[e, k][:, deep:], LANES) for k in range(slots)]
            for k in range(1, slots, 2):
                ends[k - 1] = ends[k - 1] + pltpu.roll(ends[k], LANES // 2, 1)
            blocks = jnp.concatenate([jac_ref[e, k][:, :deep] for k in range(slots)] + ends[::2], axis=1)
            product = lax.dot_general(left, blocks, NT, preferred_element_type=FULL)
            image[pl.ds(e, 3, stride=elements), :width] = product[i * QUAD : i * QUAD + 3]


def twice(tail):
    return tail + pltpu.roll(tail, LANES // 2, 1)


def quad_products(lefts, blocks):
    full = blocks[0].shape[1]
    deep = full // (2 * LANES) * (2 * LANES)
    shape = (4 * QUAD, LANES)
    low = iota(shape, 1) < LANES // 2
    mine = []
    for i in range(4):
        place = iota(shape, 0) - i * QUAD
        mine.append(jnp.logical_and(jnp.logical_and(place >= 0, place < QUAD), low if i % 2 == 0 else jnp.logical_not(low)))
    tails = [left[:, deep : deep + LANES] for left in lefts]
    left = [jnp.where(mine[i], tails[i], jnp.where(mine[i + 1], tails[i + 1], 0.0).astype(HALF)) for i in (0, 2)]
    low = iota((blocks[0].shape[0], LANES), 1) < LANES // 2
    ends = [widened(block[:, deep:], LANES) for block in blocks]
    right = [jnp.where(low, ends[i], pltpu.roll(ends[i + 1], LANES // 2, 1)) for i in (0, 2)]
    shared = lax.dot_general(
        jnp.concatenate(left, axis=1), jnp.concatenate(right, axis=1), NT, preferred_element_type=FULL
    )
    products = []
    for i, (left, block) in enumerate(zip(lefts, blocks)):
        product = lax.dot_general(left[:, :deep], block[:, :deep], NT, preferred_element_type=FULL)
        part = slice(i * QUAD, (i + 1) * QUAD)
        products.append(product[part] + shared[part])
    return products


def far_kernel(near_ref, far_ref, jac_ref, list_ref, count_ref, _shapes, _ids, out_ref, spread, sums, image):
    elements, slots, width, _ = jac_ref.shape
    far = unpacked(far_ref, near_ref.shape[0], jac_ref.shape[3], twice)
    rows, stride = far.shape
    deep = spread.shape[1]
    shape = (elements, deep, rows)
    element, row, lane = [iota(shape, dim).reshape(elements * deep, rows) for dim in range(3)]
    row = lax.bitwise_and(row, QUAD - 1)
    pick = hit(jnp.where(row < 3, row * elements + element, -1) == lane).astype(HALF)
    taken = jnp.dot(pick, far, preferred_element_type=FULL).astype(HALF)
    spread[:elements] = taken.reshape(elements, deep, stride)
    spread[elements:] = jnp.zeros((spread.shape[0] - elements, deep, stride), HALF)
    sums[...] = jnp.zeros(sums.shape, FULL)

    @pl.loop(0, count_ref[0])
    def _(step):
        for i in range(0, GROUP, 4):
            owners, lefts, blocks = [], [], []
            for side in range(4):
                word = list_ref[step * GROUP + i + side]
                block = lax.shift_right_logical(word, 5)
                owners.append(lax.div(block, slots))
                lefts.append(spread[lax.bitwise_and(word, 31)])
                blocks.append(jac_ref[owners[side], block - owners[side] * slots])
            for e, product in zip(owners, quad_products(lefts, blocks)):
                sums[e, :QUAD, :width] += product

    for e in range(elements):
        image[pl.ds(e, 3, stride=elements), :] = sums[e, :3, :]
    real = near_ref.shape[0]
    out_ref[...] = rounded(near_ref[...] - image[:real, :width], out_ref.shape[0])


def element_of_row(shape, elements, copies=3):
    row = iota(shape, 0)
    for step in range(1, copies + 1):
        row = row - jnp.where(iota(shape, 0) >= step * elements, elements, 0)
    return row


def updated(resid_refs, inv_ref, adj_ref, update):
    rows, width = adj_ref.shape
    elements = rows // 3
    stride = round_up(inv_ref.shape[2], LANES)
    resid = put_columns([ref[...] for ref in resid_refs], distances(), stride)
    resid[-1] = twice(resid[-1])
    resid = jnp.concatenate(resid, axis=1).astype(HALF)
    shape = (elements, QUAD, resid.shape[0])
    deep = elements * QUAD
    element, row, lane = [iota(shape, dim).reshape(deep, -1) for dim in range(3)]
    pick = hit(jnp.where(row < 3, row * elements + element, -1) == lane).astype(HALF)
    resid = jnp.dot(pick, resid, preferred_element_type=FULL).astype(HALF)
    update[...] = jnp.zeros(update.shape, FULL)
    for first in range(0, elements, 4):
        left = resid[first * QUAD : (first + 4) * QUAD]
        for i, product in enumerate(quad_products([left] * 4, [inv_ref[first + i] for i in range(4)])):
            update[pl.ds(first + i, 3, stride=elements), :width] = product[:3]
    short = jnp.zeros((update.shape[0] - rows, width), FULL)
    return jnp.concatenate([adj_ref[...] + update[:rows, :width], short], axis=0)


def update_kernel(*refs):
    *resid_refs, inv_ref, adj_ref, adj_out, half_out, update = refs
    adj = updated(resid_refs, inv_ref, adj_ref, update)
    adj_out[...] = adj[: adj_out.shape[0]]
    half_out[...] = adj.astype(HALF)


def split(value):
    top = value.astype(HALF)
    return top, (value - top.astype(FULL)).astype(HALF)


def gradient_kernel(*refs):
    blks = lax.axis_size("blk")
    resid_refs = refs[:blks]
    inv_ref, adj_ref, shape_ref, low_ref, target_ref, adj_out = refs[blks : blks + 6]
    part_outs = refs[blks + 6 : blks + 9]
    sorted_ref, left_ref, sums_ref, update = refs[blks + 9 :]
    adj = updated(resid_refs, inv_ref, adj_ref, update)
    adj_out[...] = adj[: adj_out.shape[0]]
    half = adj.astype(HALF)
    elements = adj_out.shape[0] // 3
    pairs = elements // 2
    tall, width = half.shape
    coords = shape_ref.shape[2]
    depth = 3 if elements % 3 == 0 and 3 * width <= 256 else 1
    block = widened(half.astype(FULL), LANES)
    left = jnp.concatenate(laid([block] * depth, width, round_up(depth * width, LANES)), axis=1)[:, : depth * width]
    shape = left.shape
    owner = element_of_row(shape, elements)
    group = jnp.zeros(shape, jnp.int32)
    for step in range(1, elements // depth):
        group = group + jnp.where(owner >= step * depth, 1, 0)
    first = (owner - group * depth) * width
    behind = iota(shape, 1) - first
    left = jnp.where(jnp.logical_and(behind >= 0, behind < width), left, 0.0).astype(HALF)
    shape = (tall, coords)
    owner = element_of_row(shape, elements)
    total = jnp.zeros(shape, FULL)
    for start in range(0, elements, depth):
        partials = jnp.concatenate([shape_ref[start + step] for step in range(depth)], axis=0)
        product = jnp.dot(left, partials, preferred_element_type=FULL)
        total = jnp.where(owner >= start, product, total)
    low = iota((tall, LANES), 1) < LANES // 2
    odd = lax.bitwise_and(owner[:, :LANES], 1) == 1
    values = [total[:, :LANES], widened(total[:, LANES:], LANES)]
    turned = [pltpu.roll(value, LANES // 2, 1) for value in values]
    value = [
        jnp.where(odd, jnp.where(low, 0.0, turned[0]), jnp.where(low, values[0], 0.0)),
        jnp.where(odd, jnp.where(low, 0.0, values[0]), jnp.where(low, turned[0], 0.0)),
        jnp.where(odd, turned[1], values[1]),
    ]
    top, rest = split(jnp.concatenate(value, axis=1))
    sorted_ref[:tall] = top.astype(FULL)
    sorted_ref[tall:] = rest.astype(FULL)
    deep = 16
    for pair in range(pairs):
        lanes = slice(pair * LANES, (pair + 1) * LANES)
        mine = iota((deep, LANES), 0) == target_ref[pair : pair + 1, :]
        for part in range(2):
            for j in range(3):
                for c in range(3):
                    at = part * tall + j * elements + 2 * pair
                    lanes_of_axis = slice(c * LANES, (c + 1) * LANES)
                    values = sorted_ref[at : at + 1, lanes_of_axis] + sorted_ref[at + 1 : at + 2, lanes_of_axis]
                    start = (part * 9 + j * 3 + c) * deep
                    left_ref[start : start + deep, lanes] = jnp.where(mine, values, 0.0).astype(HALF)
    sums = lax.dot_general(left_ref[...], low_ref[...], NT, preferred_element_type=FULL)
    span = low_ref.shape[0]
    sums = -(sums[: 9 * deep] + sums[9 * deep :])
    tiles = [(tile, tile * LANES, min(span, (tile + 1) * LANES)) for tile in range(sums_ref.shape[0])]
    for tile, start, stop in tiles:
        sums_ref[tile, :, : stop - start] = sums[:, start:stop]
    for part, out_ref in enumerate(part_outs):
        for tile, start, stop in tiles:
            found = [sums_ref[tile, pl.ds(part * blks + k, 9, stride=deep), :][:, : stop - start] for k in range(blks)]
            found = jnp.concatenate(found + [jnp.zeros((out_ref.shape[0] - 9 * blks, stop - start), FULL)], axis=0)
            out_ref[:, start:stop] = found.astype(out_ref.dtype)


def combine_kernel(own_ref, mate_ref, far_ref, *piece_outs):
    total = own_ref[...] + mate_ref[...].astype(FULL) + far_ref[...].astype(FULL)
    for k, out_ref in enumerate(piece_outs):
        piece = total[9 * k : 9 * (k + 1)]
        out_ref[...] = rounded(piece, 16) if k else piece


def local(
    adjoint_start,
    right_sides,
    jac_blocks,
    block_inverse,
    neighbours,
    pseudo_shift,
    shape_partials,
    node_ids,
):
    elements, sides, width = adjoint_start.shape
    slots, full = jac_blocks.shape[1], jac_blocks.shape[3]
    enodes = node_ids.shape[1]
    rows = sides * elements
    tall = round_up(rows, 16)
    stride = round_up(full, LANES)
    blks = lax.axis_size("blk")
    span = NODE_DEV // blks
    stacked = round_up(3 * tall, LANES)
    entries = elements * enodes

    adj_hbm = jnp.transpose(adjoint_start, (1, 0, 2)).reshape(rows, width)
    rhs = jnp.transpose(right_sides, (1, 0, 2)).reshape(rows, width)
    half_shape = jax.ShapeDtypeStruct((tall, width), HALF)

    adj_shape = jax.ShapeDtypeStruct((rows, width), FULL)
    pick, shift, far_list, far_count, adj, rhs = call(
        slots_kernel,
        "slots",
        [in_hbm(neighbours.T), in_hbm(pseudo_shift), in_hbm(adj_hbm), in_hbm(rhs), in_hbm(jac_blocks)],
        [HBM] * 5,
        [
            jax.ShapeDtypeStruct((slots * elements * QUAD, stacked), HALF),
            jax.ShapeDtypeStruct((tall, LANES), FULL),
            pltpu.SMEM((round_up(elements * (slots - 1) + GROUP, LANES),), jnp.int32),
            pltpu.SMEM((1,), jnp.int32),
            pltpu.VMEM((rows, width), FULL),
            pltpu.VMEM((rows, width), FULL),
        ],
        scratch=[
            pltpu.VMEM((slots - 1, elements), jnp.int32),
            pltpu.SMEM((slots - 1, elements), jnp.int32),
            pltpu.SMEM((elements,), FULL),
            pltpu.SemaphoreType.DMA((6,)),
        ],
        moved=16 * MIB,
    )
    low, target, shapes = call(
        nodes_kernel,
        "nodes",
        [node_ids, shape_partials],
        [VMEM, VMEM],
        [
            jax.ShapeDtypeStruct((span, entries), HALF),
            jax.ShapeDtypeStruct((entries // LANES, LANES), jnp.int32),
            jax.ShapeDtypeStruct(shape_partials.shape, HALF),
        ],
        moved=3 * MIB,
    )

    for sweep in range(SWEEPS):
        order = distances()
        blocks = [half] + over_blk(half, order) if sweep else [adj] + over_blk(adj_hbm, order)
        wide = jax.ShapeDtypeStruct((packed_rows(rows, full), LANES), HALF)
        (own,) = call(functools.partial(columns_kernel, order, rows, full), "columns", blocks, [VMEM] * blks, [wide], moved=1 * MIB)
        far, mate = to_far(own), to_mate(own)
        image = pltpu.VMEM((tall, LANES), FULL)
        near_inputs = [own, mate, pick, shift, adj, rhs]
        far_scratch = [
            pltpu.VMEM((elements + 8, 16, stride), HALF),
            pltpu.VMEM((elements, 8, LANES), FULL),
            image,
        ]
        (near,) = call(
            near_kernel,
            "near",
            near_inputs + [jac_blocks, in_hbm(block_inverse)],
            [VMEM] * 7 + [HBM],
            [adj_shape],
            [image],
            moved=12 * MIB,
        )
        (resid,) = call(
            far_kernel,
            "far",
            [near, far, jac_blocks, far_list, far_count, in_hbm(shape_partials), in_hbm(node_ids)],
            [VMEM] * 3 + [SMEM] * 2 + [HBM] * 2,
            [half_shape],
            far_scratch,
            moved=4 * MIB,
        )
        resids = [resid] + over_blk(resid, distances())
        if sweep < SWEEPS - 1:
            adj, half = call(
                update_kernel,
                "update",
                resids + [block_inverse, adj],
                [VMEM] * (blks + 2),
                [adj_shape, half_shape],
                scratch=[pltpu.VMEM((tall, LANES), FULL)],
                moved=8 * MIB,
            )
    deep = round_up(9 * blks, 16)
    adj, own, mate, far = call(
        gradient_kernel,
        "gradient",
        resids + [block_inverse, adj, shapes, low, target],
        [VMEM] * (blks + 5),
        [adj_shape] + [jax.ShapeDtypeStruct((deep, span), kind) for kind in (FULL, HALF, HALF)],
        scratch=[
            pltpu.VMEM((2 * tall, 3 * LANES), FULL),
            pltpu.VMEM((2 * 9 * 16, entries), HALF),
            pltpu.VMEM((-(-span // LANES), 9 * 16, LANES), FULL),
            pltpu.VMEM((tall, LANES), FULL),
        ],
    )
    far, mate = to_far(far), to_mate(mate)
    shapes = [jax.ShapeDtypeStruct((16, span), HALF)] * (blks - 1)
    pieces = call(
        combine_kernel, "combine", [own, mate, far], [VMEM] * 3, [jax.ShapeDtypeStruct((9, span), FULL)] + shapes
    )
    gradient = pieces[0]
    count = lax.axis_size("blk")
    for k in reversed(distances()):
        gradient = gradient + lax.ppermute(pieces[k], "blk", [(i, i ^ k) for i in range(count)])[:9].astype(FULL)
    adjoint = jnp.transpose(adj.reshape(sides, elements, width), (1, 0, 2))
    return (adjoint, gradient)


def solution(mesh):
    in_specs = (
        P("dom", None, "blk"),
        P("dom", None, "blk"),
        P("dom", None, "blk", None),
        P("dom", "blk", None),
        P("dom", None),
        P("dom"),
        P("dom", "blk", None),
        P("dom", None),
    )
    out_specs = (P("dom", None, "blk"), P(None, ("dom", "blk")))
    return jax.shard_map(local, mesh=mesh, in_specs=in_specs, out_specs=out_specs, check_vma=False)
```

```python
import functools

import jax
import jax.numpy as jnp
from jax import lax
from jax.experimental import pallas as pl
from jax.experimental.pallas import tpu as pltpu
from jax.sharding import PartitionSpec as P

SWEEPS = 2
NODE_DEV = 768
HALF = jnp.bfloat16
FULL = jnp.float32
LANES = 128
QUAD = 4
NT = (((1,), (1,)), ((), ()))
VMEM = pl.BlockSpec(memory_space=pltpu.VMEM)
SMEM = pl.BlockSpec(memory_space=pltpu.SMEM)
HBM = pl.BlockSpec(memory_space=pltpu.HBM)
GROUP = 60
MIB = 1024 * 1024


def round_up(size, unit):
    return -(-size // unit) * unit


def iota(shape, dim):
    return lax.broadcasted_iota(jnp.int32, shape, dim)


def hit(condition):
    return jnp.where(condition, 1.0, 0.0)


def in_hbm(array):
    return pltpu.with_memory_space_constraint(array, pltpu.HBM)


def call(kernel, name, args, specs, outs, scratch=(), limit=16, flops=0, moved=0, aliases=None):
    return pl.pallas_call(
        kernel,
        in_specs=specs,
        out_specs=[SMEM if getattr(out, "memory_space", None) is pltpu.SMEM else VMEM for out in outs],
        input_output_aliases=aliases or {},
        out_shape=outs,
        scratch_shapes=list(scratch),
        compiler_params=pltpu.CompilerParams(vmem_limit_bytes=limit * MIB),
        cost_estimate=pl.CostEstimate(flops=flops, bytes_accessed=moved, transcendentals=0),
        name=name,
    )(*args)


def distances():
    return list(range(1, lax.axis_size("blk")))


def over_blk(block, order):
    count = lax.axis_size("blk")
    return [lax.ppermute(block, "blk", [(i, i ^ k) for i in range(count)]) for k in order]


def to_mate(block):
    return lax.ppermute(block, "dom", [(i, i ^ 1) for i in range(lax.axis_size("dom"))])


def to_far(block):
    count = lax.axis_size("dom")
    return lax.ppermute(block, "dom", [(i, (((i + 1) ^ 1) - 1) % count) for i in range(count)])


def rounded(block, rows):
    short = rows - block.shape[0]
    if short:
        block = jnp.concatenate([block, jnp.zeros((short, block.shape[1]), block.dtype)], axis=0)
    return block.astype(HALF)


def window(ids, count):
    dom = lax.axis_index("dom")
    odd = lax.rem(dom, 2)
    place = ids - dom * count
    below = jnp.where(place < 0, 1, 0)
    above = jnp.where(place >= count, 1, 0)
    mate = odd * below + (1 - odd) * above
    return 2 * (below + above) - mate, place + (below - above) * count


def started(pairs, sems):
    copies = [pltpu.make_async_copy(source, target, sems.at[i]) for i, (source, target) in enumerate(pairs)]
    for copy in copies:
        copy.start()
    return copies


def slots_kernel(
    nb_hbm, shift_hbm, adj_hbm, rhs_hbm, _,
    pick_out, shift_out, list_out, count_out, adj_out, rhs_out, nb_ref, scalar_nb_ref, shift_ref, sems,
):
    pairs = [(nb_hbm, nb_ref), (shift_hbm, shift_ref), (adj_hbm, adj_out), (rhs_hbm, rhs_out)]
    copies = started(pairs + [(nb_hbm, scalar_nb_ref)], sems)
    copies[0].wait()
    copies[1].wait()
    copies[4].wait()
    list_far(scalar_nb_ref, list_out, count_out)
    faces, elements = nb_ref.shape
    rows_part = round_up(3 * elements, 16)
    part, inside = window(nb_ref[...], elements)
    bases = jnp.concatenate([iota((1, elements), 1), part * rows_part + inside], axis=0).astype(FULL)
    deep = elements * QUAD
    shape = (deep, elements)
    behind = iota(shape, 0) - QUAD * iota(shape, 1)
    owner = hit(jnp.logical_and(behind >= 0, behind < QUAD)).astype(HALF)
    columns = lax.dot_general(owner, bases.astype(HALF), NT, preferred_element_type=FULL)
    shape = (elements, QUAD, pick_out.shape[1])
    row, lane = iota(shape, 1).reshape(deep, -1), iota(shape, 2).reshape(deep, -1)
    offset = jnp.where(row < 3, lane - elements * row, -1).astype(FULL)
    for k in range(faces + 1):
        pick_out[k * deep : (k + 1) * deep, :] = hit(offset == columns[:, k : k + 1]).astype(HALF)
    shift_out[...] = jnp.zeros(shift_out.shape, FULL)
    for e in range(elements):
        shift_out[pl.ds(e, 3, stride=elements), :] = jnp.full((3, shift_out.shape[1]), shift_ref[e], FULL)
    for copy in (copies[2], copies[3]):
        copy.wait()


def list_far(nb_ref, list_out, count_out):
    faces, elements = nb_ref.shape

    count = jnp.int32(0)
    for e in range(elements):
        for k in range(1, faces + 1):
            part, inside = window(nb_ref[k - 1, e], elements)
            list_out[count] = (e * (faces + 1) + k) * 32 + inside
            count = count + lax.shift_right_logical(part, 1)
    for step in range(GROUP):
        list_out[count + step] = elements
    count_out[0] = lax.div(count + GROUP - 1, GROUP)


def nodes_kernel(ids_ref, shape_ref, low_out, target_out, shape_out):
    blk = lax.axis_index("blk")
    blks = lax.axis_size("blk")
    span = NODE_DEV // blks
    ids = ids_ref[...]
    pairs = ids.shape[0] // 2
    ids = [jnp.concatenate([ids[2 * p : 2 * p + 1], ids[2 * p + 1 : 2 * p + 2]], axis=1) for p in range(pairs)]
    part, inside = window(jnp.concatenate(ids, axis=0), NODE_DEV)
    owner = jnp.zeros_like(inside)
    for cut in range(1, blks):
        owner = owner + jnp.where(inside >= cut * span, 1, 0)
    low = inside - owner * span
    target_out[...] = part * blks + (owner ^ blk)
    shape = (span, LANES)
    for group in range(pairs):
        same = iota(shape, 0) == low[group : group + 1, :]
        low_out[:, group * LANES : (group + 1) * LANES] = hit(same).astype(HALF)

    elements, _, coords = shape_ref.shape
    nodes = coords // 3
    row, lane = iota((coords, coords), 0), iota((coords, coords), 1)
    axis = jnp.where(lane >= nodes, 1, 0) + jnp.where(lane >= 2 * nodes, 1, 0)
    sort = hit(row == 3 * (lane - axis * nodes) + axis).astype(HALF)
    for e in range(elements):
        shape_out[e] = jnp.dot(shape_ref[e], sort, preferred_element_type=FULL).astype(HALF)


def widened(block, lanes):
    short = lanes - block.shape[1]
    if short == 0:
        return block
    return jnp.concatenate([block, jnp.zeros((block.shape[0], short), block.dtype)], axis=1)


def laid(blocks, width, stride):
    lane = iota(blocks[0].shape, 1)
    tiles = [0.0] * (stride // LANES)
    for place, block in enumerate(blocks):
        tile, offset = divmod(place * width, LANES)
        if offset:
            block = pltpu.roll(block, offset, 1)
        if offset + width <= LANES:
            tiles[tile] = tiles[tile] + block
        else:
            tiles[tile] = tiles[tile] + jnp.where(lane >= offset, block, 0.0)
            tiles[tile + 1] = tiles[tile + 1] + jnp.where(lane < offset, block, 0.0)
    return tiles


def put_columns(blocks, order, stride):
    blk = lax.axis_index("blk")
    width = blocks[0].shape[1]
    blocks = [widened(block.astype(FULL), LANES) for block in blocks]
    placed = []
    for owner in range(len(blocks)):
        found = blocks[0]
        for k, block in zip(order, blocks[1:]):
            found = jnp.where((blk ^ owner) == k, block, found)
        placed.append(found)
    return laid(placed, width, stride)


def cut_of(rows, full):
    tail = full % LANES
    if tail == 0:
        return 0
    return round_up(rows // 2, 8) if tail <= LANES // 2 else rows


def packed_rows(rows, full):
    return round_up(full // LANES * rows + cut_of(rows, full), 16)


def columns_kernel(order, rows, full, *refs):
    *blocks, out_ref = refs
    tiles = put_columns([ref[...] for ref in blocks], order, round_up(full, LANES))
    cut = cut_of(rows, full)
    parts = [tile[:rows] for tile in tiles[: full // LANES]]
    if cut:
        last = tiles[-1][:cut]
        if cut < rows:
            lower = pltpu.roll(tiles[-1][cut:rows], LANES // 2, 1)
            last = last + jnp.concatenate([lower, jnp.zeros((2 * cut - rows, LANES), FULL)], axis=0)
        parts.append(last)
    out_ref[...] = rounded(jnp.concatenate(parts, axis=0), out_ref.shape[0])


def unpacked(ref, rows, full, last_tile=lambda tile: tile):
    block = ref[...].astype(FULL)
    whole, cut = full // LANES, cut_of(rows, full)
    tiles = [block[i * rows : (i + 1) * rows] for i in range(whole)]
    if cut:
        last = block[whole * rows : whole * rows + cut]
        if cut < rows:
            low = iota(last.shape, 1) < LANES // 2
            lower = pltpu.roll(jnp.where(low, 0.0, last), LANES // 2, 1)
            last = jnp.concatenate([jnp.where(low, last, 0.0), lower[: rows - cut]], axis=0)
        tiles.append(last_tile(last))
    return rounded(jnp.concatenate(tiles, axis=1), round_up(rows, 16))


def near_kernel(own_ref, mate_ref, pick_ref, shift_ref, adj_ref, rhs_ref, jac_ref, _, out_ref, image):
    rows, full = adj_ref.shape[0], jac_ref.shape[3]
    products([unpacked(ref, rows, full, twice) for ref in (own_ref, mate_ref)], pick_ref, jac_ref, image)
    out_ref[...] = without(shift_ref, adj_ref, rhs_ref, image)


def without(shift_ref, adj_ref, rhs_ref, image):
    rows, width = adj_ref.shape
    return rhs_ref[...] - (shift_ref[:rows, :width] * adj_ref[...] + image[:rows, :width])


def products(parts, pick_ref, jac_ref, image):
    elements, slots, width, full = jac_ref.shape
    rows_part, stride = parts[0].shape
    short = pick_ref.shape[1] - len(parts) * rows_part
    if short:
        parts = parts + [jnp.zeros((short, stride), HALF)]
    stacked = jnp.concatenate(parts, axis=0)
    picked = jnp.dot(pick_ref[...], stacked, preferred_element_type=FULL).astype(HALF)
    image[...] = jnp.zeros(image.shape, FULL)
    deep = full // (2 * LANES) * (2 * LANES)
    low = iota((4 * QUAD, LANES), 1) < LANES // 2
    for first in range(0, elements, 4):
        starts = [(k * elements + first) * QUAD for k in range(slots)]
        lefts = [picked[start : start + 4 * QUAD] for start in starts]
        tails = [left[:, deep:] for left in lefts]
        tails = [jnp.where(low, *tails[k : k + 2]) if k + 1 < slots else tails[k] for k in range(0, slots, 2)]
        left = jnp.concatenate([left[:, :deep] for left in lefts] + tails, axis=1)
        for i in range(4):
            e = first + i
            ends = [widened(jac_ref[e, k][:, deep:], LANES) for k in range(slots)]
            for k in range(1, slots, 2):
                ends[k - 1] = ends[k - 1] + pltpu.roll(ends[k], LANES // 2, 1)
            blocks = jnp.concatenate([jac_ref[e, k][:, :deep] for k in range(slots)] + ends[::2], axis=1)
            product = lax.dot_general(left, blocks, NT, preferred_element_type=FULL)
            image[pl.ds(e, 3, stride=elements), :width] = product[i * QUAD : i * QUAD + 3]


def twice(tail):
    return tail + pltpu.roll(tail, LANES // 2, 1)


def quad_products(lefts, blocks):
    full = blocks[0].shape[1]
    deep = full // (2 * LANES) * (2 * LANES)
    shape = (4 * QUAD, LANES)
    low = iota(shape, 1) < LANES // 2
    mine = []
    for i in range(4):
        place = iota(shape, 0) - i * QUAD
        mine.append(jnp.logical_and(jnp.logical_and(place >= 0, place < QUAD), low if i % 2 == 0 else jnp.logical_not(low)))
    tails = [left[:, deep : deep + LANES] for left in lefts]
    left = [jnp.where(mine[i], tails[i], jnp.where(mine[i + 1], tails[i + 1], 0.0).astype(HALF)) for i in (0, 2)]
    low = iota((blocks[0].shape[0], LANES), 1) < LANES // 2
    ends = [widened(block[:, deep:], LANES) for block in blocks]
    right = [jnp.where(low, ends[i], pltpu.roll(ends[i + 1], LANES // 2, 1)) for i in (0, 2)]
    shared = lax.dot_general(
        jnp.concatenate(left, axis=1), jnp.concatenate(right, axis=1), NT, preferred_element_type=FULL
    )
    products = []
    for i, (left, block) in enumerate(zip(lefts, blocks)):
        product = lax.dot_general(left[:, :deep], block[:, :deep], NT, preferred_element_type=FULL)
        part = slice(i * QUAD, (i + 1) * QUAD)
        products.append(product[part] + shared[part])
    return products


def far_kernel(near_ref, far_ref, jac_ref, list_ref, count_ref, _shapes, _ids, out_ref, spread, sums, image):
    elements, slots, width, _ = jac_ref.shape
    far = unpacked(far_ref, near_ref.shape[0], jac_ref.shape[3], twice)
    rows, stride = far.shape
    deep = spread.shape[1]
    shape = (elements, deep, rows)
    element, row, lane = [iota(shape, dim).reshape(elements * deep, rows) for dim in range(3)]
    row = lax.bitwise_and(row, QUAD - 1)
    pick = hit(jnp.where(row < 3, row * elements + element, -1) == lane).astype(HALF)
    taken = jnp.dot(pick, far, preferred_element_type=FULL).astype(HALF)
    spread[:elements] = taken.reshape(elements, deep, stride)
    spread[elements:] = jnp.zeros((spread.shape[0] - elements, deep, stride), HALF)
    sums[...] = jnp.zeros(sums.shape, FULL)

    @pl.loop(0, count_ref[0])
    def _(step):
        for i in range(0, GROUP, 4):
            owners, lefts, blocks = [], [], []
            for side in range(4):
                word = list_ref[step * GROUP + i + side]
                block = lax.shift_right_logical(word, 5)
                owners.append(lax.div(block, slots))
                lefts.append(spread[lax.bitwise_and(word, 31)])
                blocks.append(jac_ref[owners[side], block - owners[side] * slots])
            for e, product in zip(owners, quad_products(lefts, blocks)):
                sums[e, :QUAD, :width] += product

    for e in range(elements):
        image[pl.ds(e, 3, stride=elements), :] = sums[e, :3, :]
    real = near_ref.shape[0]
    out_ref[...] = rounded(near_ref[...] - image[:real, :width], out_ref.shape[0])


def element_of_row(shape, elements, copies=3):
    row = iota(shape, 0)
    for step in range(1, copies + 1):
        row = row - jnp.where(iota(shape, 0) >= step * elements, elements, 0)
    return row


def updated(resid_refs, inv_ref, adj_ref, update):
    rows, width = adj_ref.shape
    elements = rows // 3
    stride = round_up(inv_ref.shape[2], LANES)
    resid = put_columns([ref[...] for ref in resid_refs], distances(), stride)
    resid[-1] = twice(resid[-1])
    resid = jnp.concatenate(resid, axis=1).astype(HALF)
    shape = (elements, QUAD, resid.shape[0])
    deep = elements * QUAD
    element, row, lane = [iota(shape, dim).reshape(deep, -1) for dim in range(3)]
    pick = hit(jnp.where(row < 3, row * elements + element, -1) == lane).astype(HALF)
    resid = jnp.dot(pick, resid, preferred_element_type=FULL).astype(HALF)
    update[...] = jnp.zeros(update.shape, FULL)
    for first in range(0, elements, 4):
        left = resid[first * QUAD : (first + 4) * QUAD]
        for i, product in enumerate(quad_products([left] * 4, [inv_ref[first + i] for i in range(4)])):
            update[pl.ds(first + i, 3, stride=elements), :width] = product[:3]
    short = jnp.zeros((update.shape[0] - rows, width), FULL)
    return jnp.concatenate([adj_ref[...] + update[:rows, :width], short], axis=0)


def update_kernel(*refs):
    *resid_refs, inv_ref, adj_ref, adj_out, half_out, update = refs
    adj = updated(resid_refs, inv_ref, adj_ref, update)
    adj_out[...] = adj[: adj_out.shape[0]]
    half_out[...] = adj.astype(HALF)


def split(value):
    top = value.astype(HALF)
    return top, (value - top.astype(FULL)).astype(HALF)


def gradient_kernel(*refs):
    blks = lax.axis_size("blk")
    resid_refs = refs[:blks]
    inv_ref, adj_ref, shape_ref, low_ref, target_ref, adj_out = refs[blks : blks + 6]
    mate_out, far_out, sorted_ref, left_ref, sums_ref, update = refs[blks + 6 :]
    adj = updated(resid_refs, inv_ref, adj_ref, update)
    adj_out[...] = adj[: adj_out.shape[0]]
    half = adj.astype(HALF)
    elements = adj_out.shape[0] // 3
    pairs = elements // 2
    tall, width = half.shape
    coords = shape_ref.shape[2]
    depth = 3 if elements % 3 == 0 and 3 * width <= 256 else 1
    block = widened(half.astype(FULL), LANES)
    left = jnp.concatenate(laid([block] * depth, width, round_up(depth * width, LANES)), axis=1)[:, : depth * width]
    shape = left.shape
    owner = element_of_row(shape, elements)
    group = jnp.zeros(shape, jnp.int32)
    for step in range(1, elements // depth):
        group = group + jnp.where(owner >= step * depth, 1, 0)
    first = (owner - group * depth) * width
    behind = iota(shape, 1) - first
    left = jnp.where(jnp.logical_and(behind >= 0, behind < width), left, 0.0).astype(HALF)
    shape = (tall, coords)
    owner = element_of_row(shape, elements)
    total = jnp.zeros(shape, FULL)
    for start in range(0, elements, depth):
        partials = jnp.concatenate([shape_ref[start + step] for step in range(depth)], axis=0)
        product = jnp.dot(left, partials, preferred_element_type=FULL)
        total = jnp.where(owner >= start, product, total)
    low = iota((tall, LANES), 1) < LANES // 2
    odd = lax.bitwise_and(owner[:, :LANES], 1) == 1
    values = [total[:, :LANES], widened(total[:, LANES:], LANES)]
    turned = [pltpu.roll(value, LANES // 2, 1) for value in values]
    value = [
        jnp.where(odd, jnp.where(low, 0.0, turned[0]), jnp.where(low, values[0], 0.0)),
        jnp.where(odd, jnp.where(low, 0.0, values[0]), jnp.where(low, turned[0], 0.0)),
        jnp.where(odd, turned[1], values[1]),
    ]
    top, rest = split(jnp.concatenate(value, axis=1))
    sorted_ref[:tall] = top.astype(FULL)
    sorted_ref[tall:] = rest.astype(FULL)
    node_sums(sorted_ref, low_ref, target_ref, left_ref, sums_ref, blks)
    put_sums(mate_out, sums_ref, 0)
    put_sums(far_out, sums_ref, blks)


def own_sums_kernel(sorted_ref, low_ref, target_ref, out_ref, left_ref, sums_ref):
    node_sums(sorted_ref, low_ref, target_ref, left_ref, sums_ref, 0)
    put_sums(out_ref, sums_ref, 0)


def node_sums(sorted_ref, low_ref, target_ref, left_ref, sums_ref, first):
    deep = left_ref.shape[0] // 18
    tall = sorted_ref.shape[0] // 2
    pairs = target_ref.shape[0]
    for pair in range(pairs):
        lanes = slice(pair * LANES, (pair + 1) * LANES)
        mine = iota((deep, LANES), 0) + first == target_ref[pair : pair + 1, :]
        groups = []
        for part in range(2):
            for j in range(3):
                at = part * tall + 2 * (j * pairs + pair)
                for c in range(3):
                    axis = slice(c * LANES, (c + 1) * LANES)
                    values = sorted_ref[at : at + 1, axis] + sorted_ref[at + 1 : at + 2, axis]
                    groups.append(jnp.where(mine, values, 0.0))
        for i in range(0, 18, 2):
            both = jnp.concatenate(groups[i : i + 2], axis=0)
            left_ref[i * deep : (i + 2) * deep, lanes] = both.astype(HALF)
    sums = lax.dot_general(left_ref[...], low_ref[...], NT, preferred_element_type=FULL)
    span = low_ref.shape[0]
    sums = -(sums[: 9 * deep] + sums[9 * deep :])
    for tile in range(sums_ref.shape[0]):
        part = sums[:, tile * LANES : min(span, (tile + 1) * LANES)]
        sums_ref[tile, :, : part.shape[1]] = part


def put_sums(out_ref, sums_ref, first):
    blks = lax.axis_size("blk")
    deep = sums_ref.shape[1] // 9
    rows, span = out_ref.shape
    for tile in range(sums_ref.shape[0]):
        start, stop = tile * LANES, min(span, (tile + 1) * LANES)
        found = [sums_ref[tile, pl.ds(first + k, 9, stride=deep), :][:, : stop - start] for k in range(blks)]
        found = jnp.concatenate(found + [jnp.zeros((rows - 9 * blks, stop - start), FULL)], axis=0)
        out_ref[:, start:stop] = found.astype(out_ref.dtype)


def combine_kernel(own_ref, mate_ref, far_ref, *piece_outs):
    total = own_ref[...] + mate_ref[...].astype(FULL) + far_ref[...].astype(FULL)
    for k, out_ref in enumerate(piece_outs):
        piece = total[9 * k : 9 * (k + 1)]
        out_ref[...] = rounded(piece, 16) if k else piece


def local(
    adjoint_start,
    right_sides,
    jac_blocks,
    block_inverse,
    neighbours,
    pseudo_shift,
    shape_partials,
    node_ids,
):
    elements, sides, width = adjoint_start.shape
    slots, full = jac_blocks.shape[1], jac_blocks.shape[3]
    enodes = node_ids.shape[1]
    rows = sides * elements
    tall = round_up(rows, 16)
    stride = round_up(full, LANES)
    blks = lax.axis_size("blk")
    span = NODE_DEV // blks
    stacked = round_up(3 * tall, LANES)
    entries = elements * enodes

    adj_hbm = jnp.transpose(adjoint_start, (1, 0, 2)).reshape(rows, width)
    rhs = jnp.transpose(right_sides, (1, 0, 2)).reshape(rows, width)
    half_shape = jax.ShapeDtypeStruct((tall, width), HALF)

    adj_shape = jax.ShapeDtypeStruct((rows, width), FULL)
    pick, shift, far_list, far_count, adj, rhs = call(
        slots_kernel,
        "slots",
        [in_hbm(neighbours.T), in_hbm(pseudo_shift), in_hbm(adj_hbm), in_hbm(rhs), in_hbm(jac_blocks)],
        [HBM] * 5,
        [
            jax.ShapeDtypeStruct((slots * elements * QUAD, stacked), HALF),
            jax.ShapeDtypeStruct((tall, LANES), FULL),
            pltpu.SMEM((round_up(elements * (slots - 1) + GROUP, LANES),), jnp.int32),
            pltpu.SMEM((1,), jnp.int32),
            pltpu.VMEM((rows, width), FULL),
            pltpu.VMEM((rows, width), FULL),
        ],
        scratch=[
            pltpu.VMEM((slots - 1, elements), jnp.int32),
            pltpu.SMEM((slots - 1, elements), jnp.int32),
            pltpu.SMEM((elements,), FULL),
            pltpu.SemaphoreType.DMA((6,)),
        ],
        moved=16 * MIB,
    )
    low, target, shapes = call(
        nodes_kernel,
        "nodes",
        [node_ids, shape_partials],
        [VMEM, VMEM],
        [
            jax.ShapeDtypeStruct((span, entries), HALF),
            jax.ShapeDtypeStruct((entries // LANES, LANES), jnp.int32),
            jax.ShapeDtypeStruct(shape_partials.shape, HALF),
        ],
        moved=3 * MIB,
    )

    for sweep in range(SWEEPS):
        order = distances()
        blocks = [half] + over_blk(half, order) if sweep else [adj] + over_blk(adj_hbm, order)
        wide = jax.ShapeDtypeStruct((packed_rows(rows, full), LANES), HALF)
        (own,) = call(functools.partial(columns_kernel, order, rows, full), "columns", blocks, [VMEM] * blks, [wide], moved=1 * MIB)
        far, mate = to_far(own), to_mate(own)
        image = pltpu.VMEM((tall, LANES), FULL)
        near_inputs = [own, mate, pick, shift, adj, rhs]
        far_scratch = [
            pltpu.VMEM((elements + 8, 16, stride), HALF),
            pltpu.VMEM((elements, 8, LANES), FULL),
            image,
        ]
        (near,) = call(
            near_kernel,
            "near",
            near_inputs + [jac_blocks, in_hbm(block_inverse)],
            [VMEM] * 7 + [HBM],
            [adj_shape],
            [image],
            moved=12 * MIB,
        )
        (resid,) = call(
            far_kernel,
            "far",
            [near, far, jac_blocks, far_list, far_count, in_hbm(shape_partials), in_hbm(node_ids)],
            [VMEM] * 3 + [SMEM] * 2 + [HBM] * 2,
            [half_shape],
            far_scratch,
            moved=4 * MIB,
        )
        resids = [resid] + over_blk(resid, distances())
        if sweep < SWEEPS - 1:
            adj, half = call(
                update_kernel,
                "update",
                resids + [block_inverse, adj],
                [VMEM] * (blks + 2),
                [adj_shape, half_shape],
                scratch=[pltpu.VMEM((tall, LANES), FULL)],
                moved=8 * MIB,
            )
    deep = round_up(9 * blks, 16)
    part_shapes = [jax.ShapeDtypeStruct((deep, span), kind) for kind in (FULL, HALF)]
    sums_scratch = [
        pltpu.VMEM((18 * 2 * blks, entries), HALF),
        pltpu.VMEM((-(-span // LANES), 9 * 2 * blks, LANES), FULL),
    ]
    adj, mate, far, by_axis = call(
        gradient_kernel,
        "gradient",
        resids + [block_inverse, adj, shapes, low, target],
        [VMEM] * (blks + 5),
        [adj_shape, part_shapes[1], part_shapes[1], jax.ShapeDtypeStruct((2 * tall, 3 * LANES), FULL)],
        scratch=sums_scratch + [pltpu.VMEM((tall, LANES), FULL)],
    )
    (own,) = call(
        own_sums_kernel, "own_sums", [by_axis, low, target], [VMEM] * 3, part_shapes[:1], sums_scratch, moved=2 * MIB
    )
    far, mate = to_far(far), to_mate(mate)
    shapes = [jax.ShapeDtypeStruct((16, span), HALF)] * (blks - 1)
    pieces = call(
        combine_kernel, "combine", [own, mate, far], [VMEM] * 3, [jax.ShapeDtypeStruct((9, span), FULL)] + shapes
    )
    gradient = pieces[0]
    count = lax.axis_size("blk")
    for k in reversed(distances()):
        gradient = gradient + lax.ppermute(pieces[k], "blk", [(i, i ^ k) for i in range(count)])[:9].astype(FULL)
    adjoint = jnp.transpose(adj.reshape(sides, elements, width), (1, 0, 2))
    return (adjoint, gradient)


def solution(mesh):
    in_specs = (
        P("dom", None, "blk"),
        P("dom", None, "blk"),
        P("dom", None, "blk", None),
        P("dom", "blk", None),
        P("dom", None),
        P("dom"),
        P("dom", "blk", None),
        P("dom", None),
    )
    out_specs = (P("dom", None, "blk"), P(None, ("dom", "blk")))
    return jax.shard_map(local, mesh=mesh, in_specs=in_specs, out_specs=out_specs, check_vma=False)
```

```python
import functools
import math

import jax
import jax.numpy as jnp
from jax import lax
from jax.experimental import pallas as pl
from jax.experimental.pallas import tpu as pltpu
from jax.sharding import PartitionSpec as P

SWEEPS = 2
NODE_DEV = 768
HALF = jnp.bfloat16
FULL = jnp.float32
LANES = 128
QUAD = 4
NT = (((1,), (1,)), ((), ()))
VMEM = pl.BlockSpec(memory_space=pltpu.VMEM)
SMEM = pl.BlockSpec(memory_space=pltpu.SMEM)
HBM = pl.BlockSpec(memory_space=pltpu.HBM)
GROUP = 60
MIB = 1024 * 1024


def round_up(size, unit):
    return -(-size // unit) * unit


def iota(shape, dim):
    return lax.broadcasted_iota(jnp.int32, shape, dim)


def hit(condition):
    return jnp.where(condition, 1.0, 0.0)


def in_hbm(array):
    return pltpu.with_memory_space_constraint(array, pltpu.HBM)


def call(kernel, name, args, specs, outs, scratch=(), limit=16, flops=0, moved=0, aliases=None):
    return pl.pallas_call(
        kernel,
        in_specs=specs,
        out_specs=[SMEM if getattr(out, "memory_space", None) is pltpu.SMEM else VMEM for out in outs],
        input_output_aliases=aliases or {},
        out_shape=outs,
        scratch_shapes=list(scratch),
        compiler_params=pltpu.CompilerParams(vmem_limit_bytes=limit * MIB),
        cost_estimate=pl.CostEstimate(flops=flops, bytes_accessed=moved, transcendentals=0),
        name=name,
    )(*args)


def distances():
    return list(range(1, lax.axis_size("blk")))


def over_blk(block, order):
    count = lax.axis_size("blk")
    return [lax.ppermute(block, "blk", [(i, i ^ k) for i in range(count)]) for k in order]


def to_mate(block):
    return lax.ppermute(block, "dom", [(i, i ^ 1) for i in range(lax.axis_size("dom"))])


def to_far(block):
    count = lax.axis_size("dom")
    return lax.ppermute(block, "dom", [(i, (((i + 1) ^ 1) - 1) % count) for i in range(count)])


def rounded(block, rows):
    short = rows - block.shape[0]
    if short:
        block = jnp.concatenate([block, jnp.zeros((short, block.shape[1]), block.dtype)], axis=0)
    return block.astype(HALF)


def window(ids, count):
    dom = lax.axis_index("dom")
    odd = lax.rem(dom, 2)
    place = ids - dom * count
    below = jnp.where(place < 0, 1, 0)
    above = jnp.where(place >= count, 1, 0)
    mate = odd * below + (1 - odd) * above
    return 2 * (below + above) - mate, place + (below - above) * count


def started(pairs, sems):
    copies = [pltpu.make_async_copy(source, target, sems.at[i]) for i, (source, target) in enumerate(pairs)]
    for copy in copies:
        copy.start()
    return copies


def slots_kernel(
    nb_hbm, shift_hbm, adj_hbm, rhs_hbm, _,
    pick_out, shift_out, list_out, count_out, adj_out, rhs_out, nb_ref, scalar_nb_ref, shift_ref, sems,
):
    pairs = [(nb_hbm, nb_ref), (shift_hbm, shift_ref), (adj_hbm, adj_out), (rhs_hbm, rhs_out)]
    copies = started(pairs + [(nb_hbm, scalar_nb_ref)], sems)
    copies[0].wait()
    copies[1].wait()
    copies[4].wait()
    list_far(scalar_nb_ref, list_out, count_out)
    faces, elements = nb_ref.shape
    rows_part = round_up(3 * elements, 16)
    part, inside = window(nb_ref[...], elements)
    bases = jnp.concatenate([iota((1, elements), 1), part * rows_part + inside], axis=0).astype(FULL)
    deep = elements * QUAD
    shape = (deep, elements)
    behind = iota(shape, 0) - QUAD * iota(shape, 1)
    owner = hit(jnp.logical_and(behind >= 0, behind < QUAD)).astype(HALF)
    columns = lax.dot_general(owner, bases.astype(HALF), NT, preferred_element_type=FULL)
    shape = (elements, QUAD, pick_out.shape[1])
    row, lane = iota(shape, 1).reshape(deep, -1), iota(shape, 2).reshape(deep, -1)
    offset = jnp.where(row < 3, lane - elements * row, -1).astype(FULL)
    for k in range(faces + 1):
        pick_out[k * deep : (k + 1) * deep, :] = hit(offset == columns[:, k : k + 1]).astype(HALF)
    shift_out[...] = jnp.zeros(shift_out.shape, FULL)
    for e in range(elements):
        shift_out[pl.ds(e, 3, stride=elements), :] = jnp.full((3, shift_out.shape[1]), shift_ref[e], FULL)
    for copy in (copies[2], copies[3]):
        copy.wait()


def list_far(nb_ref, list_out, count_out):
    faces, elements = nb_ref.shape

    count = jnp.int32(0)
    for e in range(elements):
        for k in range(1, faces + 1):
            part, inside = window(nb_ref[k - 1, e], elements)
            list_out[count] = (e * (faces + 1) + k) * 32 + inside
            count = count + lax.shift_right_logical(part, 1)
    for step in range(GROUP):
        list_out[count + step] = elements
    count_out[0] = lax.div(count + GROUP - 1, GROUP)


def nodes_kernel(ids_ref, shape_ref, low_out, target_out, shape_out):
    blk = lax.axis_index("blk")
    blks = lax.axis_size("blk")
    span = NODE_DEV // blks
    ids = ids_ref[...]
    pairs = ids.shape[0] // 2
    ids = [jnp.concatenate([ids[2 * p : 2 * p + 1], ids[2 * p + 1 : 2 * p + 2]], axis=1) for p in range(pairs)]
    part, inside = window(jnp.concatenate(ids, axis=0), NODE_DEV)
    owner = jnp.zeros_like(inside)
    for cut in range(1, blks):
        owner = owner + jnp.where(inside >= cut * span, 1, 0)
    low = inside - owner * span
    target_out[...] = part * blks + (owner ^ blk)
    shape = (span, LANES)
    for group in range(pairs):
        same = iota(shape, 0) == low[group : group + 1, :]
        low_out[:, group * LANES : (group + 1) * LANES] = hit(same).astype(HALF)

    elements, _, coords = shape_ref.shape
    nodes = coords // 3
    row, lane = iota((coords, coords), 0), iota((coords, coords), 1)
    axis = jnp.where(lane >= nodes, 1, 0) + jnp.where(lane >= 2 * nodes, 1, 0)
    sort = hit(row == 3 * (lane - axis * nodes) + axis).astype(HALF)
    for e in range(elements):
        shape_out[e] = jnp.dot(shape_ref[e], sort, preferred_element_type=FULL).astype(HALF)


def widened(block, lanes):
    short = lanes - block.shape[1]
    if short == 0:
        return block
    return jnp.concatenate([block, jnp.zeros((block.shape[0], short), block.dtype)], axis=1)


def laid(blocks, width, stride):
    lane = iota(blocks[0].shape, 1)
    tiles = [0.0] * (stride // LANES)
    for place, block in enumerate(blocks):
        tile, offset = divmod(place * width, LANES)
        if offset:
            block = pltpu.roll(block, offset, 1)
        if offset + width <= LANES:
            tiles[tile] = tiles[tile] + block
        else:
            tiles[tile] = tiles[tile] + jnp.where(lane >= offset, block, 0.0)
            tiles[tile + 1] = tiles[tile + 1] + jnp.where(lane < offset, block, 0.0)
    return tiles


def put_columns(blocks, order, stride):
    blk = lax.axis_index("blk")
    width = blocks[0].shape[1]
    blocks = [widened(block.astype(FULL), LANES) for block in blocks]
    placed = []
    for owner in range(len(blocks)):
        found = blocks[0]
        for k, block in zip(order, blocks[1:]):
            found = jnp.where((blk ^ owner) == k, block, found)
        placed.append(found)
    return laid(placed, width, stride)


def cut_of(rows, full):
    tail = full % LANES
    if tail == 0:
        return 0
    return round_up(rows // 2, 8) if tail <= LANES // 2 else rows


def packed_rows(rows, full):
    return round_up(full // LANES * rows + cut_of(rows, full), 16)


def columns_kernel(order, rows, full, *refs):
    *blocks, out_ref = refs
    tiles = put_columns([ref[...] for ref in blocks], order, round_up(full, LANES))
    cut = cut_of(rows, full)
    parts = [tile[:rows] for tile in tiles[: full // LANES]]
    if cut:
        last = tiles[-1][:cut]
        if cut < rows:
            lower = pltpu.roll(tiles[-1][cut:rows], LANES // 2, 1)
            last = last + jnp.concatenate([lower, jnp.zeros((2 * cut - rows, LANES), FULL)], axis=0)
        parts.append(last)
    out_ref[...] = rounded(jnp.concatenate(parts, axis=0), out_ref.shape[0])


def unpacked(ref, rows, full, last_tile=lambda tile: tile):
    block = ref[...].astype(FULL)
    whole, cut = full // LANES, cut_of(rows, full)
    tiles = [block[i * rows : (i + 1) * rows] for i in range(whole)]
    if cut:
        last = block[whole * rows : whole * rows + cut]
        if cut < rows:
            low = iota(last.shape, 1) < LANES // 2
            lower = pltpu.roll(jnp.where(low, 0.0, last), LANES // 2, 1)
            last = jnp.concatenate([jnp.where(low, last, 0.0), lower[: rows - cut]], axis=0)
        tiles.append(last_tile(last))
    return rounded(jnp.concatenate(tiles, axis=1), round_up(rows, 16))


def near_kernel(own_ref, mate_ref, pick_ref, shift_ref, adj_ref, rhs_ref, jac_ref, _, out_ref, image):
    rows, full = adj_ref.shape[0], jac_ref.shape[3]
    products([unpacked(ref, rows, full, twice) for ref in (own_ref, mate_ref)], pick_ref, jac_ref, image)
    out_ref[...] = without(shift_ref, adj_ref, rhs_ref, image)


def without(shift_ref, adj_ref, rhs_ref, image):
    rows, width = adj_ref.shape
    return rhs_ref[...] - (shift_ref[:rows, :width] * adj_ref[...] + image[:rows, :width])


def products(parts, pick_ref, jac_ref, image):
    elements, slots, width, full = jac_ref.shape
    rows_part, stride = parts[0].shape
    short = pick_ref.shape[1] - len(parts) * rows_part
    if short:
        parts = parts + [jnp.zeros((short, stride), HALF)]
    stacked = jnp.concatenate(parts, axis=0)
    picked = jnp.dot(pick_ref[...], stacked, preferred_element_type=FULL).astype(HALF)
    image[...] = jnp.zeros(image.shape, FULL)
    deep = full // (2 * LANES) * (2 * LANES)
    low = iota((4 * QUAD, LANES), 1) < LANES // 2
    for first in range(0, elements, 4):
        starts = [(k * elements + first) * QUAD for k in range(slots)]
        lefts = [picked[start : start + 4 * QUAD] for start in starts]
        tails = [left[:, deep:] for left in lefts]
        tails = [jnp.where(low, *tails[k : k + 2]) if k + 1 < slots else tails[k] for k in range(0, slots, 2)]
        left = jnp.concatenate([left[:, :deep] for left in lefts] + tails, axis=1)
        for i in range(4):
            e = first + i
            ends = [widened(jac_ref[e, k][:, deep:], LANES) for k in range(slots)]
            for k in range(1, slots, 2):
                ends[k - 1] = ends[k - 1] + pltpu.roll(ends[k], LANES // 2, 1)
            blocks = jnp.concatenate([jac_ref[e, k][:, :deep] for k in range(slots)] + ends[::2], axis=1)
            product = lax.dot_general(left, blocks, NT, preferred_element_type=FULL)
            image[pl.ds(e, 3, stride=elements), :width] = product[i * QUAD : i * QUAD + 3]


def twice(tail):
    return tail + pltpu.roll(tail, LANES // 2, 1)


def quad_products(lefts, blocks):
    full = blocks[0].shape[1]
    deep = full // (2 * LANES) * (2 * LANES)
    shape = (4 * QUAD, LANES)
    low = iota(shape, 1) < LANES // 2
    mine = []
    for i in range(4):
        place = iota(shape, 0) - i * QUAD
        mine.append(jnp.logical_and(jnp.logical_and(place >= 0, place < QUAD), low if i % 2 == 0 else jnp.logical_not(low)))
    tails = [left[:, deep : deep + LANES] for left in lefts]
    left = [jnp.where(mine[i], tails[i], jnp.where(mine[i + 1], tails[i + 1], 0.0).astype(HALF)) for i in (0, 2)]
    low = iota((blocks[0].shape[0], LANES), 1) < LANES // 2
    ends = [widened(block[:, deep:], LANES) for block in blocks]
    right = [jnp.where(low, ends[i], pltpu.roll(ends[i + 1], LANES // 2, 1)) for i in (0, 2)]
    shared = lax.dot_general(
        jnp.concatenate(left, axis=1), jnp.concatenate(right, axis=1), NT, preferred_element_type=FULL
    )
    products = []
    for i, (left, block) in enumerate(zip(lefts, blocks)):
        product = lax.dot_general(left[:, :deep], block[:, :deep], NT, preferred_element_type=FULL)
        part = slice(i * QUAD, (i + 1) * QUAD)
        products.append(product[part] + shared[part])
    return products


def far_kernel(near_ref, far_ref, jac_ref, list_ref, count_ref, _shapes, _ids, out_ref, spread, sums, image):
    elements, slots, width, _ = jac_ref.shape
    far = unpacked(far_ref, near_ref.shape[0], jac_ref.shape[3], twice)
    rows, stride = far.shape
    deep = spread.shape[1]
    shape = (elements, deep, rows)
    element, row, lane = [iota(shape, dim).reshape(elements * deep, rows) for dim in range(3)]
    row = lax.bitwise_and(row, QUAD - 1)
    pick = hit(jnp.where(row < 3, row * elements + element, -1) == lane).astype(HALF)
    taken = jnp.dot(pick, far, preferred_element_type=FULL).astype(HALF)
    spread[:elements] = taken.reshape(elements, deep, stride)
    spread[elements:] = jnp.zeros((spread.shape[0] - elements, deep, stride), HALF)
    sums[...] = jnp.zeros(sums.shape, FULL)

    @pl.loop(0, count_ref[0])
    def _(step):
        for i in range(0, GROUP, 4):
            owners, lefts, blocks = [], [], []
            for side in range(4):
                word = list_ref[step * GROUP + i + side]
                block = lax.shift_right_logical(word, 5)
                owners.append(lax.div(block, slots))
                lefts.append(spread[lax.bitwise_and(word, 31)])
                blocks.append(jac_ref[owners[side], block - owners[side] * slots])
            for e, product in zip(owners, quad_products(lefts, blocks)):
                sums[e, :QUAD, :width] += product

    for e in range(elements):
        image[pl.ds(e, 3, stride=elements), :] = sums[e, :3, :]
    real = near_ref.shape[0]
    out_ref[...] = rounded(near_ref[...] - image[:real, :width], out_ref.shape[0])


def element_of_row(shape, elements, copies=3):
    row = iota(shape, 0)
    for step in range(1, copies + 1):
        row = row - jnp.where(iota(shape, 0) >= step * elements, elements, 0)
    return row


def updated(resid_refs, inv_ref, adj_ref, update):
    rows, width = adj_ref.shape
    elements = rows // 3
    stride = round_up(inv_ref.shape[2], LANES)
    resid = put_columns([ref[...] for ref in resid_refs], distances(), stride)
    resid[-1] = twice(resid[-1])
    resid = jnp.concatenate(resid, axis=1).astype(HALF)
    shape = (elements, QUAD, resid.shape[0])
    deep = elements * QUAD
    element, row, lane = [iota(shape, dim).reshape(deep, -1) for dim in range(3)]
    pick = hit(jnp.where(row < 3, row * elements + element, -1) == lane).astype(HALF)
    resid = jnp.dot(pick, resid, preferred_element_type=FULL).astype(HALF)
    update[...] = jnp.zeros(update.shape, FULL)
    for first in range(0, elements, 4):
        left = resid[first * QUAD : (first + 4) * QUAD]
        for i, product in enumerate(quad_products([left] * 4, [inv_ref[first + i] for i in range(4)])):
            update[pl.ds(first + i, 3, stride=elements), :width] = product[:3]
    short = jnp.zeros((update.shape[0] - rows, width), FULL)
    return jnp.concatenate([adj_ref[...] + update[:rows, :width], short], axis=0)


def update_kernel(*refs):
    *resid_refs, inv_ref, adj_ref, adj_out, half_out, update = refs
    adj = updated(resid_refs, inv_ref, adj_ref, update)
    adj_out[...] = adj[: adj_out.shape[0]]
    half_out[...] = adj.astype(HALF)


def split(value):
    top = value.astype(HALF)
    return top, (value - top.astype(FULL)).astype(HALF)


def gradient_kernel(*refs):
    blks = lax.axis_size("blk")
    resid_refs = refs[:blks]
    inv_ref, adj_ref, shape_ref, low_ref, target_ref, adj_out = refs[blks : blks + 6]
    mate_out, far_out, sorted_ref, left_ref, sums_ref, update = refs[blks + 6 :]
    adj = updated(resid_refs, inv_ref, adj_ref, update)
    adj_out[...] = adj[: adj_out.shape[0]]
    half = adj.astype(HALF)
    elements = adj_out.shape[0] // 3
    pairs = elements // 2
    tall, width = half.shape
    coords = shape_ref.shape[2]
    period = math.lcm(width, LANES) // width
    if elements % period:
        period = elements
    block = widened(half.astype(FULL), LANES)
    tiles = laid([block] * period, width, round_up(period * width, LANES))
    left = jnp.concatenate(tiles * (elements // period), axis=1)[:, : elements * width]
    behind = iota(left.shape, 1) - width * element_of_row(left.shape, elements)
    left = jnp.where(jnp.logical_and(behind >= 0, behind < width), left, 0.0).astype(HALF)
    total = jnp.dot(left, shape_ref[...].reshape(elements * width, coords), preferred_element_type=FULL)
    owner = element_of_row(total.shape, elements)
    low = iota((tall, LANES), 1) < LANES // 2
    odd = lax.bitwise_and(owner[:, :LANES], 1) == 1
    values = [total[:, :LANES], widened(total[:, LANES:], LANES)]
    turned = [pltpu.roll(value, LANES // 2, 1) for value in values]
    value = [
        jnp.where(odd, jnp.where(low, 0.0, turned[0]), jnp.where(low, values[0], 0.0)),
        jnp.where(odd, jnp.where(low, 0.0, values[0]), jnp.where(low, turned[0], 0.0)),
        jnp.where(odd, turned[1], values[1]),
    ]
    top, rest = split(jnp.concatenate(value, axis=1))
    sorted_ref[:tall] = top.astype(FULL)
    sorted_ref[tall:] = rest.astype(FULL)
    node_sums(sorted_ref, low_ref, target_ref, left_ref, sums_ref, blks)
    put_sums(mate_out, sums_ref, 0)
    put_sums(far_out, sums_ref, blks)


def own_sums_kernel(sorted_ref, low_ref, target_ref, out_ref, left_ref, sums_ref):
    node_sums(sorted_ref, low_ref, target_ref, left_ref, sums_ref, 0)
    put_sums(out_ref, sums_ref, 0)


def node_sums(sorted_ref, low_ref, target_ref, left_ref, sums_ref, first):
    deep = left_ref.shape[0] // 18
    tall = sorted_ref.shape[0] // 2
    pairs = target_ref.shape[0]
    for pair in range(pairs):
        lanes = slice(pair * LANES, (pair + 1) * LANES)
        mine = iota((deep, LANES), 0) + first == target_ref[pair : pair + 1, :]
        groups = []
        for part in range(2):
            for j in range(3):
                at = part * tall + 2 * (j * pairs + pair)
                for c in range(3):
                    axis = slice(c * LANES, (c + 1) * LANES)
                    values = sorted_ref[at : at + 1, axis] + sorted_ref[at + 1 : at + 2, axis]
                    groups.append(jnp.where(mine, values, 0.0))
        for i in range(0, 18, 2):
            both = jnp.concatenate(groups[i : i + 2], axis=0)
            left_ref[i * deep : (i + 2) * deep, lanes] = both.astype(HALF)
    sums = lax.dot_general(left_ref[...], low_ref[...], NT, preferred_element_type=FULL)
    span = low_ref.shape[0]
    sums = -(sums[: 9 * deep] + sums[9 * deep :])
    for tile in range(sums_ref.shape[0]):
        part = sums[:, tile * LANES : min(span, (tile + 1) * LANES)]
        sums_ref[tile, :, : part.shape[1]] = part


def put_sums(out_ref, sums_ref, first):
    blks = lax.axis_size("blk")
    deep = sums_ref.shape[1] // 9
    rows, span = out_ref.shape
    for tile in range(sums_ref.shape[0]):
        start, stop = tile * LANES, min(span, (tile + 1) * LANES)
        found = [sums_ref[tile, pl.ds(first + k, 9, stride=deep), :][:, : stop - start] for k in range(blks)]
        found = jnp.concatenate(found + [jnp.zeros((rows - 9 * blks, stop - start), FULL)], axis=0)
        out_ref[:, start:stop] = found.astype(out_ref.dtype)


def combine_kernel(own_ref, mate_ref, far_ref, *piece_outs):
    total = own_ref[...] + mate_ref[...].astype(FULL) + far_ref[...].astype(FULL)
    for k, out_ref in enumerate(piece_outs):
        piece = total[9 * k : 9 * (k + 1)]
        out_ref[...] = rounded(piece, 16) if k else piece


def local(
    adjoint_start,
    right_sides,
    jac_blocks,
    block_inverse,
    neighbours,
    pseudo_shift,
    shape_partials,
    node_ids,
):
    elements, sides, width = adjoint_start.shape
    slots, full = jac_blocks.shape[1], jac_blocks.shape[3]
    enodes = node_ids.shape[1]
    rows = sides * elements
    tall = round_up(rows, 16)
    stride = round_up(full, LANES)
    blks = lax.axis_size("blk")
    span = NODE_DEV // blks
    stacked = round_up(3 * tall, LANES)
    entries = elements * enodes

    adj_hbm = jnp.transpose(adjoint_start, (1, 0, 2)).reshape(rows, width)
    rhs = jnp.transpose(right_sides, (1, 0, 2)).reshape(rows, width)
    half_shape = jax.ShapeDtypeStruct((tall, width), HALF)

    adj_shape = jax.ShapeDtypeStruct((rows, width), FULL)
    pick, shift, far_list, far_count, adj, rhs = call(
        slots_kernel,
        "slots",
        [in_hbm(neighbours.T), in_hbm(pseudo_shift), in_hbm(adj_hbm), in_hbm(rhs), in_hbm(jac_blocks)],
        [HBM] * 5,
        [
            jax.ShapeDtypeStruct((slots * elements * QUAD, stacked), HALF),
            jax.ShapeDtypeStruct((tall, LANES), FULL),
            pltpu.SMEM((round_up(elements * (slots - 1) + GROUP, LANES),), jnp.int32),
            pltpu.SMEM((1,), jnp.int32),
            pltpu.VMEM((rows, width), FULL),
            pltpu.VMEM((rows, width), FULL),
        ],
        scratch=[
            pltpu.VMEM((slots - 1, elements), jnp.int32),
            pltpu.SMEM((slots - 1, elements), jnp.int32),
            pltpu.SMEM((elements,), FULL),
            pltpu.SemaphoreType.DMA((6,)),
        ],
        moved=16 * MIB,
    )
    low, target, shapes = call(
        nodes_kernel,
        "nodes",
        [node_ids, shape_partials],
        [VMEM, VMEM],
        [
            jax.ShapeDtypeStruct((span, entries), HALF),
            jax.ShapeDtypeStruct((entries // LANES, LANES), jnp.int32),
            jax.ShapeDtypeStruct(shape_partials.shape, HALF),
        ],
        moved=3 * MIB,
    )

    for sweep in range(SWEEPS):
        order = distances()
        blocks = [half] + over_blk(half, order) if sweep else [adj] + over_blk(adj_hbm, order)
        wide = jax.ShapeDtypeStruct((packed_rows(rows, full), LANES), HALF)
        (own,) = call(functools.partial(columns_kernel, order, rows, full), "columns", blocks, [VMEM] * blks, [wide], moved=1 * MIB)
        far, mate = to_far(own), to_mate(own)
        image = pltpu.VMEM((tall, LANES), FULL)
        near_inputs = [own, mate, pick, shift, adj, rhs]
        far_scratch = [
            pltpu.VMEM((elements + 8, 16, stride), HALF),
            pltpu.VMEM((elements, 8, LANES), FULL),
            image,
        ]
        (near,) = call(
            near_kernel,
            "near",
            near_inputs + [jac_blocks, in_hbm(block_inverse)],
            [VMEM] * 7 + [HBM],
            [adj_shape],
            [image],
            moved=12 * MIB,
        )
        (resid,) = call(
            far_kernel,
            "far",
            [near, far, jac_blocks, far_list, far_count, in_hbm(shape_partials), in_hbm(node_ids)],
            [VMEM] * 3 + [SMEM] * 2 + [HBM] * 2,
            [half_shape],
            far_scratch,
            moved=4 * MIB,
        )
        resids = [resid] + over_blk(resid, distances())
        if sweep < SWEEPS - 1:
            adj, half = call(
                update_kernel,
                "update",
                resids + [block_inverse, adj],
                [VMEM] * (blks + 2),
                [adj_shape, half_shape],
                scratch=[pltpu.VMEM((tall, LANES), FULL)],
                moved=8 * MIB,
            )
    deep = round_up(9 * blks, 16)
    part_shapes = [jax.ShapeDtypeStruct((deep, span), kind) for kind in (FULL, HALF)]
    sums_scratch = [
        pltpu.VMEM((18 * 2 * blks, entries), HALF),
        pltpu.VMEM((-(-span // LANES), 9 * 2 * blks, LANES), FULL),
    ]
    adj, mate, far, by_axis = call(
        gradient_kernel,
        "gradient",
        resids + [block_inverse, adj, shapes, low, target],
        [VMEM] * (blks + 5),
        [adj_shape, part_shapes[1], part_shapes[1], jax.ShapeDtypeStruct((2 * tall, 3 * LANES), FULL)],
        scratch=sums_scratch + [pltpu.VMEM((tall, LANES), FULL)],
    )
    (own,) = call(
        own_sums_kernel, "own_sums", [by_axis, low, target], [VMEM] * 3, part_shapes[:1], sums_scratch, moved=2 * MIB
    )
    far, mate = to_far(far), to_mate(mate)
    shapes = [jax.ShapeDtypeStruct((16, span), HALF)] * (blks - 1)
    pieces = call(
        combine_kernel, "combine", [own, mate, far], [VMEM] * 3, [jax.ShapeDtypeStruct((9, span), FULL)] + shapes
    )
    gradient = pieces[0]
    count = lax.axis_size("blk")
    for k in reversed(distances()):
        gradient = gradient + lax.ppermute(pieces[k], "blk", [(i, i ^ k) for i in range(count)])[:9].astype(FULL)
    adjoint = jnp.transpose(adj.reshape(sides, elements, width), (1, 0, 2))
    return (adjoint, gradient)


def solution(mesh):
    in_specs = (
        P("dom", None, "blk"),
        P("dom", None, "blk"),
        P("dom", None, "blk", None),
        P("dom", "blk", None),
        P("dom", None),
        P("dom"),
        P("dom", "blk", None),
        P("dom", None),
    )
    out_specs = (P("dom", None, "blk"), P(None, ("dom", "blk")))
    return jax.shard_map(local, mesh=mesh, in_specs=in_specs, out_specs=out_specs, check_vma=False)
```

```python
import functools

import jax
import jax.numpy as jnp
from jax import lax
from jax.experimental import pallas as pl
from jax.experimental.pallas import tpu as pltpu
from jax.sharding import PartitionSpec as P

SWEEPS = 2
NODE_DEV = 768
HALF = jnp.bfloat16
FULL = jnp.float32
LANES = 128
QUAD = 4
NT = (((1,), (1,)), ((), ()))
VMEM = pl.BlockSpec(memory_space=pltpu.VMEM)
SMEM = pl.BlockSpec(memory_space=pltpu.SMEM)
HBM = pl.BlockSpec(memory_space=pltpu.HBM)
GROUP = 64
MIB = 1024 * 1024


def round_up(size, unit):
    return -(-size // unit) * unit


def iota(shape, dim):
    return lax.broadcasted_iota(jnp.int32, shape, dim)


def hit(condition):
    return jnp.where(condition, 1.0, 0.0)


def in_hbm(array):
    return pltpu.with_memory_space_constraint(array, pltpu.HBM)


def call(kernel, name, args, specs, outs, scratch=(), limit=16, flops=0, moved=0, aliases=None):
    return pl.pallas_call(
        kernel,
        in_specs=specs,
        out_specs=[SMEM if getattr(out, "memory_space", None) is pltpu.SMEM else VMEM for out in outs],
        input_output_aliases=aliases or {},
        out_shape=outs,
        scratch_shapes=list(scratch),
        compiler_params=pltpu.CompilerParams(vmem_limit_bytes=limit * MIB),
        cost_estimate=pl.CostEstimate(flops=flops, bytes_accessed=moved, transcendentals=0),
        name=name,
    )(*args)


def distances():
    return list(range(1, lax.axis_size("blk")))


def over_blk(block, order):
    count = lax.axis_size("blk")
    return [lax.ppermute(block, "blk", [(i, i ^ k) for i in range(count)]) for k in order]


def to_mate(block):
    return lax.ppermute(block, "dom", [(i, i ^ 1) for i in range(lax.axis_size("dom"))])


def to_far(block):
    count = lax.axis_size("dom")
    return lax.ppermute(block, "dom", [(i, (((i + 1) ^ 1) - 1) % count) for i in range(count)])


def rounded(block, rows):
    short = rows - block.shape[0]
    if short:
        block = jnp.concatenate([block, jnp.zeros((short, block.shape[1]), block.dtype)], axis=0)
    return block.astype(HALF)


def window(ids, count):
    dom = lax.axis_index("dom")
    odd = lax.rem(dom, 2)
    place = ids - dom * count
    below = jnp.where(place < 0, 1, 0)
    above = jnp.where(place >= count, 1, 0)
    mate = odd * below + (1 - odd) * above
    return 2 * (below + above) - mate, place + (below - above) * count


def started(pairs, sems):
    copies = [pltpu.make_async_copy(source, target, sems.at[i]) for i, (source, target) in enumerate(pairs)]
    for copy in copies:
        copy.start()
    return copies


def slots_kernel(
    nb_hbm, shift_hbm, adj_hbm, rhs_hbm, _,
    pick_out, shift_out, list_out, count_out, adj_out, rhs_out, nb_ref, scalar_nb_ref, shift_ref, sems,
):
    pairs = [(nb_hbm, nb_ref), (shift_hbm, shift_ref), (adj_hbm, adj_out), (rhs_hbm, rhs_out)]
    copies = started(pairs + [(nb_hbm, scalar_nb_ref)], sems)
    copies[0].wait()
    copies[1].wait()
    copies[4].wait()
    list_far(scalar_nb_ref, list_out, count_out)
    faces, elements = nb_ref.shape
    rows_part = round_up(3 * elements, 16)
    part, inside = window(nb_ref[...], elements)
    bases = jnp.concatenate([iota((1, elements), 1), part * rows_part + inside], axis=0).astype(FULL)
    deep = elements * QUAD
    shape = (deep, elements)
    behind = iota(shape, 0) - QUAD * iota(shape, 1)
    owner = hit(jnp.logical_and(behind >= 0, behind < QUAD)).astype(HALF)
    columns = lax.dot_general(owner, bases.astype(HALF), NT, preferred_element_type=FULL)
    shape = (elements, QUAD, pick_out.shape[1])
    row, lane = iota(shape, 1).reshape(deep, -1), iota(shape, 2).reshape(deep, -1)
    offset = jnp.where(row < 3, lane - elements * row, -1).astype(FULL)
    for k in range(faces + 1):
        pick_out[k * deep : (k + 1) * deep, :] = hit(offset == columns[:, k : k + 1]).astype(HALF)
    shift_out[...] = jnp.zeros(shift_out.shape, FULL)
    for e in range(elements):
        shift_out[pl.ds(e, 3, stride=elements), :] = jnp.full((3, shift_out.shape[1]), shift_ref[e], FULL)
    for copy in (copies[2], copies[3]):
        copy.wait()


def list_far(nb_ref, list_out, count_out):
    faces, elements = nb_ref.shape

    count = jnp.int32(0)
    for e in range(elements):
        for k in range(1, faces + 1):
            part, inside = window(nb_ref[k - 1, e], elements)
            list_out[count] = (e * (faces + 1) + k) * 32 + inside
            count = count + lax.shift_right_logical(part, 1)
    for step in range(GROUP):
        list_out[count + step] = elements
    count_out[0] = lax.div(count + GROUP - 1, GROUP)


def nodes_kernel(ids_ref, shape_ref, low_out, target_out, shape_out):
    blk = lax.axis_index("blk")
    blks = lax.axis_size("blk")
    span = NODE_DEV // blks
    ids = ids_ref[...]
    pairs = ids.shape[0] // 2
    ids = [jnp.concatenate([ids[2 * p : 2 * p + 1], ids[2 * p + 1 : 2 * p + 2]], axis=1) for p in range(pairs)]
    part, inside = window(jnp.concatenate(ids, axis=0), NODE_DEV)
    owner = jnp.zeros_like(inside)
    for cut in range(1, blks):
        owner = owner + jnp.where(inside >= cut * span, 1, 0)
    low = inside - owner * span
    target_out[...] = part * blks + (owner ^ blk)
    shape = (span, LANES)
    for group in range(pairs):
        same = iota(shape, 0) == low[group : group + 1, :]
        low_out[:, group * LANES : (group + 1) * LANES] = hit(same).astype(HALF)

    elements, _, coords = shape_ref.shape
    nodes = coords // 3
    row, lane = iota((coords, coords), 0), iota((coords, coords), 1)
    axis = jnp.where(lane >= nodes, 1, 0) + jnp.where(lane >= 2 * nodes, 1, 0)
    sort = hit(row == 3 * (lane - axis * nodes) + axis).astype(HALF)
    for e in range(elements):
        shape_out[e] = jnp.dot(shape_ref[e], sort, preferred_element_type=FULL).astype(HALF)


def widened(block, lanes):
    short = lanes - block.shape[1]
    if short == 0:
        return block
    return jnp.concatenate([block, jnp.zeros((block.shape[0], short), block.dtype)], axis=1)


def laid(blocks, width, stride):
    lane = iota(blocks[0].shape, 1)
    tiles = [0.0] * (stride // LANES)
    for place, block in enumerate(blocks):
        tile, offset = divmod(place * width, LANES)
        if offset:
            block = pltpu.roll(block, offset, 1)
        if offset + width <= LANES:
            tiles[tile] = tiles[tile] + block
        else:
            tiles[tile] = tiles[tile] + jnp.where(lane >= offset, block, 0.0)
            tiles[tile + 1] = tiles[tile + 1] + jnp.where(lane < offset, block, 0.0)
    return tiles


def put_columns(blocks, order, stride):
    blk = lax.axis_index("blk")
    width = blocks[0].shape[1]
    blocks = [widened(block.astype(FULL), LANES) for block in blocks]
    placed = []
    for owner in range(len(blocks)):
        found = blocks[0]
        for k, block in zip(order, blocks[1:]):
            found = jnp.where((blk ^ owner) == k, block, found)
        placed.append(found)
    return laid(placed, width, stride)


def cut_of(rows, full):
    tail = full % LANES
    if tail == 0:
        return 0
    return round_up(rows // 2, 8) if tail <= LANES // 2 else rows


def packed_rows(rows, full):
    return round_up(full // LANES * rows + cut_of(rows, full), 16)


def columns_kernel(order, rows, full, *refs):
    *blocks, out_ref = refs
    tiles = put_columns([ref[...] for ref in blocks], order, round_up(full, LANES))
    cut = cut_of(rows, full)
    parts = [tile[:rows] for tile in tiles[: full // LANES]]
    if cut:
        last = tiles[-1][:cut]
        if cut < rows:
            lower = pltpu.roll(tiles[-1][cut:rows], LANES // 2, 1)
            last = last + jnp.concatenate([lower, jnp.zeros((2 * cut - rows, LANES), FULL)], axis=0)
        parts.append(last)
    out_ref[...] = rounded(jnp.concatenate(parts, axis=0), out_ref.shape[0])


def unpacked(ref, rows, full, last_tile=lambda tile: tile):
    block = ref[...].astype(FULL)
    whole, cut = full // LANES, cut_of(rows, full)
    tiles = [block[i * rows : (i + 1) * rows] for i in range(whole)]
    if cut:
        last = block[whole * rows : whole * rows + cut]
        if cut < rows:
            low = iota(last.shape, 1) < LANES // 2
            lower = pltpu.roll(jnp.where(low, 0.0, last), LANES // 2, 1)
            last = jnp.concatenate([jnp.where(low, last, 0.0), lower[: rows - cut]], axis=0)
        tiles.append(last_tile(last))
    return rounded(jnp.concatenate(tiles, axis=1), round_up(rows, 16))


def near_kernel(own_ref, mate_ref, pick_ref, shift_ref, adj_ref, rhs_ref, jac_ref, _, out_ref, image):
    rows, full = adj_ref.shape[0], jac_ref.shape[3]
    products([unpacked(ref, rows, full, twice) for ref in (own_ref, mate_ref)], pick_ref, jac_ref, image)
    out_ref[...] = without(shift_ref, adj_ref, rhs_ref, image)


def without(shift_ref, adj_ref, rhs_ref, image):
    rows, width = adj_ref.shape
    return rhs_ref[...] - (shift_ref[:rows, :width] * adj_ref[...] + image[:rows, :width])


def products(parts, pick_ref, jac_ref, image):
    elements, slots, width, full = jac_ref.shape
    rows_part, stride = parts[0].shape
    short = pick_ref.shape[1] - len(parts) * rows_part
    if short:
        parts = parts + [jnp.zeros((short, stride), HALF)]
    stacked = jnp.concatenate(parts, axis=0)
    picked = jnp.dot(pick_ref[...], stacked, preferred_element_type=FULL).astype(HALF)
    image[...] = jnp.zeros(image.shape, FULL)
    deep = full // (2 * LANES) * (2 * LANES)
    low = iota((4 * QUAD, LANES), 1) < LANES // 2
    for first in range(0, elements, 4):
        starts = [(k * elements + first) * QUAD for k in range(slots)]
        lefts = [picked[start : start + 4 * QUAD] for start in starts]
        tails = [left[:, deep:] for left in lefts]
        tails = [jnp.where(low, *tails[k : k + 2]) if k + 1 < slots else tails[k] for k in range(0, slots, 2)]
        left = jnp.concatenate([left[:, :deep] for left in lefts] + tails, axis=1)
        for i in range(4):
            e = first + i
            ends = [widened(jac_ref[e, k][:, deep:], LANES) for k in range(slots)]
            for k in range(1, slots, 2):
                ends[k - 1] = ends[k - 1] + pltpu.roll(ends[k], LANES // 2, 1)
            blocks = jnp.concatenate([jac_ref[e, k][:, :deep] for k in range(slots)] + ends[::2], axis=1)
            product = lax.dot_general(left, blocks, NT, preferred_element_type=FULL)
            image[pl.ds(e, 3, stride=elements), :width] = product[i * QUAD : i * QUAD + 3]


def twice(tail):
    return tail + pltpu.roll(tail, LANES // 2, 1)


def quad_products(lefts, blocks):
    full = blocks[0].shape[1]
    deep = full // (2 * LANES) * (2 * LANES)
    shape = (4 * QUAD, LANES)
    low = iota(shape, 1) < LANES // 2
    mine = []
    for i in range(4):
        place = iota(shape, 0) - i * QUAD
        mine.append(jnp.logical_and(jnp.logical_and(place >= 0, place < QUAD), low if i % 2 == 0 else jnp.logical_not(low)))
    tails = [left[:, deep : deep + LANES] for left in lefts]
    left = [jnp.where(mine[i], tails[i], jnp.where(mine[i + 1], tails[i + 1], 0.0).astype(HALF)) for i in (0, 2)]
    low = iota((blocks[0].shape[0], LANES), 1) < LANES // 2
    ends = [widened(block[:, deep:], LANES) for block in blocks]
    right = [jnp.where(low, ends[i], pltpu.roll(ends[i + 1], LANES // 2, 1)) for i in (0, 2)]
    shared = lax.dot_general(
        jnp.concatenate(left, axis=1), jnp.concatenate(right, axis=1), NT, preferred_element_type=FULL
    )
    products = []
    for i, (left, block) in enumerate(zip(lefts, blocks)):
        product = lax.dot_general(left[:, :deep], block[:, :deep], NT, preferred_element_type=FULL)
        part = slice(i * QUAD, (i + 1) * QUAD)
        products.append(product[part] + shared[part])
    return products


def far_kernel(near_ref, far_ref, jac_ref, list_ref, count_ref, _shapes, _ids, out_ref, spread, sums, image):
    elements, slots, width, _ = jac_ref.shape
    far = unpacked(far_ref, near_ref.shape[0], jac_ref.shape[3], twice)
    rows, stride = far.shape
    deep = spread.shape[1]
    shape = (elements, deep, rows)
    element, row, lane = [iota(shape, dim).reshape(elements * deep, rows) for dim in range(3)]
    row = lax.bitwise_and(row, QUAD - 1)
    pick = hit(jnp.where(row < 3, row * elements + element, -1) == lane).astype(HALF)
    taken = jnp.dot(pick, far, preferred_element_type=FULL).astype(HALF)
    spread[:elements] = taken.reshape(elements, deep, stride)
    spread[elements:] = jnp.zeros((spread.shape[0] - elements, deep, stride), HALF)
    sums[...] = jnp.zeros(sums.shape, FULL)

    @pl.loop(0, count_ref[0])
    def _(step):
        for i in range(0, GROUP, 4):
            owners, lefts, blocks = [], [], []
            for side in range(4):
                word = list_ref[step * GROUP + i + side]
                block = lax.shift_right_logical(word, 5)
                owners.append(lax.div(block, slots))
                lefts.append(spread[lax.bitwise_and(word, 31)])
                blocks.append(jac_ref[owners[side], block - owners[side] * slots])
            for e, product in zip(owners, quad_products(lefts, blocks)):
                sums[e, :QUAD, :width] += product

    for e in range(elements):
        image[pl.ds(e, 3, stride=elements), :] = sums[e, :3, :]
    real = near_ref.shape[0]
    out_ref[...] = rounded(near_ref[...] - image[:real, :width], out_ref.shape[0])


def element_of_row(shape, elements, copies=3):
    row = iota(shape, 0)
    for step in range(1, copies + 1):
        row = row - jnp.where(iota(shape, 0) >= step * elements, elements, 0)
    return row


def updated(resid_refs, inv_ref, adj_ref, update):
    rows, width = adj_ref.shape
    elements = rows // 3
    stride = round_up(inv_ref.shape[2], LANES)
    resid = put_columns([ref[...] for ref in resid_refs], distances(), stride)
    resid[-1] = twice(resid[-1])
    resid = jnp.concatenate(resid, axis=1).astype(HALF)
    shape = (elements, QUAD, resid.shape[0])
    deep = elements * QUAD
    element, row, lane = [iota(shape, dim).reshape(deep, -1) for dim in range(3)]
    pick = hit(jnp.where(row < 3, row * elements + element, -1) == lane).astype(HALF)
    resid = jnp.dot(pick, resid, preferred_element_type=FULL).astype(HALF)
    update[...] = jnp.zeros(update.shape, FULL)
    for first in range(0, elements, 4):
        left = resid[first * QUAD : (first + 4) * QUAD]
        for i, product in enumerate(quad_products([left] * 4, [inv_ref[first + i] for i in range(4)])):
            update[pl.ds(first + i, 3, stride=elements), :width] = product[:3]
    short = jnp.zeros((update.shape[0] - rows, width), FULL)
    return jnp.concatenate([adj_ref[...] + update[:rows, :width], short], axis=0)


def update_kernel(*refs):
    *resid_refs, inv_ref, adj_ref, adj_out, half_out, update = refs
    adj = updated(resid_refs, inv_ref, adj_ref, update)
    adj_out[...] = adj[: adj_out.shape[0]]
    half_out[...] = adj.astype(HALF)


def split(value):
    top = value.astype(HALF)
    return top, (value - top.astype(FULL)).astype(HALF)


def gradient_kernel(*refs):
    blks = lax.axis_size("blk")
    resid_refs = refs[:blks]
    inv_ref, adj_ref, shape_ref, low_ref, target_ref, adj_out = refs[blks : blks + 6]
    mate_out, far_out, sorted_ref, left_ref, sums_ref, update = refs[blks + 6 :]
    adj = updated(resid_refs, inv_ref, adj_ref, update)
    adj_out[...] = adj[: adj_out.shape[0]]
    half = adj.astype(HALF)
    elements = adj_out.shape[0] // 3
    pairs = elements // 2
    tall, width = half.shape
    coords = shape_ref.shape[2]
    depth = 3 if elements % 3 == 0 and 3 * width <= 256 else 1
    block = widened(half.astype(FULL), LANES)
    left = jnp.concatenate(laid([block] * depth, width, round_up(depth * width, LANES)), axis=1)[:, : depth * width]
    shape = left.shape
    owner = element_of_row(shape, elements)
    group = jnp.zeros(shape, jnp.int32)
    for step in range(1, elements // depth):
        group = group + jnp.where(owner >= step * depth, 1, 0)
    first = (owner - group * depth) * width
    behind = iota(shape, 1) - first
    left = jnp.where(jnp.logical_and(behind >= 0, behind < width), left, 0.0).astype(HALF)
    shape = (tall, coords)
    owner = element_of_row(shape, elements)
    total = jnp.zeros(shape, FULL)
    for start in range(0, elements, depth):
        partials = jnp.concatenate([shape_ref[start + step] for step in range(depth)], axis=0)
        product = jnp.dot(left, partials, preferred_element_type=FULL)
        total = jnp.where(owner >= start, product, total)
    low = iota((tall, LANES), 1) < LANES // 2
    odd = lax.bitwise_and(owner[:, :LANES], 1) == 1
    values = [total[:, :LANES], widened(total[:, LANES:], LANES)]
    turned = [pltpu.roll(value, LANES // 2, 1) for value in values]
    value = [
        jnp.where(odd, jnp.where(low, 0.0, turned[0]), jnp.where(low, values[0], 0.0)),
        jnp.where(odd, jnp.where(low, 0.0, values[0]), jnp.where(low, turned[0], 0.0)),
        jnp.where(odd, turned[1], values[1]),
    ]
    top, rest = split(jnp.concatenate(value, axis=1))
    sorted_ref[:tall] = top.astype(FULL)
    sorted_ref[tall:] = rest.astype(FULL)
    node_sums(sorted_ref, low_ref, target_ref, left_ref, sums_ref, blks)
    put_sums(mate_out, sums_ref, 0)
    put_sums(far_out, sums_ref, blks)


def own_sums_kernel(sorted_ref, low_ref, target_ref, out_ref, left_ref, sums_ref):
    node_sums(sorted_ref, low_ref, target_ref, left_ref, sums_ref, 0)
    put_sums(out_ref, sums_ref, 0)


def node_sums(sorted_ref, low_ref, target_ref, left_ref, sums_ref, first):
    deep = left_ref.shape[0] // 18
    tall = sorted_ref.shape[0] // 2
    pairs = target_ref.shape[0]
    for pair in range(pairs):
        lanes = slice(pair * LANES, (pair + 1) * LANES)
        mine = iota((deep, LANES), 0) + first == target_ref[pair : pair + 1, :]
        groups = []
        for part in range(2):
            for j in range(3):
                at = part * tall + 2 * (j * pairs + pair)
                for c in range(3):
                    axis = slice(c * LANES, (c + 1) * LANES)
                    values = sorted_ref[at : at + 1, axis] + sorted_ref[at + 1 : at + 2, axis]
                    groups.append(jnp.where(mine, values, 0.0))
        for i in range(0, 18, 2):
            both = jnp.concatenate(groups[i : i + 2], axis=0)
            left_ref[i * deep : (i + 2) * deep, lanes] = both.astype(HALF)
    sums = lax.dot_general(left_ref[...], low_ref[...], NT, preferred_element_type=FULL)
    span = low_ref.shape[0]
    sums = -(sums[: 9 * deep] + sums[9 * deep :])
    for tile in range(sums_ref.shape[0]):
        part = sums[:, tile * LANES : min(span, (tile + 1) * LANES)]
        sums_ref[tile, :, : part.shape[1]] = part


def put_sums(out_ref, sums_ref, first):
    blks = lax.axis_size("blk")
    deep = sums_ref.shape[1] // 9
    rows, span = out_ref.shape
    for tile in range(sums_ref.shape[0]):
        start, stop = tile * LANES, min(span, (tile + 1) * LANES)
        found = [sums_ref[tile, pl.ds(first + k, 9, stride=deep), :][:, : stop - start] for k in range(blks)]
        found = jnp.concatenate(found + [jnp.zeros((rows - 9 * blks, stop - start), FULL)], axis=0)
        out_ref[:, start:stop] = found.astype(out_ref.dtype)


def combine_kernel(own_ref, mate_ref, far_ref, *piece_outs):
    total = own_ref[...] + mate_ref[...].astype(FULL) + far_ref[...].astype(FULL)
    for k, out_ref in enumerate(piece_outs):
        piece = total[9 * k : 9 * (k + 1)]
        out_ref[...] = rounded(piece, 16) if k else piece


def local(
    adjoint_start,
    right_sides,
    jac_blocks,
    block_inverse,
    neighbours,
    pseudo_shift,
    shape_partials,
    node_ids,
):
    elements, sides, width = adjoint_start.shape
    slots, full = jac_blocks.shape[1], jac_blocks.shape[3]
    enodes = node_ids.shape[1]
    rows = sides * elements
    tall = round_up(rows, 16)
    stride = round_up(full, LANES)
    blks = lax.axis_size("blk")
    span = NODE_DEV // blks
    stacked = round_up(3 * tall, LANES)
    entries = elements * enodes

    adj_hbm = jnp.transpose(adjoint_start, (1, 0, 2)).reshape(rows, width)
    rhs = jnp.transpose(right_sides, (1, 0, 2)).reshape(rows, width)
    half_shape = jax.ShapeDtypeStruct((tall, width), HALF)

    adj_shape = jax.ShapeDtypeStruct((rows, width), FULL)
    pick, shift, far_list, far_count, adj, rhs = call(
        slots_kernel,
        "slots",
        [in_hbm(neighbours.T), in_hbm(pseudo_shift), in_hbm(adj_hbm), in_hbm(rhs), in_hbm(jac_blocks)],
        [HBM] * 5,
        [
            jax.ShapeDtypeStruct((slots * elements * QUAD, stacked), HALF),
            jax.ShapeDtypeStruct((tall, LANES), FULL),
            pltpu.SMEM((round_up(elements * (slots - 1) + GROUP, LANES),), jnp.int32),
            pltpu.SMEM((1,), jnp.int32),
            pltpu.VMEM((rows, width), FULL),
            pltpu.VMEM((rows, width), FULL),
        ],
        scratch=[
            pltpu.VMEM((slots - 1, elements), jnp.int32),
            pltpu.SMEM((slots - 1, elements), jnp.int32),
            pltpu.SMEM((elements,), FULL),
            pltpu.SemaphoreType.DMA((6,)),
        ],
        moved=16 * MIB,
    )
    low, target, shapes = call(
        nodes_kernel,
        "nodes",
        [node_ids, shape_partials],
        [VMEM, VMEM],
        [
            jax.ShapeDtypeStruct((span, entries), HALF),
            jax.ShapeDtypeStruct((entries // LANES, LANES), jnp.int32),
            jax.ShapeDtypeStruct(shape_partials.shape, HALF),
        ],
        moved=3 * MIB,
    )

    for sweep in range(SWEEPS):
        order = distances()
        blocks = [half] + over_blk(half, order) if sweep else [adj] + over_blk(adj_hbm, order)
        wide = jax.ShapeDtypeStruct((packed_rows(rows, full), LANES), HALF)
        (own,) = call(functools.partial(columns_kernel, order, rows, full), "columns", blocks, [VMEM] * blks, [wide], moved=1 * MIB)
        far, mate = to_far(own), to_mate(own)
        image = pltpu.VMEM((tall, LANES), FULL)
        near_inputs = [own, mate, pick, shift, adj, rhs]
        far_scratch = [
            pltpu.VMEM((elements + 8, 16, stride), HALF),
            pltpu.VMEM((elements, 8, LANES), FULL),
            image,
        ]
        (near,) = call(
            near_kernel,
            "near",
            near_inputs + [jac_blocks, in_hbm(block_inverse)],
            [VMEM] * 7 + [HBM],
            [adj_shape],
            [image],
            moved=12 * MIB,
        )
        (resid,) = call(
            far_kernel,
            "far",
            [near, far, jac_blocks, far_list, far_count, in_hbm(shape_partials), in_hbm(node_ids)],
            [VMEM] * 3 + [SMEM] * 2 + [HBM] * 2,
            [half_shape],
            far_scratch,
            moved=4 * MIB,
        )
        resids = [resid] + over_blk(resid, distances())
        if sweep < SWEEPS - 1:
            adj, half = call(
                update_kernel,
                "update",
                resids + [block_inverse, adj],
                [VMEM] * (blks + 2),
                [adj_shape, half_shape],
                scratch=[pltpu.VMEM((tall, LANES), FULL)],
                moved=8 * MIB,
            )
    deep = round_up(9 * blks, 16)
    part_shapes = [jax.ShapeDtypeStruct((deep, span), kind) for kind in (FULL, HALF)]
    sums_scratch = [
        pltpu.VMEM((18 * 2 * blks, entries), HALF),
        pltpu.VMEM((-(-span // LANES), 9 * 2 * blks, LANES), FULL),
    ]
    adj, mate, far, by_axis = call(
        gradient_kernel,
        "gradient",
        resids + [block_inverse, adj, shapes, low, target],
        [VMEM] * (blks + 5),
        [adj_shape, part_shapes[1], part_shapes[1], jax.ShapeDtypeStruct((2 * tall, 3 * LANES), FULL)],
        scratch=sums_scratch + [pltpu.VMEM((tall, LANES), FULL)],
    )
    (own,) = call(
        own_sums_kernel, "own_sums", [by_axis, low, target], [VMEM] * 3, part_shapes[:1], sums_scratch, moved=2 * MIB
    )
    far, mate = to_far(far), to_mate(mate)
    shapes = [jax.ShapeDtypeStruct((16, span), HALF)] * (blks - 1)
    pieces = call(
        combine_kernel, "combine", [own, mate, far], [VMEM] * 3, [jax.ShapeDtypeStruct((9, span), FULL)] + shapes
    )
    gradient = pieces[0]
    count = lax.axis_size("blk")
    for k in reversed(distances()):
        gradient = gradient + lax.ppermute(pieces[k], "blk", [(i, i ^ k) for i in range(count)])[:9].astype(FULL)
    adjoint = jnp.transpose(adj.reshape(sides, elements, width), (1, 0, 2))
    return (adjoint, gradient)


def solution(mesh):
    in_specs = (
        P("dom", None, "blk"),
        P("dom", None, "blk"),
        P("dom", None, "blk", None),
        P("dom", "blk", None),
        P("dom", None),
        P("dom"),
        P("dom", "blk", None),
        P("dom", None),
    )
    out_specs = (P("dom", None, "blk"), P(None, ("dom", "blk")))
    return jax.shard_map(local, mesh=mesh, in_specs=in_specs, out_specs=out_specs, check_vma=False)
```
